32 devices in a mesh: dp: 4 (over y, x), fsdp: 8 (over z, core).
Axes of the slice: x: 2, y: 2, z: 4, core: 2. Of those that a mesh axis runs over, the one named last changes fastest.
Arguments:
- tokens_in: bfloat16 [12288, 2048], P(('dp', 'fsdp')), may hold values from -6 to 6
- out_grad: bfloat16 [12288, 2048], P(('dp', 'fsdp')), may hold values from -6 to 6
- kv_grad_next: bfloat16 [12288, 256], P(('dp', 'fsdp')), may hold values from -6 to 6
- doc_ids: int32 [32, 384], P(('dp', 'fsdp')), may hold values from 0 to 5, never falling along the last dimension, each value on 1 to 192 neighbouring positions
- gains: float32 [2, 2048], P(None, ('dp', 'fsdp')), may hold values from 0.5 to 1.5
- gains_mom: float32 [2, 2048], P(None, ('dp', 'fsdp')), may hold values from -1792 to 1792
- gains_ema: float32 [2, 2048], P(None, ('dp', 'fsdp')), may hold values from 0.5 to 1.5
- w_query: float32 [2048, 2048], P(('dp', 'fsdp')), may hold values from -0.125 to 0.125
- query_mom: float32 [2048, 2048], P(('dp', 'fsdp')), may hold values from -896 to 896
- query_ema: float32 [2048, 2048], P(('dp', 'fsdp')), may hold values from -0.125 to 0.125
- w_keyval: float32 [2048, 256], P(('dp', 'fsdp')), may hold values from -0.125 to 0.125
- keyval_mom: float32 [2048, 256], P(('dp', 'fsdp')), may hold values from -4096 to 4096
- keyval_ema: float32 [2048, 256], P(('dp', 'fsdp')), may hold values from -0.125 to 0.125
- w_output: float32 [2048, 2048], P(('dp', 'fsdp')), may hold values from -0.5 to 0.5
- output_mom: float32 [2048, 2048], P(('dp', 'fsdp')), may hold values from -384 to 384
- output_ema: float32 [2048, 2048], P(('dp', 'fsdp')), may hold values from -0.5 to 0.5
- w_gate: float32 [2048, 5632], P(('dp', 'fsdp')), may hold values from -0.125 to 0.125
- gate_mom: float32 [2048, 5632], P(('dp', 'fsdp')), may hold values from -384 to 384
- gate_ema: float32 [2048, 5632], P(('dp', 'fsdp')), may hold values from -0.125 to 0.125
- w_up: float32 [2048, 5632], P(('dp', 'fsdp')), may hold values from -0.125 to 0.125
- up_mom: float32 [2048, 5632], P(('dp', 'fsdp')), may hold values from -384 to 384
- up_ema: float32 [2048, 5632], P(('dp', 'fsdp')), may hold values from -0.125 to 0.125
- w_down: float32 [5632, 2048], P(('dp', 'fsdp')), may hold values from -0.15625 to 0.15625
- down_mom: float32 [5632, 2048], P(('dp', 'fsdp')), may hold values from -320 to 320
- down_ema: float32 [5632, 2048], P(('dp', 'fsdp')), may hold values from -0.15625 to 0.15625
Outputs:
- layer_out: float32 [12288, 2048], P(('dp', 'fsdp'))
- shared_kv: float32 [12288, 256], P(('dp', 'fsdp'))
- input_grad: float32 [12288, 2048], P(('dp', 'fsdp'))
- gains_mom_new: float32 [2, 2048], P(None, ('dp', 'fsdp'))
- gains_new: float32 [2, 2048], P(None, ('dp', 'fsdp'))
- gains_ema_new: float32 [2, 2048], P(None, ('dp', 'fsdp'))
- query_mom_new: float32 [2048, 2048], P(('dp', 'fsdp'))
- query_new: float32 [2048, 2048], P(('dp', 'fsdp'))
- query_ema_new: float32 [2048, 2048], P(('dp', 'fsdp'))
- keyval_mom_new: float32 [2048, 256], P(('dp', 'fsdp'))
- keyval_new: float32 [2048, 256], P(('dp', 'fsdp'))
- keyval_ema_new: float32 [2048, 256], P(('dp', 'fsdp'))
- output_mom_new: float32 [2048, 2048], P(('dp', 'fsdp'))
- output_new: float32 [2048, 2048], P(('dp', 'fsdp'))
- output_ema_new: float32 [2048, 2048], P(('dp', 'fsdp'))
- gate_mom_new: float32 [2048, 5632], P(('dp', 'fsdp'))
- gate_new: float32 [2048, 5632], P(('dp', 'fsdp'))
- gate_ema_new: float32 [2048, 5632], P(('dp', 'fsdp'))
- up_mom_new: float32 [2048, 5632], P(('dp', 'fsdp'))
- up_new: float32 [2048, 5632], P(('dp', 'fsdp'))
- up_ema_new: float32 [2048, 5632], P(('dp', 'fsdp'))
- down_mom_new: float32 [5632, 2048], P(('dp', 'fsdp'))
- down_new: float32 [5632, 2048], P(('dp', 'fsdp'))
- down_ema_new: float32 [5632, 2048], P(('dp', 'fsdp'))
The draws below stay inside these ranges and needn't reach their ends.
Inputs may be any that keep to these rules, and one draw needn't show every extreme that they name: `doc_ids`: each row is one sequence; document numbers start at 0 and never fall along a row; a document has 1 to 192 tokens and one in each row has exactly 192.
All inputs are finite; a program needn't handle non-finite values.
Results may differ from the reference program's by a relative error of at most 0.014.
The reference program's roundings to bfloat16 on the way count: a program that leaves them out, or rounds other values in their place, can miss the bound.
Values may be sent and summed in bfloat16 or wider, within the bound.
No kernel may reach another device: no remote copies, remote signals or barrier semaphores. Data moves between devices by JAX's collectives and lax.ppermute only.
A program may use at most 448 MiB of HBM per device.

```python
import math
import jax
import jax.numpy as jnp
import numpy as np
from jax import lax

D = 2048
H = 16
HD = 128
FF = 5632
LENGTH = 384
SEQS = 32
TOKENS = 12288
DOCS = 6
MOST = 192


def steps_of(key, dims, split, smallest, top_value):
    def one(dim, blocks):
        steps = jax.random.uniform(jax.random.fold_in(jax.random.fold_in(key, 6), dim), (blocks,), jnp.float32, smallest / len(split), top_value / len(split))
        return jnp.repeat(jnp.exp(steps), dims[dim] // blocks).reshape((-1,) + (1,) * (len(dims) - dim - 1))

    gain = one(*split[0])
    for cut in split[1:]:
        gain = gain * one(*cut)
    return gain


def split_up(amount, total, reach, skew):
    weights = [(1 << 20) // math.isqrt(grade ** skew) + 1 for grade in range(2, amount + 1)]
    surplus, counts = total - reach - (amount - 1), [1] * (amount - 1)
    while surplus > 0:
        candidates = [i for i in range(amount - 1) if counts[i] < reach]
        whole, budget = sum([weights[i] for i in candidates]), surplus
        for i in candidates:
            extra = min(reach - counts[i], max(1, budget * weights[i] // whole), surplus)
            counts[i] = counts[i] + extra
            surplus = surplus - extra
    return np.array([reach] + counts)


def uneven_parts(key, count, total, most, skew):
    if count == 2:
        one = jax.random.randint(key, (), max(1, total - most), min(most, total - 1) + 1)
        return jnp.stack([one, total - one])
    sizes = jnp.asarray(split_up(count, total, most, skew), jnp.int32)
    twos = (count - 1) // 2
    source_of, taker = sizes[1:1 + 2 * twos:2], sizes[2:2 + 2 * twos:2]
    room = jnp.minimum(source_of - 1, most - taker)
    shifted = jax.random.randint(jax.random.fold_in(key, 1), (twos,), 0, 1 << 20) % (room + 1)
    sizes = sizes.at[1:1 + 2 * twos:2].set(source_of - shifted).at[2:2 + 2 * twos:2].set(taker + shifted)
    return sizes[jax.random.permutation(jax.random.fold_in(key, 2), count)]


def scatter_about(stream_key, shape, spread, most, cuts=(), kind=jnp.bfloat16):
    result = jax.random.normal(stream_key, shape, jnp.float32) * spread
    if len(cuts) > 0:
        result = steps_of(stream_key, shape, cuts, -0.22, 0.18) * result
    return jnp.clip(result, min=-most, max=most).astype(kind)


def setup_inputs(seed: int = 0) -> dict:
    streams_of = jax.random.split(jax.random.key(seed), 26)
    tokens_in = scatter_about(streams_of[0], (TOKENS, D), 1.0, 6.0, ((0, 32),))
    out_grad = scatter_about(streams_of[1], (TOKENS, D), 1.0, 6.0, ((0, 32),))
    kv_grad_next = scatter_about(streams_of[2], (TOKENS, 2 * HD), 1.0, 6.0, ((0, 32),))
    doc_ids = jax.vmap(lambda own: jnp.searchsorted(jnp.cumsum(uneven_parts(own, DOCS, LENGTH, MOST, 2)), jnp.arange(LENGTH), side="right"))(jax.random.split(streams_of[3], SEQS)).reshape((SEQS, LENGTH)).astype(jnp.int32)
    gains = jnp.clip(1.0 + 0.1 * jax.random.normal(streams_of[4], (2, D), jnp.float32), 0.5, 1.5)
    gains_mom = scatter_about(streams_of[5], (2, D), (2.6 * TOKENS ** 0.5), 1792.0, ((1, 32),), jnp.float32)
    gains_ema = jnp.clip(1.0 + 0.1 * jax.random.normal(streams_of[6], (2, D), jnp.float32), 0.5, 1.5)
    w_query = scatter_about(streams_of[7], (D, H * HD), D ** -0.5, 0.125, ((0, 32),), jnp.float32)
    query_mom = scatter_about(streams_of[8], (D, H * HD), (1.4 * TOKENS ** 0.5), 896.0, ((0, 32),), jnp.float32)
    query_ema = scatter_about(streams_of[9], (D, H * HD), D ** -0.5, 0.125, ((0, 32),), jnp.float32)
    w_keyval = scatter_about(streams_of[10], (D, 2 * HD), D ** -0.5, 0.125, ((0, 32),), jnp.float32)
    keyval_mom = scatter_about(streams_of[11], (D, 2 * HD), (6 * TOKENS ** 0.5), 4096.0, ((0, 32),), jnp.float32)
    keyval_ema = scatter_about(streams_of[12], (D, 2 * HD), D ** -0.5, 0.125, ((0, 32),), jnp.float32)
    w_output = scatter_about(streams_of[13], (H * HD, D), (H * HD // 16) ** -0.5, 0.5, ((0, 32),), jnp.float32)
    output_mom = scatter_about(streams_of[14], (H * HD, D), (0.6 * TOKENS ** 0.5), 384.0, ((0, 32),), jnp.float32)
    output_ema = scatter_about(streams_of[15], (H * HD, D), (H * HD // 16) ** -0.5, 0.5, ((0, 32),), jnp.float32)
    w_gate = scatter_about(streams_of[16], (D, FF), D ** -0.5, 0.125, ((0, 32),), jnp.float32)
    gate_mom = scatter_about(streams_of[17], (D, FF), (0.6 * TOKENS ** 0.5), 384.0, ((0, 32),), jnp.float32)
    gate_ema = scatter_about(streams_of[18], (D, FF), D ** -0.5, 0.125, ((0, 32),), jnp.float32)
    w_up = scatter_about(streams_of[19], (D, FF), D ** -0.5, 0.125, ((0, 32),), jnp.float32)
    up_mom = scatter_about(streams_of[20], (D, FF), (0.6 * TOKENS ** 0.5), 384.0, ((0, 32),), jnp.float32)
    up_ema = scatter_about(streams_of[21], (D, FF), D ** -0.5, 0.125, ((0, 32),), jnp.float32)
    w_down = scatter_about(streams_of[22], (FF, D), (FF // 4) ** -0.5, 0.15625, ((0, 32),), jnp.float32)
    down_mom = scatter_about(streams_of[23], (FF, D), (0.5 * TOKENS ** 0.5), 320.0, ((0, 32),), jnp.float32)
    down_ema = scatter_about(streams_of[24], (FF, D), (FF // 4) ** -0.5, 0.15625, ((0, 32),), jnp.float32)
    return {"tokens_in": tokens_in, "out_grad": out_grad, "kv_grad_next": kv_grad_next, "doc_ids": doc_ids, "gains": gains, "gains_mom": gains_mom, "gains_ema": gains_ema, "w_query": w_query, "query_mom": query_mom, "query_ema": query_ema, "w_keyval": w_keyval, "keyval_mom": keyval_mom, "keyval_ema": keyval_ema, "w_output": w_output, "output_mom": output_mom, "output_ema": output_ema, "w_gate": w_gate, "gate_mom": gate_mom, "gate_ema": gate_ema, "w_up": w_up, "up_mom": up_mom, "up_ema": up_ema, "w_down": w_down, "down_mom": down_mom, "down_ema": down_ema}


EPS = 1e-05
THETA = 10000.0
MOMENTUM = 0.9
AVERAGE = 0.75
NEG = -1e+30

@jax.custom_vjp
def low(v):
    return lax.optimization_barrier(v.astype(jnp.bfloat16)).astype(jnp.float32)

@jax.custom_vjp
def low_back(v):
    return v

def low_keep(v):
    return (low(v), None)

def low_pass(kept, grad):
    return (grad,)

def back_keep(v):
    return (v, None)

def back_low(kept, grad):
    return (low(grad),)
low.defvjp(low_keep, low_pass)
low_back.defvjp(back_keep, back_low)

def positions_of(doc_ids):
    length = doc_ids.shape[-1]
    offsets = jnp.broadcast_to(jnp.arange(length, dtype=jnp.int32), doc_ids.shape)
    change = jnp.concatenate([jnp.ones(doc_ids.shape[:-1] + (1,), dtype=jnp.bool_), doc_ids[..., 1:] != doc_ids[..., :-1]], axis=-1)
    starts = lax.cummax(jnp.where(change, offsets, 0), axis=doc_ids.ndim - 1)
    return (offsets - starts).astype(jnp.int32)

def rotation(positions, head_dim):
    half_dim = head_dim // 2
    inverse = THETA ** (-(jnp.arange(half_dim, dtype=jnp.float32) * 2.0) / head_dim)
    angles = positions.astype(jnp.float32)[..., None] * inverse
    return (jnp.cos(angles), jnp.sin(angles))

def rotate(values, cosine, sine_table):
    half_dim = values.shape[-1] // 2
    upper = values[..., :half_dim]
    lower = values[..., half_dim:]
    return jnp.concatenate([upper * cosine - lower * sine_table, lower * cosine + upper * sine_table], axis=-1)

def attend(queries, shared, doc_row):
    length = doc_row.shape[0]
    block_rows = min(512, length)
    nblocks = length // block_rows
    head_dim = shared.shape[-1] // 2
    head_count = queries.shape[1]
    key_rows = shared[:, :head_dim]
    value_rows = shared[:, head_dim:]
    offsets = jnp.arange(length, dtype=jnp.int32)

    def one_block(pieces):
        qblock, query_ids, query_pos = pieces
        scores = low_back(jnp.einsum('qhd,kd->hqk', qblock, key_rows, precision=lax.Precision.HIGHEST))
        allowed = (query_ids[:, None] == doc_row[None, :]) & (offsets[None, :] <= query_pos[:, None])
        scores = jnp.where(allowed[None], scores, NEG)
        top_score = lax.optimization_barrier(jnp.max(scores, axis=-1, keepdims=True))
        weights = jnp.exp(scores - top_score)
        probabilities = low(weights / lax.optimization_barrier(jnp.sum(weights, axis=-1, keepdims=True)))
        return jnp.einsum('hqk,kd->qhd', probabilities, value_rows, precision=lax.Precision.HIGHEST)
    mixed = lax.map(jax.checkpoint(one_block), (queries.reshape(nblocks, block_rows, head_count, head_dim), doc_row.reshape(nblocks, block_rows), offsets.reshape(nblocks, block_rows)))
    return mixed.reshape(length, head_count, head_dim)

def forward(tokens, gains, w_query, w_keyval, w_output, w_gate, w_up, w_down, doc_ids):
    seq_count, length = doc_ids.shape
    gains_low = low(gains)
    query_low = low(w_query)
    keyval_low = low(w_keyval)
    output_low = low(w_output)
    gate_low = low(w_gate)
    up_low = low(w_up)
    down_low = low(w_down)
    inv_rms = lax.rsqrt(lax.optimization_barrier(jnp.mean(tokens * tokens, axis=-1, keepdims=True)) + EPS)
    normed = low(tokens * inv_rms * gains_low[0])
    query_raw = low_back(jnp.dot(normed, query_low, precision=lax.Precision.HIGHEST, preferred_element_type=jnp.float32))
    keyval_raw = low_back(jnp.dot(normed, keyval_low, precision=lax.Precision.HIGHEST, preferred_element_type=jnp.float32))
    head_dim = keyval_raw.shape[-1] // 2
    head_count = query_raw.shape[-1] // head_dim
    cosine, sine_table = rotation(positions_of(doc_ids).reshape(-1), head_dim)
    turned = rotate(query_raw.reshape(-1, head_count, head_dim), cosine[:, None], sine_table[:, None]) * head_dim ** (-0.5)
    queries = low_back(low(turned))
    shared = low_back(low(jnp.concatenate([rotate(keyval_raw[:, :head_dim], cosine, sine_table), keyval_raw[:, head_dim:]], axis=-1)))
    mixed = jax.vmap(attend)(queries.reshape(seq_count, length, head_count, head_dim), shared.reshape(seq_count, length, 2 * head_dim), doc_ids)
    attended = low_back(low(mixed.reshape(seq_count * length, head_count * head_dim)))
    branch = low_back(jnp.dot(attended, output_low, precision=lax.Precision.HIGHEST, preferred_element_type=jnp.float32))
    resid = tokens + branch
    inv_rms2 = lax.rsqrt(lax.optimization_barrier(jnp.mean(resid * resid, axis=-1, keepdims=True)) + EPS)
    normed2 = low(resid * inv_rms2 * gains_low[1])
    gate = low_back(jnp.dot(normed2, gate_low, precision=lax.Precision.HIGHEST, preferred_element_type=jnp.float32))
    up = low_back(jnp.dot(normed2, up_low, precision=lax.Precision.HIGHEST, preferred_element_type=jnp.float32))
    hidden = low_back(low(jax.nn.silu(gate) * up))
    layer_out = resid + jnp.dot(hidden, down_low, precision=lax.Precision.HIGHEST, preferred_element_type=jnp.float32)
    return (layer_out, shared)

def update(weight, moment, average, grad, rate):
    moment_new = MOMENTUM * moment + grad
    weight_new = weight - rate * (grad + MOMENTUM * moment_new)
    average_new = AVERAGE * average + (1.0 - AVERAGE) * weight_new
    return (moment_new, weight_new, average_new)

def reference(tokens_in, out_grad, kv_grad_next, doc_ids, gains, gains_mom, gains_ema, w_query, query_mom, query_ema, w_keyval, keyval_mom, keyval_ema, w_output, output_mom, output_ema, w_gate, gate_mom, gate_ema, w_up, up_mom, up_ema, w_down, down_mom, down_ema):
    group_size = 4
    seqs_total, length = doc_ids.shape
    groups = seqs_total // group_size
    rows = group_size * length
    width = tokens_in.shape[1]
    kv_width = kv_grad_next.shape[1]
    tok_all = tokens_in.astype(jnp.float32).reshape(groups, rows, width)
    cot_all = out_grad.astype(jnp.float32).reshape(groups, rows, width)
    cot_shared = kv_grad_next.astype(jnp.float32).reshape(groups, rows, kv_width)
    ids_all = doc_ids.reshape(groups, group_size, length)
    params = (gains, w_query, w_keyval, w_output, w_gate, w_up, w_down)

    def step_group(totals, pieces):
        tok_group, cot_group, shared_group, ids_group = pieces

        def local(tok_in, p_gains, p_query, p_keyval, p_output, p_gate, p_up, p_down):
            return forward(tok_in, p_gains, p_query, p_keyval, p_output, p_gate, p_up, p_down, ids_group)
        results, pullback = jax.vjp(local, tok_group, *params)
        grads = pullback((cot_group, shared_group))
        totals = tuple((total + grad for total, grad in zip(totals, grads[1:])))
        return (totals, (results[0], results[1], grads[0]))
    zeros = tuple((jnp.zeros_like(param) for param in params))
    totals, stacked = lax.scan(step_group, zeros, (tok_all, cot_all, cot_shared, ids_all))
    layer_out = stacked[0].reshape(TOKENS, width)
    shared_kv = stacked[1].reshape(TOKENS, kv_width)
    input_grad = stacked[2].reshape(TOKENS, width)
    gains_out = update(gains, gains_mom, gains_ema, totals[0], 0.1 / math.sqrt(TOKENS))
    query_out = update(w_query, query_mom, query_ema, totals[1], 0.6 / math.sqrt(D * TOKENS))
    keyval_out = update(w_keyval, keyval_mom, keyval_ema, totals[2], 0.15 / math.sqrt(D * TOKENS))
    output_out = update(w_output, output_mom, output_ema, totals[3], 5.0 / math.sqrt(H * HD * TOKENS))
    gate_out = update(w_gate, gate_mom, gate_ema, totals[4], 0.6 / math.sqrt(D * TOKENS))
    up_out = update(w_up, up_mom, up_ema, totals[5], 0.6 / math.sqrt(D * TOKENS))
    down_out = update(w_down, down_mom, down_ema, totals[6], 1.5 / math.sqrt(FF * TOKENS))
    return (layer_out, shared_kv, input_grad, gains_out[0], gains_out[1], gains_out[2], query_out[0], query_out[1], query_out[2], keyval_out[0], keyval_out[1], keyval_out[2], output_out[0], output_out[1], output_out[2], gate_out[0], gate_out[1], gate_out[2], up_out[0], up_out[1], up_out[2], down_out[0], down_out[1], down_out[2])
```

```python
import functools
import math

import jax
import jax.numpy as jnp
from jax import lax
from jax.experimental import pallas as pl
from jax.experimental.pallas import tpu as pltpu
from jax.sharding import PartitionSpec as P

EPS = 1e-05
THETA = 10000.0
MOMENTUM = 0.9
AVERAGE = 0.75
NEG = -1e30
F32 = jnp.float32
BF16 = jnp.bfloat16
BOTH = ("dp", "fsdp")
COST = 0.2
VMEM_BYTES = 60 * 1024 * 1024


def positions_of(doc_ids):
    length = doc_ids.shape[-1]
    offsets = jnp.arange(length, dtype=jnp.int32)
    same = doc_ids[..., :, None] == doc_ids[..., None, :]
    starts = jnp.min(jnp.where(same, offsets, length), axis=-1)
    return offsets - starts


def rotation(positions, head_dim):
    half_dim = head_dim // 2
    inverse = THETA ** (-(jnp.arange(half_dim, dtype=F32) * 2.0) / head_dim)
    angles = positions.astype(F32)[..., None] * inverse
    cosine, sine = jnp.cos(angles), jnp.sin(angles)
    return (
        jnp.concatenate([cosine, cosine], axis=-1),
        jnp.concatenate([-sine, sine], axis=-1),
    )


def dot(left, right, contract, kind=F32):
    return lax.dot_general(
        left, right, ((contract[:1], contract[1:]), ((), ())), preferred_element_type=F32
    ).astype(kind)


def limits(flops=0, moved=0, steps=1):
    semantics = ("arbitrary",) * steps if steps else None
    return {
        "compiler_params": pltpu.CompilerParams(
            vmem_limit_bytes=VMEM_BYTES, dimension_semantics=semantics
        ),
        "cost_estimate": pl.CostEstimate(
            flops=int(flops * COST), bytes_accessed=int(moved * COST), transcendentals=0
        ),
    }


def swap_halves(values):
    return pltpu.roll(values, values.shape[-1] // 2, values.ndim - 1)


def set_bias(bias, ids_row, ids_col):
    shape = bias.shape
    later = lax.broadcasted_iota(jnp.int32, shape, 1) > lax.broadcasted_iota(jnp.int32, shape, 0)
    apart = (ids_col[0] != ids_row[0]) | later
    bias[...] = jnp.where(apart, NEG, 0.0)


def probabilities(query, keys, bias):
    scores = dot(query, keys, (1, 1)) + bias[...]
    weights = jnp.exp(scores - jnp.max(scores, axis=-1, keepdims=True))
    return weights / jnp.sum(weights, axis=-1, keepdims=True)


def attend_kernel(
    scale, q_raw, k_raw, v_raw, cosine, sine, ids_row, ids_col, queries, attended, shared, bias
):
    head_dim = q_raw.shape[1]

    @pl.when(pl.program_id(1) == 0)
    def _():
        set_bias(bias, ids_row, ids_col)
        key = k_raw[...]
        turned = key * cosine[...] + swap_halves(key) * sine[...]
        shared[:, :head_dim] = turned.astype(BF16)
        shared[:, head_dim:] = v_raw[...].astype(BF16)

    raw = q_raw[...]
    query = ((raw * cosine[...] + swap_halves(raw) * sine[...]) * scale).astype(BF16)
    queries[...] = query
    probs = probabilities(query, shared[:, :head_dim], bias).astype(BF16)
    attended[...] = dot(probs, shared[:, head_dim:], (1, 0), BF16)


def attend(raw, cosine, sine, doc_ids, head_count, head_dim):
    seq_count, length = doc_ids.shape
    rows = seq_count * length
    column = lambda which: pl.BlockSpec((length, head_dim), which)
    whole = pl.BlockSpec((length, head_dim), lambda s, h: (s, 0))
    return pl.pallas_call(
        functools.partial(attend_kernel, head_dim ** (-0.5)),
        grid=(seq_count, head_count),
        in_specs=[
            column(lambda s, h: (s, h)),
            column(lambda s, h: (s, head_count)),
            column(lambda s, h: (s, head_count + 1)),
            whole,
            whole,
            pl.BlockSpec((1, 1, length), lambda s, h: (s, 0, 0)),
            pl.BlockSpec((1, length, 1), lambda s, h: (s, 0, 0)),
        ],
        out_specs=[
            column(lambda s, h: (s, h)),
            column(lambda s, h: (s, h)),
            pl.BlockSpec((length, 2 * head_dim), lambda s, h: (s, 0)),
        ],
        out_shape=[
            jax.ShapeDtypeStruct((rows, head_count * head_dim), BF16),
            jax.ShapeDtypeStruct((rows, head_count * head_dim), BF16),
            jax.ShapeDtypeStruct((rows, 2 * head_dim), BF16),
        ],
        scratch_shapes=[pltpu.VMEM((length, length), F32)],
        name="attend",
        **limits(6 * rows * length * head_dim * head_count, 10 * rows * head_count * head_dim, 2),
    )(raw, raw, raw, cosine, sine, doc_ids[:, None, :], doc_ids[:, :, None])


def attend_back_kernel(
    scale, head_count, query_ref, grad_ref, shared, kv_next, cosine, sine, ids_row, ids_col,
    out, bias, grad_keys, grad_values,
):
    head_dim = query_ref.shape[1]
    head = pl.program_id(1)

    def turn_back(grads):
        return grads * cosine[...] - swap_halves(grads) * sine[...]

    @pl.when(head == 0)
    def _():
        set_bias(bias, ids_row, ids_col)
        grad_keys[...] = jnp.zeros_like(grad_keys)
        grad_values[...] = jnp.zeros_like(grad_values)

    @pl.when(head < head_count)
    def _():
        query, grad = query_ref[...], grad_ref[...]
        keys, values = shared[:, :head_dim], shared[:, head_dim:]
        probs = probabilities(query, keys, bias)
        grad_probs = dot(grad, values, (1, 1))
        inner = jnp.sum(probs * grad_probs, axis=-1, keepdims=True)
        grad_scores = (probs * (grad_probs - inner)).astype(BF16)
        grad_query = dot(grad_scores, keys, (1, 0), BF16).astype(F32) * scale
        out[...] = turn_back(grad_query).astype(BF16)
        grad_keys[...] += dot(grad_scores, query, (0, 0))
        grad_values[...] += dot(probs.astype(BF16), grad, (0, 0))

    @pl.when(head == head_count)
    def _():
        grads = (grad_keys[...] + kv_next[:, :head_dim].astype(F32)).astype(BF16).astype(F32)
        out[...] = turn_back(grads).astype(BF16)

    @pl.when(head == head_count + 1)
    def _():
        out[...] = (grad_values[...] + kv_next[:, head_dim:].astype(F32)).astype(BF16)

    @pl.when(head == head_count + 2)
    def _():
        out[...] = jnp.zeros_like(out)


def attend_back(queries, grads, shared, kv_next, cosine, sine, doc_ids, head_count, head_dim):
    seq_count, length = doc_ids.shape
    rows = seq_count * length
    block = (length, head_dim)
    own = pl.BlockSpec(block, lambda s, h: (s, jnp.minimum(h, head_count - 1)))
    whole = pl.BlockSpec(block, lambda s, h: (s, 0))
    pair = pl.BlockSpec((length, 2 * head_dim), lambda s, h: (s, 0))
    return pl.pallas_call(
        functools.partial(attend_back_kernel, head_dim ** (-0.5), head_count),
        grid=(seq_count, head_count + 3),
        in_specs=[
            own,
            own,
            pair,
            pair,
            whole,
            whole,
            pl.BlockSpec((1, 1, length), lambda s, h: (s, 0, 0)),
            pl.BlockSpec((1, length, 1), lambda s, h: (s, 0, 0)),
        ],
        out_specs=pl.BlockSpec(block, lambda s, h: (s, h)),
        out_shape=jax.ShapeDtypeStruct((rows, (head_count + 3) * head_dim), BF16),
        scratch_shapes=[
            pltpu.VMEM((length, length), F32),
            pltpu.VMEM(block, F32),
            pltpu.VMEM(block, F32),
        ],
        name="attend_back",
        **limits(14 * rows * length * head_dim * head_count, 8 * rows * head_count * head_dim, 2),
    )(queries, grads, shared, kv_next, cosine, sine, doc_ids[:, None, :], doc_ids[:, :, None])


def ffn_kernel(normed, cot, gate_w, up_w, down_w, hidden, grad_gate, grad_up, grad_normed, out):
    whole = lambda ref: lambda: ref[...]
    ffn_tile(
        normed, cot, whole(gate_w), whole(up_w), whole(down_w), hidden, grad_gate, grad_up,
        grad_normed, out,
    )


def ffn_tile(normed, cot, gate_w, up_w, down_w, hidden, grad_gate, grad_up, grad_normed, out):
    gate = dot(normed[...], gate_w(), (1, 0))
    up = dot(normed[...], up_w(), (1, 0))
    sigma = 1.0 / (1.0 + jnp.exp(-gate))
    activated = gate * sigma
    hidden[...] = (activated * up).astype(BF16)
    grad_hidden = dot(cot[...], down_w(), (1, 1), BF16).astype(F32)
    grad_up[...] = (grad_hidden * activated).astype(BF16)
    grad_gate[...] = (grad_hidden * up * (sigma * (1.0 + gate * (1.0 - sigma)))).astype(BF16)
    total = dot(grad_gate[...], gate_w(), (1, 1)) + dot(grad_up[...], up_w(), (1, 1))
    grad_normed[...] = total.astype(BF16)
    out[...] = dot(hidden[...], down_w(), (1, 0), BF16)


def ffn_held_kernel(
    spot, normed, cot, held, down, hidden, grad_gate, grad_up, grad_normed, out,
    gate_w, up_w, down_w, sems,
):
    count, f_size, rows, units = gate_w.shape
    first = pl.program_id(0) == 0
    copies = [
        [
            pltpu.make_async_copy(held.at[:, k, which], buffer.at[spot[0] ^ k], sems.at[which, k])
            for k in range(count)
        ]
        for which, buffer in enumerate((gate_w, up_w))
    ]
    copies.append([pltpu.make_async_copy(down, down_w, sems.at[2, 0])])

    @pl.when(first)
    def _():
        for some in copies:
            for copy in some:
                copy.start()

    def ready(which, buffer):
        @pl.when(first)
        def _():
            for copy in copies[which]:
                copy.wait()

        return buffer

    units_of = lambda buffer: buffer[...].reshape(count * f_size * rows, units)
    seen = set()

    def weight(which, buffer, value):
        def read():
            if which not in seen:
                seen.add(which)
                ready(which, buffer)
            return value(buffer)

        return read

    ffn_tile(
        normed, cot, weight(0, gate_w, units_of), weight(1, up_w, units_of),
        weight(2, down_w, lambda ref: ref[...]), hidden, grad_gate, grad_up, grad_normed, out,
    )


def ffn_held(spot, normed, cot, held, down):
    count, width = normed.shape
    f_size, t_size, _, rows, units = held.shape
    tile = math.gcd(count, 256)
    token = pl.BlockSpec((tile, width), lambda t: (t, 0))
    inner = pl.BlockSpec((tile, units), lambda t: (t, 0))
    weights = pltpu.VMEM((t_size, f_size, rows, units), BF16)
    return pl.pallas_call(
        ffn_held_kernel,
        grid=(count // tile,),
        in_specs=[pl.BlockSpec(memory_space=pltpu.SMEM), token, token]
        + [pl.BlockSpec(memory_space=pl.ANY)] * 2,
        out_specs=[inner, inner, inner, token, token],
        out_shape=[jax.ShapeDtypeStruct((count, units), BF16)] * 3
        + [jax.ShapeDtypeStruct((count, width), BF16)] * 2,
        scratch_shapes=[
            weights,
            weights,
            pltpu.VMEM((units, width), BF16),
            pltpu.SemaphoreType.DMA((3, t_size)),
        ],
        name="ffn",
        **limits(12 * count * width * units, 6 * width * units + 8 * count * width),
    )(spot, normed, cot, held, down)


def ffn(normed, cot, gate_w, up_w, down_w):
    count, width = normed.shape
    units = gate_w.shape[1]
    tile = math.gcd(count, 256)
    token = pl.BlockSpec((tile, width), lambda t: (t, 0))
    inner = pl.BlockSpec((tile, units), lambda t: (t, 0))
    fixed = lambda shape: pl.BlockSpec(shape, lambda t: (0, 0), pipeline_mode=pl.Buffered(1))
    return pl.pallas_call(
        ffn_kernel,
        grid=(count // tile,),
        in_specs=[token, token, fixed(gate_w.shape), fixed(up_w.shape), fixed(down_w.shape)],
        out_specs=[inner, inner, inner, token, token],
        out_shape=[jax.ShapeDtypeStruct((count, units), BF16)] * 3
        + [jax.ShapeDtypeStruct((count, width), BF16)] * 2,
        name="ffn",
        **limits(12 * count * width * units, 6 * width * units + 8 * count * width),
    )(normed, cot, gate_w, up_w, down_w)


def dp_swap(value, k):
    size = lax.axis_size("dp")
    return lax.ppermute(value, "dp", [(i, i ^ k) for i in range(size)])


def z_swap(value, k):
    size = lax.axis_size("fsdp")
    return lax.ppermute(value, "fsdp", [(i, i ^ (2 * k)) for i in range(size)])


def core_swap(value):
    size = lax.axis_size("fsdp")
    return lax.ppermute(value, "fsdp", [(i, i ^ 1) for i in range(size)])


def pick(array, index, axis=0):
    return lax.dynamic_index_in_dim(array, index, axis, keepdims=False)


def put(buffer, piece, index, axis=0):
    return lax.dynamic_update_index_in_dim(buffer, piece, index, axis)


def plane_gather(value):
    size = lax.axis_size("dp")
    if size != 4:
        return [value] + [dp_swap(value, k) for k in range(1, size)]
    half = value.shape[0] // 2
    one, two = dp_swap(value, 1), dp_swap(value, 2)
    first = dp_swap(one[:half], 2)
    second = dp_swap(two[half:], 1)
    return [value, one, two, jnp.concatenate([first, second], axis=0)]


def plane_scatter(parts):
    size = len(parts)
    if size != 4:
        total = parts[0].astype(F32)
        for k in range(1, size):
            total = total + dp_swap(parts[k], k).astype(F32)
        return total
    half = parts[0].shape[0] // 2
    far_two = dp_swap(parts[3][:half], 1)
    far_one = dp_swap(parts[3][half:], 2)
    for_two = jnp.concatenate(
        [(parts[2][:half].astype(F32) + far_two.astype(F32)).astype(BF16), parts[2][half:]], axis=0
    )
    for_one = jnp.concatenate(
        [parts[1][:half], (parts[1][half:].astype(F32) + far_one.astype(F32)).astype(BF16)], axis=0
    )
    return (
        parts[0].astype(F32)
        + dp_swap(for_one, 1).astype(F32)
        + dp_swap(for_two, 2).astype(F32)
    )


def line_scatter(terms):
    count = terms.shape[0]
    size = lax.axis_size("fsdp")
    z = lax.axis_index("fsdp") // 2
    right = left = None
    for step in range(count - 1):
        out = pick(terms, jnp.clip(count - 1 - step + z, 0, count - 1))
        if right is not None:
            out = (out.astype(F32) + right.astype(F32)).astype(BF16)
        right = lax.ppermute(
            out, "fsdp", [(i, i + 2) for i in range(size - 2) if i // 2 <= step]
        )
        out = pick(terms, jnp.clip(z - (count - 1 - step), 0, count - 1))
        if left is not None:
            out = (out.astype(F32) + left.astype(F32)).astype(BF16)
        left = lax.ppermute(
            out, "fsdp", [(i, i - 2) for i in range(2, size) if count - 1 - i // 2 <= step]
        )
    return pick(terms, z).astype(F32) + right.astype(F32) + left.astype(F32)


def gather_rows(block):
    t_size, f_size = lax.axis_size("dp"), lax.axis_size("fsdp")
    z_size = f_size // 2
    dp, fs = lax.axis_index("dp"), lax.axis_index("fsdp")
    z, core = fs // 2, fs % 2
    rows, cols = block.shape
    line = jnp.zeros((z_size, rows, cols), block.dtype)
    line = put(line, block, z)
    for k in range(1, z_size):
        line = put(line, z_swap(block, k), z ^ k)
    plane = jnp.zeros((t_size, z_size, rows, cols), block.dtype)
    for k, piece in enumerate(plane_gather(line)):
        plane = put(plane, piece, dp ^ k)
    whole = jnp.zeros((t_size, z_size, 2, rows, cols), block.dtype)
    whole = put(whole, plane, core, 2)
    whole = put(whole, core_swap(plane), 1 - core, 2)
    return whole.reshape(t_size * f_size * rows, cols)


def core_sum(mine, other):
    return (mine.astype(F32) + core_swap(other).astype(F32)).astype(BF16)


def scatter_rows(grads):
    t_size, f_size = lax.axis_size("dp"), lax.axis_size("fsdp")
    z_size = f_size // 2
    dp, fs = lax.axis_index("dp"), lax.axis_index("fsdp")
    core = fs % 2
    rows = grads.shape[0] // (t_size * f_size)
    split = grads.reshape(t_size, z_size, 2, rows, grads.shape[1])
    chip = core_sum(pick(split, core, 2), pick(split, 1 - core, 2))
    line = plane_scatter([pick(chip, dp ^ k) for k in range(t_size)])
    return line_scatter(line.astype(BF16))


def scatter_fsdp(split, axis):
    f_size = lax.axis_size("fsdp")
    core = lax.axis_index("fsdp") % 2
    shape = split.shape
    pairs = split.reshape(shape[:axis] + (f_size // 2, 2) + shape[axis + 1 :])
    chip = core_sum(pick(pairs, core, axis + 1), pick(pairs, 1 - core, axis + 1))
    return line_scatter(jnp.moveaxis(chip, axis, 0))


def place():
    fs = lax.axis_index("fsdp")
    return jnp.stack([lax.axis_index("dp"), fs // 2, fs % 2]).astype(jnp.int32)


def slices_kernel(spot, gate, up, *outs):
    units = outs[0].shape[-1]
    for k, out in enumerate(outs):
        at = pl.ds(pl.multiple_of((spot[0] ^ k) * units, units), units)
        out[0] = gate[:, at].astype(BF16)
        out[1] = up[:, at].astype(BF16)


def slices(spot, gate, up, count):
    rows, units = gate.shape[0], gate.shape[1] // count
    whole = pl.BlockSpec(memory_space=pltpu.VMEM)
    return pl.pallas_call(
        slices_kernel,
        in_specs=[pl.BlockSpec(memory_space=pltpu.SMEM), whole, whole],
        out_specs=[whole] * count,
        out_shape=[jax.ShapeDtypeStruct((2, rows, units), BF16)] * count,
        name="slices",
        **limits(0, 12 * gate.size, 0),
    )(spot, gate, up)


LINE_ORDER = (0, 2, 1, 3)
PIECES = ((0, (0, 2, 1, 3)), (1, (0, 2, 1, 3)), (2, (0, 2, 1, 3)), (3, (0, 2)), (3, (1, 3)))


def fetch_rows(spot, pieces, held, sems):
    z, core = spot[1], spot[2]
    copies = [[] for _ in range(4)]
    for side in range(2):
        for (k, line), piece in zip(PIECES, pieces[side * len(PIECES) :]):
            for at, j in enumerate(line):
                slot = held.at[k, z ^ j, core ^ side]
                sem = sems.at[k, 2 * j + side]
                copies[k].append(pltpu.make_async_copy(piece.at[at], slot, sem))
    for some in copies:
        for copy in some:
            copy.start()
    return copies


def gathered_dot_kernel(back, spot, left, *refs):
    pieces, (out, held, sems) = refs[:-3], refs[-3:]
    copies = fetch_rows(spot, pieces, held, sems)
    count, z_size, cores, rows, cols = held.shape
    block = z_size * cores * rows
    for k in range(count):
        for copy in copies[k]:
            copy.wait()
        weight = held[k].reshape(block, cols)
        at = pl.ds(pl.multiple_of((spot[0] ^ k) * block, block), block)
        if back:
            out[:, at] = dot(left[...], weight, (1, 1), out.dtype)
        elif k == 0:
            out[...] = dot(left[:, at], weight, (1, 0))
        else:
            out[...] += dot(left[:, at], weight, (1, 0))


def gathered_dot(spot, left, pieces, back=False, kind=F32):
    rows, cols = pieces[0].shape[1:]
    count, width = left.shape[0], 32 * rows if back else cols
    whole = pl.BlockSpec(memory_space=pltpu.VMEM)
    return pl.pallas_call(
        functools.partial(gathered_dot_kernel, back),
        in_specs=[pl.BlockSpec(memory_space=pltpu.SMEM), whole]
        + [pl.BlockSpec(memory_space=pl.ANY)] * len(pieces),
        out_specs=whole,
        out_shape=jax.ShapeDtypeStruct((count, width), kind),
        scratch_shapes=[
            pltpu.VMEM((4, 4, 2, rows, cols), BF16),
            pltpu.SemaphoreType.DMA((4, 8)),
        ],
        name="gathered_dot",
        **limits(64 * count * rows * cols, 64 * rows * cols + 4 * count * width, 0),
    )(spot, left, *pieces)


def gather_line(block):
    two = jnp.stack([block, z_swap(block, 2)])
    return jnp.concatenate([two, z_swap(two, 1)])


def gather_plane(line):
    one, two = dp_swap(line, 1), dp_swap(line, 2)
    half = line.shape[0] // 2
    return [line, one, two, dp_swap(one[:half], 2), dp_swap(two[half:], 1)]


def spread(line):
    mine = gather_plane(line)
    return mine + [core_swap(piece) for piece in mine]


def after(value, *others):
    return lax.optimization_barrier((value, *others))[0]


def gather_gains(spot, pieces):
    dp, z, core = spot[0], spot[1], spot[2]
    rows = pieces[0].shape[1]
    ends = [piece[:, :, -128:] for piece in pieces]
    sides = []
    for side in (ends[:5], ends[5:]):
        far = jnp.concatenate(side[3:])
        sides.append(jnp.stack(side[:3] + [far]))
    got = jnp.stack(sides, axis=2)
    got = got[dp ^ jnp.arange(4)]
    line = jnp.array([0, 2, 1, 3], jnp.int32)
    got = got[:, line[z ^ jnp.arange(4)]]
    return got[:, :, core ^ jnp.arange(2)].reshape(32 * rows, 128)


def row_grads_kernel(spot, left, right, *refs):
    extra = refs[0] if len(refs) == 4 else None
    mine, other, held = refs[-3:]
    count, _, rows, cols = held.shape
    found = dot(left[...], right[...], (0, 0), BF16)
    for i in range(count):
        for core in range(2):
            at = (2 * i + core) * rows
            held[i, core, :, : found.shape[1]] = found[at : at + rows]
            if extra is not None:
                held[i, core, :, found.shape[1] :] = extra[at : at + rows]
    z, core = spot[1], spot[2]
    for half in range(2):
        for at in range(2):
            mine[half, 0, at] = held[z ^ (2 * at + half), core]
            other[half, 0, at] = held[z ^ (2 * at + half), 1 - core]


def row_grads(spot, left, right, right_cols, extra=None):
    count, width = left.shape
    rows = width // 32
    cols = right_cols + (0 if extra is None else extra.shape[1])
    turn = lambda k, spot: spot[0] ^ k ^ (k >> 1)
    out = pl.BlockSpec((2, 1, 2, rows, cols), lambda k, spot: (0, k, 0, 0, 0))
    specs = [
        pl.BlockSpec((count, width // 4), lambda k, spot: (0, turn(k, spot))),
        pl.BlockSpec((count, right_cols), lambda k, spot: (0, 0)),
    ]
    operands = [left, right]
    if extra is not None:
        specs.append(pl.BlockSpec((width // 4, extra.shape[1]), lambda k, spot: (turn(k, spot), 0)))
        operands.append(extra)
    return pl.pallas_call(
        row_grads_kernel,
        grid_spec=pltpu.PrefetchScalarGridSpec(
            num_scalar_prefetch=1,
            grid=(4,),
            in_specs=specs,
            out_specs=[out, out],
            scratch_shapes=[pltpu.VMEM((4, 2, rows, cols), BF16)],
        ),
        out_shape=[jax.ShapeDtypeStruct((2, 4, 2, rows, cols), BF16)] * 2,
        name="row_grads",
        **limits(2 * count * width * cols, 2 * width * cols + 2 * count * (width + cols)),
    )(spot, *operands)


def add_low(left, right):
    return (left.astype(F32) + right.astype(F32)).astype(BF16)


def scatter_line(terms):
    near = add_low(terms[:2], z_swap(terms[2:], 1))
    return near[0].astype(F32) + z_swap(near[1], 2).astype(F32)


def scatter_fast(mine, other):
    chip = add_low(mine, core_swap(other))
    even, odd = chip[0], chip[1]
    sent_even, sent_odd = dp_swap(even[1:3], 1), dp_swap(odd[2:4], 2)
    even_own, even_far = add_low(even[0], sent_even[0]), add_low(even[3], sent_even[1])
    odd_own, odd_far = add_low(odd[0], sent_odd[1]), add_low(odd[1], sent_odd[0])
    even = add_low(even_own, dp_swap(even_far, 2))
    odd = add_low(odd_own, dp_swap(odd_far, 1))
    return scatter_line(jnp.concatenate([even, odd]))


def unit_grads_kernel(spot, left, gate, up, mine, other, held):
    count, _, rows, units = held.shape
    z, core = spot[1], spot[2]
    for which, right in enumerate((gate, up)):
        found = dot(left[...], right[...], (0, 0), BF16)
        for i in range(count):
            for side in range(2):
                at = (2 * i + side) * rows
                held[i, side] = found[at : at + rows]
        for at, j in enumerate(LINE_ORDER):
            mine[at, 0, which] = held[z ^ j, core]
            other[at, 0, which] = held[z ^ j, 1 - core]


def unit_grads(spot, left, gate, up):
    count, width = left.shape
    units, rows = gate.shape[1], width // 32
    out = pl.BlockSpec((4, 1, 2, rows, units), lambda k, spot: (0, k, 0, 0, 0))
    right = pl.BlockSpec((count, units), lambda k, spot: (0, 0))
    return pl.pallas_call(
        unit_grads_kernel,
        grid_spec=pltpu.PrefetchScalarGridSpec(
            num_scalar_prefetch=1,
            grid=(4,),
            in_specs=[
                pl.BlockSpec((count, width // 4), lambda k, spot: (0, spot[0] ^ k)),
                right,
                right,
            ],
            out_specs=[out, out],
            scratch_shapes=[pltpu.VMEM((4, 2, rows, units), BF16)],
        ),
        out_shape=[jax.ShapeDtypeStruct((4, 4, 2, rows, units), BF16)] * 2,
        name="unit_grads",
        **limits(4 * count * width * units, 4 * width * units + 2 * count * (width + 2 * units)),
    )(spot, left, gate, up)


def down_grads_kernel(spot, left, right, mine, other, held):
    count, _, rows, cols = held.shape
    z, core = spot[1], spot[2]
    found = dot(left[...], right[...], (0, 0), BF16)
    for i in range(count):
        for side in range(2):
            at = (2 * i + side) * rows
            held[i, side] = found[at : at + rows]
    for at, j in enumerate(LINE_ORDER):
        mine[at] = held[z ^ j, core]
        other[at] = held[z ^ j, 1 - core]


def down_grads(spot, left, right):
    count, units = left.shape
    width = right.shape[1]
    rows, tile = units // 8, width // 4
    out = pl.BlockSpec((4, rows, tile), lambda n, spot: (0, 0, n))
    return pl.pallas_call(
        down_grads_kernel,
        grid_spec=pltpu.PrefetchScalarGridSpec(
            num_scalar_prefetch=1,
            grid=(4,),
            in_specs=[
                pl.BlockSpec((count, units), lambda n, spot: (0, 0)),
                pl.BlockSpec((count, tile), lambda n, spot: (0, n)),
            ],
            out_specs=[out, out],
            scratch_shapes=[pltpu.VMEM((4, 2, rows, tile), BF16)],
        ),
        out_shape=[jax.ShapeDtypeStruct((4, rows, width), BF16)] * 2,
        name="down_grads",
        **limits(2 * count * width * units, 2 * width * units + 2 * count * (width + units)),
    )(spot, left, right)


def update_units_kernel(which, rate, spot, weight, moment, average, *refs):
    pieces, outs = refs[:-3], refs[-3:]
    units = pieces[0].shape[-1]
    for k, piece in enumerate(pieces):
        at = pl.ds(pl.multiple_of((spot[0] ^ k) * units, units), units)
        results = update(
            weight[:, at], moment[:, at], average[:, at], piece[which].astype(F32), rate
        )
        for out, result in zip(outs, results):
            out[:, at] = result


def update_units(spot, weight, moment, average, pieces, which, rate):
    whole = pl.BlockSpec(memory_space=pltpu.VMEM)
    return pl.pallas_call(
        functools.partial(update_units_kernel, which, rate),
        in_specs=[pl.BlockSpec(memory_space=pltpu.SMEM)] + [whole] * (3 + len(pieces)),
        out_specs=[whole] * 3,
        out_shape=[jax.ShapeDtypeStruct(weight.shape, F32)] * 3,
        name="update_units",
        **limits(0, 32 * weight.size, 0),
    )(spot, weight, moment, average, *pieces)


def norm_back(grad_normed, scaled, inv_rms, gain_full):
    grad_scaled = grad_normed * gain_full
    grad_gain = jnp.sum(grad_normed * scaled, axis=0)
    grad_in = inv_rms * (
        grad_scaled - scaled * jnp.mean(grad_scaled * scaled, axis=-1, keepdims=True)
    )
    return (grad_gain, grad_in)


def update(weight, moment, average, grad, rate):
    moment_new = MOMENTUM * moment + grad
    weight_new = weight - rate * (grad + MOMENTUM * moment_new)
    average_new = AVERAGE * average + (1.0 - AVERAGE) * weight_new
    return (moment_new, weight_new, average_new)


def shards(
    tokens_in,
    out_grad,
    kv_grad_next,
    doc_ids,
    gains,
    gains_mom,
    gains_ema,
    w_query,
    query_mom,
    query_ema,
    w_keyval,
    keyval_mom,
    keyval_ema,
    w_output,
    output_mom,
    output_ema,
    w_gate,
    gate_mom,
    gate_ema,
    w_up,
    up_mom,
    up_ema,
    w_down,
    down_mom,
    down_ema,
):
    t_size, f_size = lax.axis_size("dp"), lax.axis_size("fsdp")
    dp = lax.axis_index("dp")
    seq_count, length = doc_ids.shape
    width = tokens_in.shape[1]
    head_dim = w_keyval.shape[1] // 2
    head_count = w_query.shape[1] // head_dim
    hidden_units = w_gate.shape[1]
    rows = seq_count * length
    heads_width = head_count * head_dim
    tokens_total = rows * t_size * f_size
    own_rows = w_query.shape[0]
    slice_units = hidden_units // t_size

    gain_cols = jnp.zeros((own_rows, 128), BF16).at[:, :2].set(gains.astype(BF16).T)
    qkv_block = jnp.concatenate([w_query.astype(BF16), w_keyval.astype(BF16), gain_cols], axis=1)
    fast = t_size == 4 and f_size == 8 and own_rows % 16 == 0
    spot = place()

    def to_slices(weight):
        split = weight.astype(BF16).reshape(own_rows, t_size, slice_units)
        held = jnp.zeros((t_size, own_rows, slice_units), BF16)
        held = put(held, pick(split, dp, 1), dp)
        for k in range(1, t_size):
            held = put(held, dp_swap(pick(split, dp ^ k, 1), k), dp ^ k)
        whole = lax.all_gather(held, "fsdp", axis=0)
        return jnp.swapaxes(whole, 0, 1).reshape(width, slice_units)

    if fast:
        qkv_line = gather_line(qkv_block)
        qkv_pieces = spread(qkv_line)
        output_line = gather_line(after(w_output.astype(BF16), qkv_line))
        output_pieces = spread(after(output_line, qkv_pieces[3], qkv_pieces[4]))
        pieces = slices(spot, w_gate, w_up, t_size)
        held = jnp.stack([pieces[0]] + [dp_swap(pieces[k], k) for k in range(1, t_size)])
        held = lax.all_gather(after(held, output_line), "fsdp", axis=0)
        gain_rows = gather_gains(spot, qkv_pieces)
        down_block = after(w_down.astype(BF16), qkv_pieces[1], qkv_pieces[2])
    else:
        qkv_full = gather_rows(qkv_block)
        output_full = gather_rows(w_output.astype(BF16))
        gate_slice = to_slices(w_gate)
        up_slice = to_slices(w_up)
        gain_rows = qkv_full[:, -128:]
        down_block = w_down.astype(BF16)
    down_slice = lax.all_gather(down_block, "fsdp", axis=0, tiled=True)
    cot_all = jnp.concatenate(plane_gather(out_grad), axis=0)

    inputs = tokens_in.astype(F32)
    inv_rms = lax.rsqrt(jnp.mean(inputs * inputs, axis=-1, keepdims=True) + EPS)
    scaled = inputs * inv_rms
    gains_full = gain_rows[:, :2].astype(F32).T
    gain_attn, gain_ffn = gains_full[0], gains_full[1]
    normed = (scaled * gain_attn).astype(BF16)
    raw = gathered_dot(spot, normed, qkv_pieces) if fast else dot(normed, qkv_full, (1, 0))
    cosine, sine = rotation(positions_of(doc_ids).reshape(rows), head_dim)
    queries, attended, shared = attend(raw, cosine, sine, doc_ids, head_count, head_dim)
    if fast:
        resid = inputs + gathered_dot(spot, attended, output_pieces)
    else:
        resid = inputs + dot(attended, output_full, (1, 0))

    inv_rms2 = lax.rsqrt(jnp.mean(resid * resid, axis=-1, keepdims=True) + EPS)
    scaled2 = resid * inv_rms2
    normed2 = (scaled2 * gain_ffn).astype(BF16)
    normed2_all = jnp.concatenate(plane_gather(normed2), axis=0)
    if fast:
        results = ffn_held(spot, normed2_all, cot_all, held, down_slice)
    else:
        results = ffn(normed2_all, cot_all, gate_slice, up_slice, down_slice)
    hidden, grad_gate, grad_up, grad_normed2_part, ffn_part = results
    grad_normed2 = plane_scatter(
        [grad_normed2_part[k * rows : (k + 1) * rows] for k in range(t_size)]
    )
    ffn_out = plane_scatter([ffn_part[k * rows : (k + 1) * rows] for k in range(t_size)])
    layer_out = resid + ffn_out
    def from_slices(grads):
        own = scatter_fsdp(grads.reshape(t_size, f_size, own_rows, slice_units), 1)
        own = own.reshape(t_size, own_rows, slice_units)
        held = jnp.zeros((own_rows, t_size, slice_units), F32)
        held = put(held, pick(own, dp), dp, 1)
        for k in range(1, t_size):
            sent = dp_swap(pick(own, dp ^ k).astype(BF16), k)
            held = put(held, sent.astype(F32), dp ^ k, 1)
        return held.reshape(own_rows, hidden_units)

    if fast:
        mine, other = down_grads(spot, hidden, cot_all)
        down_sum = scatter_line(add_low(mine, core_swap(other)))
        mine, other = unit_grads(spot, normed2_all, grad_gate, grad_up)
        unit_sum = scatter_line(add_low(mine, core_swap(other)))
        unit_pieces = [unit_sum[0]] + [
            dp_swap(unit_sum[k].astype(BF16), k) for k in range(1, t_size)
        ]
    else:
        grad_down_w = dot(hidden, cot_all, (0, 0), BF16)
        down_sum = scatter_fsdp(grad_down_w.reshape(f_size, -1, width), 0)
        gate_sum = from_slices(dot(normed2_all, grad_gate, (0, 0), BF16))
        up_sum = from_slices(dot(normed2_all, grad_up, (0, 0), BF16))

    grad_gain_ffn, grad_through = norm_back(grad_normed2, scaled2, inv_rms2, gain_ffn)
    grad_resid = out_grad.astype(F32) + grad_through
    grad_branch = grad_resid.astype(BF16)
    if fast:
        grad_attended = gathered_dot(spot, grad_branch, output_pieces, True, BF16)
    else:
        grad_attended = dot(grad_branch, output_full, (1, 1), BF16)
    if fast:
        output_sum = scatter_fast(*row_grads(spot, attended, grad_branch, width))
    else:
        output_sum = scatter_rows(dot(attended, grad_branch, (0, 0), BF16))
    grad_raw = attend_back(
        queries, grad_attended, shared, kv_grad_next, cosine, sine, doc_ids, head_count, head_dim
    )
    if fast:
        grad_normed = gathered_dot(spot, grad_raw, qkv_pieces, True)
    else:
        grad_normed = dot(grad_raw, qkv_full, (1, 1))
    grad_gain_attn, grad_first = norm_back(grad_normed, scaled, inv_rms, gain_attn)
    input_grad = grad_resid + grad_first
    gain_grads = jnp.zeros((width, 128), BF16)
    gain_grads = gain_grads.at[:, :2].set(
        jnp.stack([grad_gain_attn, grad_gain_ffn], axis=0).astype(BF16).T
    )
    if fast:
        raw_width = grad_raw.shape[1] - 128
        qkv_sum = scatter_fast(*row_grads(spot, normed, grad_raw, raw_width, gain_grads))
    else:
        qkv_sum = scatter_rows(dot(normed, grad_raw, (0, 0), BF16).at[:, -128:].set(gain_grads))
    query_sum = qkv_sum[:, :heads_width]
    keyval_sum = qkv_sum[:, heads_width : heads_width + 2 * head_dim]
    gains_sum = qkv_sum[:, -128:-126].T

    def rate(strength, fan):
        return strength / math.sqrt(fan * tokens_total)

    gains_out = update(gains, gains_mom, gains_ema, gains_sum, rate(0.1, 1))
    query_out = update(w_query, query_mom, query_ema, query_sum, rate(0.6, width))
    keyval_out = update(w_keyval, keyval_mom, keyval_ema, keyval_sum, rate(0.15, width))
    output_out = update(w_output, output_mom, output_ema, output_sum, rate(5.0, heads_width))
    if fast:
        strength = rate(0.6, width)
        gate_out = update_units(spot, w_gate, gate_mom, gate_ema, unit_pieces, 0, strength)
        up_out = update_units(spot, w_up, up_mom, up_ema, unit_pieces, 1, strength)
    else:
        gate_out = update(w_gate, gate_mom, gate_ema, gate_sum, rate(0.6, width))
        up_out = update(w_up, up_mom, up_ema, up_sum, rate(0.6, width))
    down_out = update(w_down, down_mom, down_ema, down_sum, rate(1.5, hidden_units))
    return (
        layer_out,
        shared.astype(F32),
        input_grad,
        *gains_out,
        *query_out,
        *keyval_out,
        *output_out,
        *gate_out,
        *up_out,
        *down_out,
    )


def solution(mesh):
    rows = P(BOTH, None)
    cols = P(None, BOTH)
    return jax.shard_map(
        shards,
        mesh=mesh,
        in_specs=(rows,) * 4 + (cols,) * 3 + (rows,) * 18,
        out_specs=(rows,) * 3 + (cols,) * 3 + (rows,) * 18,
        check_vma=False,
    )
```

```python
import functools
import math

import jax
import jax.numpy as jnp
from jax import lax
from jax.experimental import pallas as pl
from jax.experimental.pallas import tpu as pltpu
from jax.sharding import PartitionSpec as P

EPS = 1e-05
THETA = 10000.0
MOMENTUM = 0.9
AVERAGE = 0.75
NEG = -1e30
F32 = jnp.float32
BF16 = jnp.bfloat16
BOTH = ("dp", "fsdp")
COST = 0.0
VMEM_BYTES = 60 * 1024 * 1024


def positions_of(doc_ids):
    length = doc_ids.shape[-1]
    offsets = jnp.arange(length, dtype=jnp.int32)
    same = doc_ids[..., :, None] == doc_ids[..., None, :]
    starts = jnp.min(jnp.where(same, offsets, length), axis=-1)
    return offsets - starts


def rotation(positions, head_dim):
    half_dim = head_dim // 2
    inverse = THETA ** (-(jnp.arange(half_dim, dtype=F32) * 2.0) / head_dim)
    angles = positions.astype(F32)[..., None] * inverse
    cosine, sine = jnp.cos(angles), jnp.sin(angles)
    return (
        jnp.concatenate([cosine, cosine], axis=-1),
        jnp.concatenate([-sine, sine], axis=-1),
    )


def dot(left, right, contract, kind=F32):
    return lax.dot_general(
        left, right, ((contract[:1], contract[1:]), ((), ())), preferred_element_type=F32
    ).astype(kind)


def limits(flops=0, moved=0, steps=1):
    semantics = ("arbitrary",) * steps if steps else None
    return {
        "compiler_params": pltpu.CompilerParams(
            vmem_limit_bytes=VMEM_BYTES, dimension_semantics=semantics
        ),
        "cost_estimate": pl.CostEstimate(
            flops=int(flops * COST), bytes_accessed=int(moved * COST), transcendentals=0
        ),
    }


def swap_halves(values):
    return pltpu.roll(values, values.shape[-1] // 2, values.ndim - 1)


def set_bias(bias, ids_row, ids_col):
    shape = bias.shape
    later = lax.broadcasted_iota(jnp.int32, shape, 1) > lax.broadcasted_iota(jnp.int32, shape, 0)
    apart = (ids_col[0] != ids_row[0]) | later
    bias[...] = jnp.where(apart, NEG, 0.0)


def probabilities(query, keys, bias):
    scores = dot(query, keys, (1, 1)) + bias[...]
    weights = jnp.exp(scores - jnp.max(scores, axis=-1, keepdims=True))
    return weights / jnp.sum(weights, axis=-1, keepdims=True)


def attend_kernel(
    scale, q_raw, k_raw, v_raw, cosine, sine, ids_row, ids_col, queries, attended, shared, bias
):
    head_dim = q_raw.shape[1]

    @pl.when(pl.program_id(1) == 0)
    def _():
        set_bias(bias, ids_row, ids_col)
        key = k_raw[...]
        turned = key * cosine[...] + swap_halves(key) * sine[...]
        shared[:, :head_dim] = turned.astype(BF16)
        shared[:, head_dim:] = v_raw[...].astype(BF16)

    raw = q_raw[...]
    query = ((raw * cosine[...] + swap_halves(raw) * sine[...]) * scale).astype(BF16)
    queries[...] = query
    probs = probabilities(query, shared[:, :head_dim], bias).astype(BF16)
    attended[...] = dot(probs, shared[:, head_dim:], (1, 0), BF16)


def attend(raw, cosine, sine, doc_ids, head_count, head_dim):
    seq_count, length = doc_ids.shape
    rows = seq_count * length
    column = lambda which: pl.BlockSpec((length, head_dim), which)
    whole = pl.BlockSpec((length, head_dim), lambda s, h: (s, 0))
    return pl.pallas_call(
        functools.partial(attend_kernel, head_dim ** (-0.5)),
        grid=(seq_count, head_count),
        in_specs=[
            column(lambda s, h: (s, h)),
            column(lambda s, h: (s, head_count)),
            column(lambda s, h: (s, head_count + 1)),
            whole,
            whole,
            pl.BlockSpec((1, 1, length), lambda s, h: (s, 0, 0)),
            pl.BlockSpec((1, length, 1), lambda s, h: (s, 0, 0)),
        ],
        out_specs=[
            column(lambda s, h: (s, h)),
            column(lambda s, h: (s, h)),
            pl.BlockSpec((length, 2 * head_dim), lambda s, h: (s, 0)),
        ],
        out_shape=[
            jax.ShapeDtypeStruct((rows, head_count * head_dim), BF16),
            jax.ShapeDtypeStruct((rows, head_count * head_dim), BF16),
            jax.ShapeDtypeStruct((rows, 2 * head_dim), BF16),
        ],
        scratch_shapes=[pltpu.VMEM((length, length), F32)],
        name="attend",
        **limits(6 * rows * length * head_dim * head_count, 10 * rows * head_count * head_dim, 2),
    )(raw, raw, raw, cosine, sine, doc_ids[:, None, :], doc_ids[:, :, None])


def attend_back_kernel(
    scale, head_count, query_ref, grad_ref, shared, kv_next, cosine, sine, ids_row, ids_col,
    out, bias, grad_keys, grad_values,
):
    head_dim = query_ref.shape[1]
    head = pl.program_id(1)

    def turn_back(grads):
        return grads * cosine[...] - swap_halves(grads) * sine[...]

    @pl.when(head == 0)
    def _():
        set_bias(bias, ids_row, ids_col)
        grad_keys[...] = jnp.zeros_like(grad_keys)
        grad_values[...] = jnp.zeros_like(grad_values)

    @pl.when(head < head_count)
    def _():
        query, grad = query_ref[...], grad_ref[...]
        keys, values = shared[:, :head_dim], shared[:, head_dim:]
        probs = probabilities(query, keys, bias)
        grad_probs = dot(grad, values, (1, 1))
        inner = jnp.sum(probs * grad_probs, axis=-1, keepdims=True)
        grad_scores = (probs * (grad_probs - inner)).astype(BF16)
        grad_query = dot(grad_scores, keys, (1, 0), BF16).astype(F32) * scale
        out[...] = turn_back(grad_query).astype(BF16)
        grad_keys[...] += dot(grad_scores, query, (0, 0))
        grad_values[...] += dot(probs.astype(BF16), grad, (0, 0))

    @pl.when(head == head_count)
    def _():
        grads = (grad_keys[...] + kv_next[:, :head_dim].astype(F32)).astype(BF16).astype(F32)
        out[...] = turn_back(grads).astype(BF16)

    @pl.when(head == head_count + 1)
    def _():
        out[...] = (grad_values[...] + kv_next[:, head_dim:].astype(F32)).astype(BF16)

    @pl.when(head == head_count + 2)
    def _():
        out[...] = jnp.zeros_like(out)


def attend_back(queries, grads, shared, kv_next, cosine, sine, doc_ids, head_count, head_dim):
    seq_count, length = doc_ids.shape
    rows = seq_count * length
    block = (length, head_dim)
    own = pl.BlockSpec(block, lambda s, h: (s, jnp.minimum(h, head_count - 1)))
    whole = pl.BlockSpec(block, lambda s, h: (s, 0))
    pair = pl.BlockSpec((length, 2 * head_dim), lambda s, h: (s, 0))
    return pl.pallas_call(
        functools.partial(attend_back_kernel, head_dim ** (-0.5), head_count),
        grid=(seq_count, head_count + 3),
        in_specs=[
            own,
            own,
            pair,
            pair,
            whole,
            whole,
            pl.BlockSpec((1, 1, length), lambda s, h: (s, 0, 0)),
            pl.BlockSpec((1, length, 1), lambda s, h: (s, 0, 0)),
        ],
        out_specs=pl.BlockSpec(block, lambda s, h: (s, h)),
        out_shape=jax.ShapeDtypeStruct((rows, (head_count + 3) * head_dim), BF16),
        scratch_shapes=[
            pltpu.VMEM((length, length), F32),
            pltpu.VMEM(block, F32),
            pltpu.VMEM(block, F32),
        ],
        name="attend_back",
        **limits(14 * rows * length * head_dim * head_count, 8 * rows * head_count * head_dim, 2),
    )(queries, grads, shared, kv_next, cosine, sine, doc_ids[:, None, :], doc_ids[:, :, None])


def ffn_kernel(normed, cot, gate_w, up_w, down_w, hidden, grad_gate, grad_up, grad_normed, out):
    whole = lambda ref: lambda: ref[...]
    ffn_tile(
        normed, cot, whole(gate_w), whole(up_w), whole(down_w), hidden, grad_gate, grad_up,
        grad_normed, out,
    )


def ffn_tile(normed, cot, gate_w, up_w, down_w, hidden, grad_gate, grad_up, grad_normed, out):
    gate = dot(normed[...], gate_w(), (1, 0))
    up = dot(normed[...], up_w(), (1, 0))
    sigma = 1.0 / (1.0 + jnp.exp(-gate))
    activated = gate * sigma
    hidden[...] = (activated * up).astype(BF16)
    grad_hidden = dot(cot[...], down_w(), (1, 1), BF16).astype(F32)
    grad_up[...] = (grad_hidden * activated).astype(BF16)
    grad_gate[...] = (grad_hidden * up * (sigma * (1.0 + gate * (1.0 - sigma)))).astype(BF16)
    total = dot(grad_gate[...], gate_w(), (1, 1)) + dot(grad_up[...], up_w(), (1, 1))
    grad_normed[...] = total.astype(BF16)
    out[...] = dot(hidden[...], down_w(), (1, 0), BF16)


def ffn(normed, cot, gate_w, up_w, down_w):
    count, width = normed.shape
    units = gate_w.shape[1]
    tile = math.gcd(count, 256)
    token = pl.BlockSpec((tile, width), lambda t: (t, 0))
    inner = pl.BlockSpec((tile, units), lambda t: (t, 0))
    fixed = lambda shape: pl.BlockSpec(shape, lambda t: (0, 0), pipeline_mode=pl.Buffered(1))
    return pl.pallas_call(
        ffn_kernel,
        grid=(count // tile,),
        in_specs=[token, token, fixed(gate_w.shape), fixed(up_w.shape), fixed(down_w.shape)],
        out_specs=[inner, inner, inner, token, token],
        out_shape=[jax.ShapeDtypeStruct((count, units), BF16)] * 3
        + [jax.ShapeDtypeStruct((count, width), BF16)] * 2,
        name="ffn",
        **limits(12 * count * width * units, 6 * width * units + 8 * count * width),
    )(normed, cot, gate_w, up_w, down_w)


def dp_swap(value, k):
    size = lax.axis_size("dp")
    return lax.ppermute(value, "dp", [(i, i ^ k) for i in range(size)])


def z_swap(value, k):
    size = lax.axis_size("fsdp")
    return lax.ppermute(value, "fsdp", [(i, i ^ (2 * k)) for i in range(size)])


def core_swap(value):
    size = lax.axis_size("fsdp")
    return lax.ppermute(value, "fsdp", [(i, i ^ 1) for i in range(size)])


def pick(array, index, axis=0):
    return lax.dynamic_index_in_dim(array, index, axis, keepdims=False)


def put(buffer, piece, index, axis=0):
    return lax.dynamic_update_index_in_dim(buffer, piece, index, axis)


def plane_gather(value):
    size = lax.axis_size("dp")
    if size != 4:
        return [value] + [dp_swap(value, k) for k in range(1, size)]
    half = value.shape[0] // 2
    one, two = dp_swap(value, 1), dp_swap(value, 2)
    first = dp_swap(one[:half], 2)
    second = dp_swap(two[half:], 1)
    return [value, one, two, jnp.concatenate([first, second], axis=0)]


def plane_scatter(parts):
    size = len(parts)
    if size != 4:
        total = parts[0].astype(F32)
        for k in range(1, size):
            total = total + dp_swap(parts[k], k).astype(F32)
        return total
    half = parts[0].shape[0] // 2
    far_two = dp_swap(parts[3][:half], 1)
    far_one = dp_swap(parts[3][half:], 2)
    for_two = jnp.concatenate(
        [(parts[2][:half].astype(F32) + far_two.astype(F32)).astype(BF16), parts[2][half:]], axis=0
    )
    for_one = jnp.concatenate(
        [parts[1][:half], (parts[1][half:].astype(F32) + far_one.astype(F32)).astype(BF16)], axis=0
    )
    return (
        parts[0].astype(F32)
        + dp_swap(for_one, 1).astype(F32)
        + dp_swap(for_two, 2).astype(F32)
    )


def line_scatter(terms):
    count = terms.shape[0]
    size = lax.axis_size("fsdp")
    z = lax.axis_index("fsdp") // 2
    right = left = None
    for step in range(count - 1):
        out = pick(terms, jnp.clip(count - 1 - step + z, 0, count - 1))
        if right is not None:
            out = (out.astype(F32) + right.astype(F32)).astype(BF16)
        right = lax.ppermute(
            out, "fsdp", [(i, i + 2) for i in range(size - 2) if i // 2 <= step]
        )
        out = pick(terms, jnp.clip(z - (count - 1 - step), 0, count - 1))
        if left is not None:
            out = (out.astype(F32) + left.astype(F32)).astype(BF16)
        left = lax.ppermute(
            out, "fsdp", [(i, i - 2) for i in range(2, size) if count - 1 - i // 2 <= step]
        )
    return pick(terms, z).astype(F32) + right.astype(F32) + left.astype(F32)


def gather_rows(block):
    t_size, f_size = lax.axis_size("dp"), lax.axis_size("fsdp")
    z_size = f_size // 2
    dp, fs = lax.axis_index("dp"), lax.axis_index("fsdp")
    z, core = fs // 2, fs % 2
    rows, cols = block.shape
    line = jnp.zeros((z_size, rows, cols), block.dtype)
    line = put(line, block, z)
    for k in range(1, z_size):
        line = put(line, z_swap(block, k), z ^ k)
    plane = jnp.zeros((t_size, z_size, rows, cols), block.dtype)
    for k, piece in enumerate(plane_gather(line)):
        plane = put(plane, piece, dp ^ k)
    whole = jnp.zeros((t_size, z_size, 2, rows, cols), block.dtype)
    whole = put(whole, plane, core, 2)
    whole = put(whole, core_swap(plane), 1 - core, 2)
    return whole.reshape(t_size * f_size * rows, cols)


def core_sum(mine, other):
    return (mine.astype(F32) + core_swap(other).astype(F32)).astype(BF16)


def scatter_rows(grads):
    t_size, f_size = lax.axis_size("dp"), lax.axis_size("fsdp")
    z_size = f_size // 2
    dp, fs = lax.axis_index("dp"), lax.axis_index("fsdp")
    core = fs % 2
    rows = grads.shape[0] // (t_size * f_size)
    split = grads.reshape(t_size, z_size, 2, rows, grads.shape[1])
    chip = core_sum(pick(split, core, 2), pick(split, 1 - core, 2))
    line = plane_scatter([pick(chip, dp ^ k) for k in range(t_size)])
    return line_scatter(line.astype(BF16))


def scatter_fsdp(split, axis):
    f_size = lax.axis_size("fsdp")
    core = lax.axis_index("fsdp") % 2
    shape = split.shape
    pairs = split.reshape(shape[:axis] + (f_size // 2, 2) + shape[axis + 1 :])
    chip = core_sum(pick(pairs, core, axis + 1), pick(pairs, 1 - core, axis + 1))
    return line_scatter(jnp.moveaxis(chip, axis, 0))


def norm_back(grad_normed, scaled, inv_rms, gain_full):
    grad_scaled = grad_normed * gain_full
    grad_gain = jnp.sum(grad_normed * scaled, axis=0)
    grad_in = inv_rms * (
        grad_scaled - scaled * jnp.mean(grad_scaled * scaled, axis=-1, keepdims=True)
    )
    return (grad_gain, grad_in)


def update(weight, moment, average, grad, rate):
    moment_new = MOMENTUM * moment + grad
    weight_new = weight - rate * (grad + MOMENTUM * moment_new)
    average_new = AVERAGE * average + (1.0 - AVERAGE) * weight_new
    return (moment_new, weight_new, average_new)


LINE_ORDER = (0, 2, 1, 3)
PIECES = ((0, LINE_ORDER), (1, LINE_ORDER), (2, LINE_ORDER), (3, (0, 2)), (3, (1, 3)))
SMEM = pl.BlockSpec(memory_space=pltpu.SMEM)
VMEM = pl.BlockSpec(memory_space=pltpu.VMEM)
ANY = pl.BlockSpec(memory_space=pl.ANY)


def place():
    fs = lax.axis_index("fsdp")
    return jnp.stack([lax.axis_index("dp"), fs // 2, fs % 2]).astype(jnp.int32)


def after(value, *others):
    leaves, tree = jax.tree.flatten(value)
    kept = lax.optimization_barrier((*leaves, *others))[: len(leaves)]
    return jax.tree.unflatten(tree, kept)


SPLIT = 96


def slices_kernel(spot, gate, up, down, *outs):
    outs, packed = outs[:-1], outs[-1]
    units = packed.shape[1]
    for k, out in enumerate(outs):
        at = pl.ds(pl.multiple_of((spot[0] ^ k) * units, units), units)
        out[0] = gate[:, at].astype(BF16)
        out[1] = up[:, at].astype(BF16)
    rows, width = down.shape
    rest = width - units
    packed[:rows] = down[:, :units].astype(BF16)
    packed[rows:] = jnp.zeros((SPLIT, units), BF16)
    packed[rows : rows + SPLIT, :rest] = down[:SPLIT, units:].astype(BF16)
    packed[rows : 2 * rows - SPLIT, rest : 2 * rest] = down[SPLIT:, units:].astype(BF16)


def slices(spot, gate, up, down, count):
    rows, units = gate.shape[0], gate.shape[1] // count
    return pl.pallas_call(
        slices_kernel,
        in_specs=[SMEM, VMEM, VMEM, VMEM],
        out_specs=[VMEM] * (count + 1),
        out_shape=[jax.ShapeDtypeStruct((2, rows, units), BF16)] * count
        + [jax.ShapeDtypeStruct((down.shape[0] + SPLIT, units), BF16)],
        name="slices",
        **limits(0, 12 * gate.size, 0),
    )(spot, gate, up, down)


def gather_line(block):
    two, one = z_swap(block, 2), z_swap(block, 1)
    return jnp.stack([block, two, one, z_swap(two, 1)])


def plane_near(value):
    return dp_swap(value, 1), dp_swap(value, 2)


def plane_far(one, two):
    first, second = cut(one, 0), cut(two, 1)
    return dp_swap(first, 2), dp_swap(second, 1)


def cut_kernel(whole, out):
    out[...] = whole[...]


def cut(whole, index):
    half = whole.shape[0] // 2
    rest = (0,) * (whole.ndim - 1)
    steps = 2 if whole.ndim > 2 else half // 96
    block = (half // steps,) + whole.shape[1:]
    return pl.pallas_call(
        cut_kernel,
        grid=(steps,),
        in_specs=[pl.BlockSpec(block, lambda g: (index * steps + g,) + rest)],
        out_specs=pl.BlockSpec(block, lambda g: (g,) + rest),
        out_shape=jax.ShapeDtypeStruct((half,) + whole.shape[1:], whole.dtype),
        name="cut",
        **limits(0, 2 * whole.size),
    )(whole)


def fetch_rows(spot, pieces, held, sems):
    z, core = spot[1], spot[2]
    copies = [[] for _ in range(4)]
    for side in range(2):
        for (k, line), piece in zip(PIECES, pieces[side * len(PIECES) :]):
            for at, j in enumerate(line):
                slot = held.at[k, z ^ j, core ^ side]
                sem = sems.at[k, 2 * j + side]
                copies[k].append(pltpu.make_async_copy(piece.at[at], slot, sem))
    for some in copies:
        for copy in some:
            copy.start()
    return copies


def blocks_of(spot, copies, held):
    count, z_size, cores, rows, cols = held.shape
    size = z_size * cores * rows
    for k in range(count):
        for copy in copies[k]:
            copy.wait()
        at = pl.ds(pl.multiple_of((spot[0] ^ k) * size, size), size)
        yield k, at, held[k].reshape(size, cols)


def held_shapes(pieces):
    rows, cols = pieces[0].shape[1:]
    return [pltpu.VMEM((4, 4, 2, rows, cols), BF16), pltpu.SemaphoreType.DMA((4, 8))]


def inverse_rms(values):
    return lax.rsqrt(jnp.mean(values * values, axis=-1, keepdims=True) + EPS)


def enter_kernel(spot, tokens, *refs):
    pieces, (raw, normed, gains, held, sems) = refs[:-5], refs[-5:]
    copies = fetch_rows(spot, pieces, held, sems)
    values = tokens[...].astype(F32)
    inv_rms = inverse_rms(values)
    cols = raw.shape[1]
    for k, at, weight in blocks_of(spot, copies, held):
        turned = weight[:, cols:].astype(F32).T
        gains[:, at] = turned[: gains.shape[0]]
        scaled = tokens[:, at].astype(F32) * inv_rms
        normed[:, at] = (scaled * turned[:1]).astype(BF16)
        found = dot(normed[:, at], weight[:, :cols], (1, 0))
        raw[...] = found if k == 0 else raw[...] + found


def enter(spot, tokens, pieces):
    count, width = tokens.shape
    cols = pieces[0].shape[2] - 128
    return pl.pallas_call(
        enter_kernel,
        in_specs=[SMEM, VMEM] + [ANY] * len(pieces),
        out_specs=[VMEM] * 3,
        out_shape=[
            jax.ShapeDtypeStruct((count, cols), F32),
            jax.ShapeDtypeStruct((count, width), BF16),
            jax.ShapeDtypeStruct((8, width), F32),
        ],
        scratch_shapes=held_shapes(pieces),
        name="enter",
        **limits(2 * count * width * cols, 2 * width * cols, 0),
    )(spot, tokens, *pieces)


def leave_kernel(spot, attended, tokens, gains, *refs):
    pieces, (resid, normed, held, sems) = refs[:-4], refs[-4:]
    copies = fetch_rows(spot, pieces, held, sems)
    resid[...] = tokens[...].astype(F32)
    for _, at, weight in blocks_of(spot, copies, held):
        resid[...] += dot(attended[:, at], weight, (1, 0))
    values = resid[...]
    normed[...] = (values * inverse_rms(values) * gains[1:2]).astype(BF16)


def leave(spot, attended, tokens, gains, pieces):
    count, width = tokens.shape
    return pl.pallas_call(
        leave_kernel,
        in_specs=[SMEM] + [VMEM] * 3 + [ANY] * len(pieces),
        out_specs=[VMEM] * 2,
        out_shape=[
            jax.ShapeDtypeStruct((count, width), F32),
            jax.ShapeDtypeStruct((count, width), BF16),
        ],
        scratch_shapes=held_shapes(pieces),
        name="leave",
        **limits(2 * count * width * width, 2 * width * width, 0),
    )(spot, attended, tokens, gains, *pieces)


def leave_back_kernel(spot, grads, *refs):
    pieces, (out, held, sems) = refs[:-3], refs[-3:]
    copies = fetch_rows(spot, pieces, held, sems)
    for _, at, weight in blocks_of(spot, copies, held):
        out[:, at] = dot(grads[...], weight, (1, 1), BF16)


def leave_back(spot, grads, pieces):
    count, width = grads.shape
    return pl.pallas_call(
        leave_back_kernel,
        in_specs=[SMEM, VMEM] + [ANY] * len(pieces),
        out_specs=VMEM,
        out_shape=jax.ShapeDtypeStruct((count, width), BF16),
        scratch_shapes=held_shapes(pieces),
        name="leave_back",
        **limits(2 * count * width * width, 2 * width * width, 0),
    )(spot, grads, *pieces)


def enter_back_kernel(spot, grads, tokens, gains, grad_resid, *refs):
    pieces, (out, grad_gain, held, sems) = refs[:-4], refs[-4:]
    copies = fetch_rows(spot, pieces, held, sems)
    for _, at, weight in blocks_of(spot, copies, held):
        out[:, at] = dot(grads[...], weight, (1, 1))
    values = tokens[...].astype(F32)
    inv_rms = inverse_rms(values)
    total, through = norm_back(out[...], values * inv_rms, inv_rms, gains[:1])
    grad_gain[...] = jnp.broadcast_to(total[None], grad_gain.shape)
    out[...] = grad_resid[...] + through


def enter_back(spot, grads, tokens, gains, grad_resid, pieces):
    count, width = tokens.shape
    return pl.pallas_call(
        enter_back_kernel,
        in_specs=[SMEM] + [VMEM] * 4 + [ANY] * len(pieces),
        out_specs=[VMEM] * 2,
        out_shape=[
            jax.ShapeDtypeStruct((count, width), F32),
            jax.ShapeDtypeStruct((8, width), F32),
        ],
        scratch_shapes=held_shapes(pieces),
        name="enter_back",
        **limits(2 * count * width * width, 2 * width * width, 0),
    )(spot, grads, tokens, gains, grad_resid, *pieces)


TOKEN_ORDER = (1, 3, 2, 0)


def ffn_all_kernel(spot, *refs):
    ins, held_in = (refs[:5], refs[5:10]), refs[10]
    wholes, (hidden, grad_gate, grad_up, sums, out) = refs[11:13], refs[13:18]
    gate_w, up_w, down_w, tiles, grad_tile, out_tile, sems, in_sems, out_sems = refs[18:]
    count, f_size, rows, units = gate_w.shape
    step = pl.program_id(0)
    first = step == 0
    size = tiles.shape[2]
    half = size // 2
    copies = [
        [
            pltpu.make_async_copy(
                held_in.at[:, pl.ds((2 * k + which) * rows, rows)], buffer.at[spot[0] ^ k],
                sems.at[which, k],
            )
            for k in range(count)
        ]
        for which, buffer in enumerate((gate_w, up_w))
    ]
    above, (low, width) = 2 * count * rows, down_w.shape[1:]
    rest = width - units
    copies.append(
        [
            pltpu.make_async_copy(
                held_in.at[:, pl.ds(above, low)], down_w.at[:, :, pl.ds(0, units)], sems.at[2, 0]
            ),
            pltpu.make_async_copy(
                held_in.at[:, pl.ds(above + low, SPLIT), pl.ds(0, rest)],
                down_w.at[:, pl.ds(0, SPLIT), pl.ds(units, rest)],
                sems.at[2, 1],
            ),
            pltpu.make_async_copy(
                held_in.at[:, pl.ds(above + low, low - SPLIT), pl.ds(rest, rest)],
                down_w.at[:, pl.ds(SPLIT, low - SPLIT), pl.ds(units, rest)],
                sems.at[2, 2],
            ),
        ]
    )

    def brought(at):
        k, some = TOKEN_ORDER[at], []
        for which, pieces in enumerate(ins):
            slot = tiles.at[at % 2, which]
            parts = pieces[k : k + 1] if k < 3 else pieces[3:]
            for i, piece in enumerate(parts):
                target = slot.at[pl.ds(i * half, half)] if k == 3 else slot
                some.append(pltpu.make_async_copy(piece, target, in_sems.at[at % 2, which, i]))
        return some

    def kept(at):
        return [
            pltpu.make_async_copy(
                tiles.at[at % 2, which], whole.at[pl.ds(at * size, size)], out_sems.at[at % 2, which]
            )
            for which, whole in enumerate(wholes)
        ]

    for at in range(4):

        @pl.when(step == at)
        def _():
            if at == 0:
                for copy in brought(0):
                    copy.start()
                for held in copies:
                    for copy in held:
                        copy.start()
            for copy in brought(at):
                copy.wait()
            if at > 0:
                for copy in kept(at - 1):
                    copy.wait()
            for copy in kept(at):
                copy.start()
            if at < 3:
                for copy in brought(at + 1):
                    copy.start()

    normed, cot = tiles.at[step % 2, 0], tiles.at[step % 2, 1]

    def weight(which, buffer):
        waited = []

        def read():
            if not waited:
                waited.append(True)

                @pl.when(first)
                def _():
                    for copy in copies[which]:
                        copy.wait()

            return buffer[...].reshape(-1, buffer.shape[-1])

        return read

    ffn_tile(
        normed, cot, weight(0, gate_w), weight(1, up_w), weight(2, down_w),
        hidden, grad_gate, grad_up, grad_tile, out_tile,
    )
    for i in range(2):
        sums[i, 0] = grad_tile[i * half : (i + 1) * half]
        out[i, 0] = out_tile[i * half : (i + 1) * half]

    @pl.when(step == 3)
    def _():
        for copy in kept(3):
            copy.wait()


def ffn_all(spot, normed, cot, held_in, t_size, low):
    count, width = normed[0].shape
    half = count // 2
    f_size, above, units = held_in.shape
    rows = (above - low - SPLIT) // (2 * t_size)
    inner = pl.BlockSpec((count, units), lambda t: (t, 0))
    sums = pl.BlockSpec((2, 1, half, width), lambda t: (0, t, 0, 0))
    weights = pltpu.VMEM((t_size, f_size, rows, units), BF16)
    total = 4 * count
    return pl.pallas_call(
        ffn_all_kernel,
        grid=(4,),
        in_specs=[SMEM] + [ANY] * 11,
        out_specs=[ANY, ANY, inner, inner, inner, sums, sums],
        scratch_shapes=[
            weights,
            weights,
            pltpu.VMEM((f_size, low, width), BF16),
            pltpu.VMEM((2, 2, count, width), BF16),
            pltpu.VMEM((count, width), BF16),
            pltpu.VMEM((count, width), BF16),
            pltpu.SemaphoreType.DMA((3, t_size)),
            pltpu.SemaphoreType.DMA((2, 2, 2)),
            pltpu.SemaphoreType.DMA((2, 2)),
        ],
        out_shape=[jax.ShapeDtypeStruct((total, width), BF16)] * 2
        + [jax.ShapeDtypeStruct((total, units), BF16)] * 3
        + [jax.ShapeDtypeStruct((2, 4, half, width), BF16)] * 2,
        name="ffn_all",
        **limits(12 * total * width * units, 6 * width * units + 8 * total * width),
    )(spot, *normed, *cot, held_in)


class TokenSum:
    def __init__(self, terms):
        self.own = terms
        self.sent = add([[(terms, 0)], [(terms, 5)]], 2)
        self.a, self.b = dp_swap(self.sent[0], 1), dp_swap(self.sent[1], 2)

    def cross(self):
        self.crossed = add([[(self.own, 2), (self.a, 1)], [(self.own, 4), (self.b, 0)]], 1)
        self.last_a, self.last_b = dp_swap(self.crossed[0], 2), dp_swap(self.crossed[1], 1)

    def parts(self):
        return [
            [(flat(self.own), 3), (self.a, 0), (self.last_a, 0)],
            [(flat(self.own), 7), (self.b, 1), (self.last_b, 0)],
        ]


def add_kernel(counts, *refs):
    outs = refs[len(refs) - len(counts) :]
    at = 0
    for count, out in zip(counts, outs):
        total = refs[at][...].astype(F32)
        for ref in refs[at + 1 : at + count]:
            total = total + ref[...].astype(F32)
        out[...] = total.astype(out.dtype)
        at += count


def flat(array):
    return array.reshape((-1,) + array.shape[-2:])


def add(jobs, count, group=1):
    operands = [flat(array) for job in jobs for array, _ in job]
    starts = [start for job in jobs for _, start in job]
    block = (group,) + operands[0].shape[1:]
    spec = lambda start: pl.BlockSpec(block, lambda g: (g + start // group, 0, 0))
    return pl.pallas_call(
        functools.partial(add_kernel, [len(job) for job in jobs]),
        grid=(count // group,),
        in_specs=[spec(start) for start in starts],
        out_specs=[spec(0)] * len(jobs),
        out_shape=[jax.ShapeDtypeStruct((count,) + block[1:], BF16)] * len(jobs),
        name="add",
        **limits(0, 2 * (len(starts) + len(jobs)) * count * block[1] * block[2]),
    )(*operands)


def turns(step):
    return jnp.minimum(step, 2), jnp.maximum(step - 3, 0)


def half_specs(parts, rows):
    specs = []
    for side, terms in enumerate(parts):
        for array, start in terms:
            shape = (1, rows, array.shape[-1])
            specs.append(
                pl.BlockSpec(shape, lambda t, side=side, start=start: (start, turns(t)[side], 0))
            )
    return specs


def half_total(refs, side):
    some = refs[side * 3 : side * 3 + 3]
    return some[0][0].astype(F32) + some[1][0].astype(F32) + some[2][0].astype(F32)


def branch_kernel(resid, cot, gains, *refs):
    terms, (grad_resid, grad_branch, grad_gain) = refs[:6], refs[6:]
    step = pl.program_id(0)

    def finish(grads):
        inv_rms = inverse_rms(resid[...])
        total, through = norm_back(grads, resid[...] * inv_rms, inv_rms, gains[1:2])
        sums = jnp.broadcast_to(total[None], grad_gain.shape)

        @pl.when(step == 0)
        def _():
            grad_gain[...] = sums

        @pl.when(step > 0)
        def _():
            grad_gain[...] += sums

        grads = cot[...].astype(F32) + through
        grad_resid[...] = grads
        grad_branch[...] = grads.astype(BF16)

    for side in range(2):

        @pl.when(step // 3 == side)
        def _():
            finish(half_total(terms, side))


def branch(resid, cot, gains, parts):
    count, width = resid.shape
    rows = count // 6
    token = pl.BlockSpec((rows, width), lambda t: (t, 0))
    fixed = pl.BlockSpec((8, width), lambda t: (0, 0))
    return pl.pallas_call(
        branch_kernel,
        grid=(6,),
        in_specs=[token, token, fixed] + half_specs(parts, rows),
        out_specs=[token, token, fixed],
        out_shape=[
            jax.ShapeDtypeStruct((count, width), F32),
            jax.ShapeDtypeStruct((count, width), BF16),
            jax.ShapeDtypeStruct((8, width), F32),
        ],
        name="branch",
        **limits(0, 18 * count * width),
    )(resid, cot, gains, *[array for terms in parts for array, _ in terms])


def layer_out_kernel(resid, *refs):
    terms, out = refs[:6], refs[6]
    for side in range(2):

        @pl.when(pl.program_id(0) // 3 == side)
        def _():
            out[...] = resid[...] + half_total(terms, side)


def layer_out_of(resid, parts):
    count, width = resid.shape
    rows = count // 6
    token = pl.BlockSpec((rows, width), lambda t: (t, 0))
    return pl.pallas_call(
        layer_out_kernel,
        grid=(6,),
        in_specs=[token] + half_specs(parts, rows),
        out_specs=token,
        out_shape=jax.ShapeDtypeStruct((count, width), F32),
        name="layer_out",
        **limits(0, 14 * count * width),
    )(resid, *[array for terms in parts for array, _ in terms])


def row_grads_kernel(spot, left, right, *refs):
    gains = refs[:-3]
    mine, other, held = refs[-3:]
    count, _, rows, cols = held.shape
    found = dot(left[...], right[...], (0, 0), BF16)
    if gains:
        shape = (128, left.shape[1])
        which = lax.broadcasted_iota(jnp.int32, shape, 0)
        one, two = gains[0][:1], gains[1][:1]
        extra = jnp.where(which == 0, one, jnp.where(which == 1, two, 0.0)).T.astype(BF16)
    for i in range(count):
        for core in range(2):
            at = (2 * i + core) * rows
            held[i, core, :, : found.shape[1]] = found[at : at + rows]
            if gains:
                held[i, core, :, found.shape[1] :] = extra[at : at + rows]
    z, core = spot[1], spot[2]
    for half in range(2):
        for at in range(2):
            mine[half, 0, at] = held[z ^ (2 * at + half), core]
            other[half, 0, at] = held[z ^ (2 * at + half), 1 - core]


def row_grads(spot, left, right, right_cols, gains=()):
    count, width = left.shape
    rows = width // 32
    cols = right_cols + (128 if gains else 0)
    turn = lambda k, spot: spot[0] ^ k ^ (k >> 1)
    out = pl.BlockSpec((2, 1, 2, rows, cols), lambda k, spot: (0, k, 0, 0, 0))
    gain = pl.BlockSpec((8, width // 4), lambda k, spot: (0, turn(k, spot)))
    return pl.pallas_call(
        row_grads_kernel,
        grid_spec=pltpu.PrefetchScalarGridSpec(
            num_scalar_prefetch=1,
            grid=(4,),
            in_specs=[
                pl.BlockSpec((count, width // 4), lambda k, spot: (0, turn(k, spot))),
                pl.BlockSpec((count, right_cols), lambda k, spot: (0, 0)),
            ]
            + [gain] * len(gains),
            out_specs=[out, out],
            scratch_shapes=[pltpu.VMEM((4, 2, rows, cols), BF16)],
        ),
        out_shape=[jax.ShapeDtypeStruct((2, 4, 2, rows, cols), BF16)] * 2,
        name="row_grads",
        **limits(2 * count * width * cols, 2 * width * cols + 2 * count * (width + cols)),
    )(spot, left, right, *gains)


class RowSum:
    def __init__(self, mine, other):
        self.mine, self.other = mine, core_swap(other)

    def plane(self):
        pair = lambda start: [(self.mine, start), (self.other, start)]
        a, b = self.sent = add([pair(2), pair(12)], 4, 2)
        self.a, self.b = dp_swap(a, 1), dp_swap(b, 2)

    def cross(self):
        a, b = self.crossed = add(
            [
                [(self.mine, 6), (self.other, 6), (self.a, 2)],
                [(self.mine, 10), (self.other, 10), (self.b, 0)],
            ],
            2,
        )
        self.last_a, self.last_b = dp_swap(a, 2), dp_swap(b, 1)

    def near(self):
        terms = [(self.mine, 8), (self.other, 8), (self.b, 2), (self.last_b, 0)]
        self.odd = add([terms], 2)[0]
        self.line = z_swap(self.odd, 1)

    def terms(self, at):
        return [(x, at) for x in (self.mine, self.other, self.a, self.last_a, self.line)]

    def far(self):
        self.rest = add([self.terms(1)], 1)[0]
        self.last = z_swap(self.rest, 2)

    def final(self):
        return self.terms(0) + [(self.last, 0)]


class LineSum:
    def __init__(self, mine, other):
        self.mine, self.other = mine, core_swap(other)

    def line(self):
        blocks = self.mine.shape[0]
        count = flat(self.mine).shape[0]
        self.chip = add([[(self.mine, 0), (self.other, 0)]], count, count // blocks)[0]
        size = lax.axis_size("fsdp")
        groups = [list(range(core, size, 2)) for core in range(2)]
        self.total = lax.psum_scatter(
            self.chip, "fsdp", scatter_dimension=0, axis_index_groups=groups, tiled=True
        )


def chunk_dot(lefts, rights):
    found = dot(lefts[0][...], rights[0][...], (0, 0))
    for left, right in zip(lefts[1:], rights[1:]):
        found = found + dot(left[...], right[...], (0, 0))
    return found.astype(BF16)


def place_line(spot, found, held, mine, other):
    count, _, rows, _ = held.shape
    core = spot[2]
    for i in range(count):
        for side in range(2):
            at = (2 * i + side) * rows
            held[i, side] = found[at : at + rows]
    for at in range(count):
        mine[at] = held[at, core].reshape(mine.shape[1:])
        other[at] = held[at, 1 - core].reshape(other.shape[1:])


def line_grads_kernel(spot, *refs):
    mine, other, held = refs[-3:]
    chunks = (len(refs) - 3) // 2
    found = chunk_dot(refs[:chunks], refs[chunks : 2 * chunks])
    place_line(spot, found, held, mine, other)


def unit_grads(spot, lefts, rights):
    count, width = lefts[0].shape
    units, rows = rights[0].shape[1], width // 32
    out = pl.BlockSpec((4, 1, rows, units), lambda k, spot: (0, k, 0, 0))
    left = pl.BlockSpec((count, width // 4), lambda k, spot: (0, spot[0] ^ k))
    right = pl.BlockSpec((count, units), lambda k, spot: (0, 0), pipeline_mode=pl.Buffered(1))
    total = count * len(lefts)
    return pl.pallas_call(
        line_grads_kernel,
        grid_spec=pltpu.PrefetchScalarGridSpec(
            num_scalar_prefetch=1,
            grid=(4,),
            in_specs=[left] * len(lefts) + [right] * len(rights),
            out_specs=[out, out],
            scratch_shapes=[pltpu.VMEM((4, 2, rows, units), BF16)],
        ),
        out_shape=[jax.ShapeDtypeStruct((4, 4, rows, units), BF16)] * 2,
        name="unit_grads",
        **limits(2 * total * width * units, 2 * width * units + 2 * total * (width + units)),
    )(spot, *lefts, *rights)


def down_grads(spot, lefts, rights):
    count, units = lefts[0].shape
    width = rights[0].shape[1]
    rows, tile = units // 8, width // 4
    out = pl.BlockSpec((4, rows, tile), lambda n, spot: (0, 0, n))
    left = pl.BlockSpec((count, units), lambda n, spot: (0, 0), pipeline_mode=pl.Buffered(1))
    right = pl.BlockSpec((count, tile), lambda n, spot: (0, n))
    total = count * len(lefts)
    return pl.pallas_call(
        line_grads_kernel,
        grid_spec=pltpu.PrefetchScalarGridSpec(
            num_scalar_prefetch=1,
            grid=(4,),
            in_specs=[left] * len(lefts) + [right] * len(rights),
            out_specs=[out, out],
            scratch_shapes=[pltpu.VMEM((4, 2, rows, tile), BF16)],
        ),
        out_shape=[jax.ShapeDtypeStruct((4, rows, width), BF16)] * 2,
        name="down_grads",
        **limits(2 * total * width * units, 2 * width * units + 2 * total * (width + units)),
    )(spot, *lefts, *rights)


def sum_of(refs):
    total = refs[0][0].astype(F32)
    for ref in refs[1:]:
        total = total + ref[0].astype(F32)
    return total


def update_rows_kernel(rates, count, *refs):
    terms, rest = refs[:count], refs[count:]
    held = 3 * len(rates)
    ins, outs = rest[:held], rest[held:]
    grads = sum_of(terms)
    at = 0
    for i, rate in enumerate(rates):
        own = ins[3 * i : 3 * i + 3]
        cols = own[0].shape[1]
        piece = grads[:, at : at + cols]
        at += cols
        results = update(*[ref[...] for ref in own], piece, rate)
        for out, result in zip(outs[3 * i :], results):
            out[...] = result
    if at < grads.shape[1]:
        outs[-1][...] = grads[:, at:]


def update_rows(terms, weights, rates):
    operands = [flat(array) for array, _ in terms]
    block = (1,) + operands[0].shape[1:]
    left = block[2] - sum(w[0].shape[1] for w in weights)
    arrays = [array for some in weights for array in some]
    shapes = [jax.ShapeDtypeStruct(array.shape, F32) for array in arrays]
    if left:
        shapes.append(jax.ShapeDtypeStruct((block[1], left), F32))
    whole = lambda shape: pl.BlockSpec(shape, lambda g: (0, 0))
    return pl.pallas_call(
        functools.partial(update_rows_kernel, rates, len(terms)),
        grid=(1,),
        in_specs=[pl.BlockSpec(block, lambda g, start=start: (start, 0, 0)) for _, start in terms]
        + [whole(array.shape) for array in arrays],
        out_specs=[whole(shape.shape) for shape in shapes],
        out_shape=shapes,
        name="update_rows",
        **limits(0, 32 * arrays[0].size),
    )(*operands, *arrays)


def update_units_kernel(rate, spot, weight, moment, average, *refs):
    pieces, outs = refs[:4], refs[4:]
    units = pieces[0].shape[-1]
    for k in range(4):
        grads = pieces[k][0].astype(F32)
        at = pl.ds(pl.multiple_of((spot[0] ^ k) * units, units), units)
        results = update(weight[:, at], moment[:, at], average[:, at], grads, rate)
        for out, result in zip(outs, results):
            out[:, at] = result


def update_units(spot, weight, moment, average, pieces, rate):
    block = (1,) + pieces[0].shape[1:]
    first = pl.BlockSpec(block, lambda g: (0, 0, 0))
    whole = pl.BlockSpec(weight.shape, lambda g: (0, 0))
    return pl.pallas_call(
        functools.partial(update_units_kernel, rate),
        grid=(1,),
        in_specs=[SMEM] + [whole] * 3 + [first] * 4,
        out_specs=[whole] * 3,
        out_shape=[jax.ShapeDtypeStruct(weight.shape, F32)] * 3,
        name="update_units",
        **limits(0, 32 * weight.size),
    )(spot, weight, moment, average, *pieces)


def shards_any(
    tokens_in,
    out_grad,
    kv_grad_next,
    doc_ids,
    gains,
    gains_mom,
    gains_ema,
    w_query,
    query_mom,
    query_ema,
    w_keyval,
    keyval_mom,
    keyval_ema,
    w_output,
    output_mom,
    output_ema,
    w_gate,
    gate_mom,
    gate_ema,
    w_up,
    up_mom,
    up_ema,
    w_down,
    down_mom,
    down_ema,
):
    t_size, f_size = lax.axis_size("dp"), lax.axis_size("fsdp")
    dp = lax.axis_index("dp")
    seq_count, length = doc_ids.shape
    width = tokens_in.shape[1]
    head_dim = w_keyval.shape[1] // 2
    head_count = w_query.shape[1] // head_dim
    hidden_units = w_gate.shape[1]
    rows = seq_count * length
    heads_width = head_count * head_dim
    tokens_total = rows * t_size * f_size
    own_rows = w_query.shape[0]
    slice_units = hidden_units // t_size

    gain_cols = jnp.zeros((own_rows, 128), BF16).at[:, :2].set(gains.astype(BF16).T)
    qkv_block = jnp.concatenate([w_query.astype(BF16), w_keyval.astype(BF16), gain_cols], axis=1)

    def to_slices(weight):
        split = weight.astype(BF16).reshape(own_rows, t_size, slice_units)
        held = jnp.zeros((t_size, own_rows, slice_units), BF16)
        held = put(held, pick(split, dp, 1), dp)
        for k in range(1, t_size):
            held = put(held, dp_swap(pick(split, dp ^ k, 1), k), dp ^ k)
        whole = lax.all_gather(held, "fsdp", axis=0)
        return jnp.swapaxes(whole, 0, 1).reshape(width, slice_units)

    qkv_full = gather_rows(qkv_block)
    output_full = gather_rows(w_output.astype(BF16))
    gate_slice = to_slices(w_gate)
    up_slice = to_slices(w_up)
    gain_rows = qkv_full[:, -128:]
    down_block = w_down.astype(BF16)
    down_slice = lax.all_gather(down_block, "fsdp", axis=0, tiled=True)
    cot_all = jnp.concatenate(plane_gather(out_grad), axis=0)

    inputs = tokens_in.astype(F32)
    inv_rms = lax.rsqrt(jnp.mean(inputs * inputs, axis=-1, keepdims=True) + EPS)
    scaled = inputs * inv_rms
    gains_full = gain_rows[:, :2].astype(F32).T
    gain_attn, gain_ffn = gains_full[0], gains_full[1]
    normed = (scaled * gain_attn).astype(BF16)
    raw = dot(normed, qkv_full, (1, 0))
    cosine, sine = rotation(positions_of(doc_ids).reshape(rows), head_dim)
    queries, attended, shared = attend(raw, cosine, sine, doc_ids, head_count, head_dim)
    resid = inputs + dot(attended, output_full, (1, 0))

    inv_rms2 = lax.rsqrt(jnp.mean(resid * resid, axis=-1, keepdims=True) + EPS)
    scaled2 = resid * inv_rms2
    normed2 = (scaled2 * gain_ffn).astype(BF16)
    normed2_all = jnp.concatenate(plane_gather(normed2), axis=0)
    results = ffn(normed2_all, cot_all, gate_slice, up_slice, down_slice)
    hidden, grad_gate, grad_up, grad_normed2_part, ffn_part = results
    grad_normed2 = plane_scatter(
        [grad_normed2_part[k * rows : (k + 1) * rows] for k in range(t_size)]
    )
    ffn_out = plane_scatter([ffn_part[k * rows : (k + 1) * rows] for k in range(t_size)])
    layer_out = resid + ffn_out
    def from_slices(grads):
        own = scatter_fsdp(grads.reshape(t_size, f_size, own_rows, slice_units), 1)
        own = own.reshape(t_size, own_rows, slice_units)
        held = jnp.zeros((own_rows, t_size, slice_units), F32)
        held = put(held, pick(own, dp), dp, 1)
        for k in range(1, t_size):
            sent = dp_swap(pick(own, dp ^ k).astype(BF16), k)
            held = put(held, sent.astype(F32), dp ^ k, 1)
        return held.reshape(own_rows, hidden_units)

    grad_down_w = dot(hidden, cot_all, (0, 0), BF16)
    down_sum = scatter_fsdp(grad_down_w.reshape(f_size, -1, width), 0)
    gate_sum = from_slices(dot(normed2_all, grad_gate, (0, 0), BF16))
    up_sum = from_slices(dot(normed2_all, grad_up, (0, 0), BF16))

    grad_gain_ffn, grad_through = norm_back(grad_normed2, scaled2, inv_rms2, gain_ffn)
    grad_resid = out_grad.astype(F32) + grad_through
    grad_branch = grad_resid.astype(BF16)
    grad_attended = dot(grad_branch, output_full, (1, 1), BF16)
    output_sum = scatter_rows(dot(attended, grad_branch, (0, 0), BF16))
    grad_raw = attend_back(
        queries, grad_attended, shared, kv_grad_next, cosine, sine, doc_ids, head_count, head_dim
    )
    grad_normed = dot(grad_raw, qkv_full, (1, 1))
    grad_gain_attn, grad_first = norm_back(grad_normed, scaled, inv_rms, gain_attn)
    input_grad = grad_resid + grad_first
    gain_grads = jnp.zeros((width, 128), BF16)
    gain_grads = gain_grads.at[:, :2].set(
        jnp.stack([grad_gain_attn, grad_gain_ffn], axis=0).astype(BF16).T
    )
    qkv_sum = scatter_rows(dot(normed, grad_raw, (0, 0), BF16).at[:, -128:].set(gain_grads))
    query_sum = qkv_sum[:, :heads_width]
    keyval_sum = qkv_sum[:, heads_width : heads_width + 2 * head_dim]
    gains_sum = qkv_sum[:, -128:-126].T

    def rate(strength, fan):
        return strength / math.sqrt(fan * tokens_total)

    gains_out = update(gains, gains_mom, gains_ema, gains_sum, rate(0.1, 1))
    query_out = update(w_query, query_mom, query_ema, query_sum, rate(0.6, width))
    keyval_out = update(w_keyval, keyval_mom, keyval_ema, keyval_sum, rate(0.15, width))
    output_out = update(w_output, output_mom, output_ema, output_sum, rate(5.0, heads_width))
    gate_out = update(w_gate, gate_mom, gate_ema, gate_sum, rate(0.6, width))
    up_out = update(w_up, up_mom, up_ema, up_sum, rate(0.6, width))
    down_out = update(w_down, down_mom, down_ema, down_sum, rate(1.5, hidden_units))
    return (
        layer_out,
        shared.astype(F32),
        input_grad,
        *gains_out,
        *query_out,
        *keyval_out,
        *output_out,
        *gate_out,
        *up_out,
        *down_out,
    )


def shards_fast(
    tokens_in,
    out_grad,
    kv_grad_next,
    doc_ids,
    gains,
    gains_mom,
    gains_ema,
    w_query,
    query_mom,
    query_ema,
    w_keyval,
    keyval_mom,
    keyval_ema,
    w_output,
    output_mom,
    output_ema,
    w_gate,
    gate_mom,
    gate_ema,
    w_up,
    up_mom,
    up_ema,
    w_down,
    down_mom,
    down_ema,
):
    t_size, f_size = lax.axis_size("dp"), lax.axis_size("fsdp")
    seq_count, length = doc_ids.shape
    width = tokens_in.shape[1]
    head_dim = w_keyval.shape[1] // 2
    head_count = w_query.shape[1] // head_dim
    hidden_units = w_gate.shape[1]
    rows = seq_count * length
    half = rows // 2
    heads_width = head_count * head_dim
    raw_width = heads_width + 2 * head_dim
    tokens_total = rows * t_size * f_size
    own_rows = w_query.shape[0]
    spot = place()

    gain_cols = jnp.zeros((own_rows, 128), BF16).at[:, :2].set(gains.astype(BF16).T)
    qkv_block = jnp.concatenate([w_query.astype(BF16), w_keyval.astype(BF16), gain_cols], axis=1)
    qkv_line = gather_line(qkv_block)

    *sent, packed = slices(spot, w_gate, w_up, w_down, t_size)
    got = [sent[0]] + [dp_swap(sent[k], k) for k in range(1, t_size)]
    packed = jnp.concatenate([flat(piece).reshape(-1, piece.shape[-1]) for piece in got] + [packed])
    output_line = gather_line(after(w_output.astype(BF16), qkv_line))
    units_all = lax.all_gather(after(packed, output_line), "fsdp", axis=0)

    qkv_near = plane_near(qkv_line)
    qkv_far = plane_far(*qkv_near)
    qkv_mine = [qkv_line, *qkv_near, *qkv_far]
    qkv_pieces = qkv_mine + [core_swap(piece) for piece in qkv_mine]
    output_near = plane_near(after(output_line, *qkv_far))
    cot_near = plane_near(after(out_grad, *qkv_pieces[8:]))

    raw, normed, gains_full = enter(spot, after(tokens_in, output_line), qkv_pieces)
    cosine, sine = rotation(positions_of(doc_ids).reshape(rows), head_dim)
    queries, attended, shared = attend(raw, cosine, sine, doc_ids, head_count, head_dim)
    output_mine = [output_line, *output_near, *plane_far(*after(output_near, attended))]
    output_pieces = output_mine + [core_swap(piece) for piece in output_mine]
    cot = [out_grad, *cot_near, *plane_far(*cot_near)]
    resid, normed2 = leave(spot, after(attended, *cot_near), tokens_in, gains_full, output_pieces)

    normed2_near = plane_near(normed2)
    normed2_all = [normed2, *normed2_near, *plane_far(*normed2_near)]
    tokens2, cots, hidden, grad_gate, grad_up, grad_terms, out_terms = ffn_all(
        spot, normed2_all, cot, units_all, t_size, w_down.shape[0]
    )
    normed2_sum = TokenSum(grad_terms)
    down = LineSum(*down_grads(spot, [after(hidden, *normed2_sum.sent)], [cots]))
    gate = LineSum(*unit_grads(spot, [after(tokens2, down.mine)], [grad_gate]))
    up = LineSum(*unit_grads(spot, [after(tokens2, gate.mine)], [grad_up]))
    normed2_sum.a, normed2_sum.b = after((normed2_sum.a, normed2_sum.b), up.mine)
    normed2_sum.cross()
    down.other = after(down.other, *normed2_sum.crossed)
    down.line()
    grad_resid, grad_branch, grad_gain_ffn = branch(
        after(resid, down.chip), out_grad, gains_full, normed2_sum.parts()
    )
    out_sum = TokenSum(after(out_terms, grad_branch))

    grad_attended = leave_back(spot, after(grad_branch, *out_sum.sent), output_pieces)
    gate.other = after(gate.other, grad_attended)
    gate.line()
    output = RowSum(*row_grads(spot, attended, after(grad_branch, grad_attended), width))
    grad_raw = attend_back(
        queries, after(grad_attended, output.mine, gate.chip), shared, kv_grad_next, cosine, sine,
        doc_ids, head_count, head_dim,
    )
    output.other, up.other = after((output.other, up.other), grad_raw)
    output.plane()
    up.line()
    grad_raw = after(grad_raw, up.chip, *output.sent, down.total)
    input_grad, grad_gain_attn = enter_back(
        spot, grad_raw, tokens_in, gains_full, grad_resid, qkv_pieces
    )
    out_sum.a, out_sum.b = after((out_sum.a, out_sum.b), input_grad)
    out_sum.cross()
    mine, other = row_grads(
        spot, after(normed, *out_sum.crossed), grad_raw, raw_width,
        (grad_gain_attn, grad_gain_ffn),
    )
    qkv = RowSum(mine, other)
    output.a, output.b = after((output.a, output.b), mine)
    output.cross()
    qkv.other = after(qkv.other, gate.total, *output.crossed)
    qkv.plane()

    def rate(strength, fan):
        return strength / math.sqrt(fan * tokens_total)

    def exchange(total):
        pieces = [total[k : k + 1] for k in range(t_size)]
        return pieces[:1] + [dp_swap(pieces[k], k) for k in range(1, t_size)]

    gate_pieces = exchange(flat(after(gate.total, *qkv.sent)))
    output.last_a, output.last_b, out_sum.last_a, out_sum.last_b, down.total = after(
        (output.last_a, output.last_b, out_sum.last_a, out_sum.last_b, down.total), *qkv.sent
    )
    output.near()
    layer_out = layer_out_of(resid, out_sum.parts())
    down_out = update_rows(
        [(down.total, 0)], [(w_down, down_mom, down_ema)], [rate(1.5, hidden_units)]
    )
    qkv.a, qkv.b = after((qkv.a, qkv.b), output.odd, layer_out, down_out[0])
    qkv.cross()
    output.line, gate_pieces = after((output.line, gate_pieces), *qkv.crossed)
    output.far()
    gate_out = update_units(spot, w_gate, gate_mom, gate_ema, gate_pieces, rate(0.6, width))
    qkv.last_a, qkv.last_b = after((qkv.last_a, qkv.last_b), output.rest, gate_out[0])
    qkv.near()
    up_pieces = exchange(flat(after(up.total, qkv.odd)))
    output_out = update_rows(
        [(after(x, qkv.odd), at) for x, at in output.final()], [(w_output, output_mom, output_ema)],
        [rate(5.0, heads_width)],
    )
    qkv.line = after(qkv.line, output_out[0])
    qkv.far()
    up_out = update_units(
        spot, w_up, up_mom, up_ema, after(up_pieces, qkv.rest), rate(0.6, width)
    )
    qkv.last = after(qkv.last, up_out[0])
    *qkv_out, left_over = update_rows(
        qkv.final(),
        [(w_query, query_mom, query_ema), (w_keyval, keyval_mom, keyval_ema)],
        [rate(0.6, width), rate(0.15, width)],
    )
    gains_out = update(gains, gains_mom, gains_ema, left_over[:, :2].T, rate(0.1, 1))
    return (
        layer_out,
        shared.astype(F32),
        input_grad,
        *gains_out,
        *qkv_out,
        *output_out,
        *gate_out,
        *up_out,
        *down_out,
    )


def solution(mesh):
    rows = P(BOTH, None)
    shards = shards_fast if dict(mesh.shape) == {"dp": 4, "fsdp": 8} else shards_any
    cols = P(None, BOTH)
    return jax.shard_map(
        shards,
        mesh=mesh,
        in_specs=(rows,) * 4 + (cols,) * 3 + (rows,) * 18,
        out_specs=(rows,) * 3 + (cols,) * 3 + (rows,) * 18,
        check_vma=False,
    )
```

```python
import functools
import math

import jax
import jax.numpy as jnp
from jax import lax
from jax.experimental import pallas as pl
from jax.experimental.pallas import tpu as pltpu
from jax.sharding import PartitionSpec as P

EPS = 1e-05
THETA = 10000.0
MOMENTUM = 0.9
AVERAGE = 0.75
NEG = -1e30
F32 = jnp.float32
BF16 = jnp.bfloat16
BOTH = ("dp", "fsdp")
COST = 40.0
VMEM_BYTES = 60 * 1024 * 1024


def positions_of(doc_ids):
    length = doc_ids.shape[-1]
    offsets = jnp.arange(length, dtype=jnp.int32)
    same = doc_ids[..., :, None] == doc_ids[..., None, :]
    starts = jnp.min(jnp.where(same, offsets, length), axis=-1)
    return offsets - starts


def rotation(positions, head_dim):
    half_dim = head_dim // 2
    inverse = THETA ** (-(jnp.arange(half_dim, dtype=F32) * 2.0) / head_dim)
    angles = positions.astype(F32)[..., None] * inverse
    cosine, sine = jnp.cos(angles), jnp.sin(angles)
    return (
        jnp.concatenate([cosine, cosine], axis=-1),
        jnp.concatenate([-sine, sine], axis=-1),
    )


def dot(left, right, contract, kind=F32):
    return lax.dot_general(
        left, right, ((contract[:1], contract[1:]), ((), ())), preferred_element_type=F32
    ).astype(kind)


def limits(flops=0, moved=0, steps=1):
    semantics = ("arbitrary",) * steps if steps else None
    return {
        "compiler_params": pltpu.CompilerParams(
            vmem_limit_bytes=VMEM_BYTES, dimension_semantics=semantics
        ),
        "cost_estimate": pl.CostEstimate(
            flops=int(flops * COST), bytes_accessed=int(moved * COST), transcendentals=0
        ),
    }


def swap_halves(values):
    return pltpu.roll(values, values.shape[-1] // 2, values.ndim - 1)


def set_bias(bias, ids_row, ids_col):
    shape = bias.shape
    later = lax.broadcasted_iota(jnp.int32, shape, 1) > lax.broadcasted_iota(jnp.int32, shape, 0)
    apart = (ids_col[0] != ids_row[0]) | later
    bias[...] = jnp.where(apart, NEG, 0.0)


def probabilities(query, keys, bias):
    scores = dot(query, keys, (1, 1)) + bias[...]
    weights = jnp.exp(scores - jnp.max(scores, axis=-1, keepdims=True))
    return weights / jnp.sum(weights, axis=-1, keepdims=True)


def attend_kernel(
    scale, q_raw, k_raw, v_raw, cosine, sine, ids_row, ids_col, queries, attended, shared, bias
):
    head_dim = q_raw.shape[1]

    @pl.when(pl.program_id(1) == 0)
    def _():
        set_bias(bias, ids_row, ids_col)
        key = k_raw[...]
        turned = key * cosine[...] + swap_halves(key) * sine[...]
        shared[:, :head_dim] = turned.astype(BF16)
        shared[:, head_dim:] = v_raw[...].astype(BF16)

    raw = q_raw[...]
    query = ((raw * cosine[...] + swap_halves(raw) * sine[...]) * scale).astype(BF16)
    queries[...] = query
    probs = probabilities(query, shared[:, :head_dim], bias).astype(BF16)
    attended[...] = dot(probs, shared[:, head_dim:], (1, 0), BF16)


def attend(raw, cosine, sine, doc_ids, head_count, head_dim):
    seq_count, length = doc_ids.shape
    rows = seq_count * length
    column = lambda which: pl.BlockSpec((length, head_dim), which)
    whole = pl.BlockSpec((length, head_dim), lambda s, h: (s, 0))
    return pl.pallas_call(
        functools.partial(attend_kernel, head_dim ** (-0.5)),
        grid=(seq_count, head_count),
        in_specs=[
            column(lambda s, h: (s, h)),
            column(lambda s, h: (s, head_count)),
            column(lambda s, h: (s, head_count + 1)),
            whole,
            whole,
            pl.BlockSpec((1, 1, length), lambda s, h: (s, 0, 0)),
            pl.BlockSpec((1, length, 1), lambda s, h: (s, 0, 0)),
        ],
        out_specs=[
            column(lambda s, h: (s, h)),
            column(lambda s, h: (s, h)),
            pl.BlockSpec((length, 2 * head_dim), lambda s, h: (s, 0)),
        ],
        out_shape=[
            jax.ShapeDtypeStruct((rows, head_count * head_dim), BF16),
            jax.ShapeDtypeStruct((rows, head_count * head_dim), BF16),
            jax.ShapeDtypeStruct((rows, 2 * head_dim), BF16),
        ],
        scratch_shapes=[pltpu.VMEM((length, length), F32)],
        name="attend",
        **limits(6 * rows * length * head_dim * head_count, 10 * rows * head_count * head_dim, 2),
    )(raw, raw, raw, cosine, sine, doc_ids[:, None, :], doc_ids[:, :, None])


def attend_back_kernel(
    scale, head_count, query_ref, grad_ref, shared, kv_next, cosine, sine, ids_row, ids_col,
    out, bias, grad_keys, grad_values,
):
    head_dim = query_ref.shape[1]
    head = pl.program_id(1)

    def turn_back(grads):
        return grads * cosine[...] - swap_halves(grads) * sine[...]

    @pl.when(head == 0)
    def _():
        set_bias(bias, ids_row, ids_col)
        grad_keys[...] = jnp.zeros_like(grad_keys)
        grad_values[...] = jnp.zeros_like(grad_values)

    @pl.when(head < head_count)
    def _():
        query, grad = query_ref[...], grad_ref[...]
        keys, values = shared[:, :head_dim], shared[:, head_dim:]
        probs = probabilities(query, keys, bias)
        grad_probs = dot(grad, values, (1, 1))
        inner = jnp.sum(probs * grad_probs, axis=-1, keepdims=True)
        grad_scores = (probs * (grad_probs - inner)).astype(BF16)
        grad_query = dot(grad_scores, keys, (1, 0), BF16).astype(F32) * scale
        out[...] = turn_back(grad_query).astype(BF16)
        grad_keys[...] += dot(grad_scores, query, (0, 0))
        grad_values[...] += dot(probs.astype(BF16), grad, (0, 0))

    @pl.when(head == head_count)
    def _():
        grads = (grad_keys[...] + kv_next[:, :head_dim].astype(F32)).astype(BF16).astype(F32)
        out[...] = turn_back(grads).astype(BF16)

    @pl.when(head == head_count + 1)
    def _():
        out[...] = (grad_values[...] + kv_next[:, head_dim:].astype(F32)).astype(BF16)

    @pl.when(head == head_count + 2)
    def _():
        out[...] = jnp.zeros_like(out)


def attend_back(queries, grads, shared, kv_next, cosine, sine, doc_ids, head_count, head_dim):
    seq_count, length = doc_ids.shape
    rows = seq_count * length
    block = (length, head_dim)
    own = pl.BlockSpec(block, lambda s, h: (s, jnp.minimum(h, head_count - 1)))
    whole = pl.BlockSpec(block, lambda s, h: (s, 0))
    pair = pl.BlockSpec((length, 2 * head_dim), lambda s, h: (s, 0))
    return pl.pallas_call(
        functools.partial(attend_back_kernel, head_dim ** (-0.5), head_count),
        grid=(seq_count, head_count + 3),
        in_specs=[
            own,
            own,
            pair,
            pair,
            whole,
            whole,
            pl.BlockSpec((1, 1, length), lambda s, h: (s, 0, 0)),
            pl.BlockSpec((1, length, 1), lambda s, h: (s, 0, 0)),
        ],
        out_specs=pl.BlockSpec(block, lambda s, h: (s, h)),
        out_shape=jax.ShapeDtypeStruct((rows, (head_count + 3) * head_dim), BF16),
        scratch_shapes=[
            pltpu.VMEM((length, length), F32),
            pltpu.VMEM(block, F32),
            pltpu.VMEM(block, F32),
        ],
        name="attend_back",
        **limits(14 * rows * length * head_dim * head_count, 8 * rows * head_count * head_dim, 2),
    )(queries, grads, shared, kv_next, cosine, sine, doc_ids[:, None, :], doc_ids[:, :, None])


def ffn_kernel(normed, cot, gate_w, up_w, down_w, hidden, grad_gate, grad_up, grad_normed, out):
    whole = lambda ref: lambda: ref[...]
    ffn_tile(
        normed, cot, whole(gate_w), whole(up_w), whole(down_w), hidden, grad_gate, grad_up,
        grad_normed, out,
    )


def ffn_tile(normed, cot, gate_w, up_w, down_w, hidden, grad_gate, grad_up, grad_normed, out):
    gate = dot(normed[...], gate_w(), (1, 0))
    up = dot(normed[...], up_w(), (1, 0))
    sigma = 1.0 / (1.0 + jnp.exp(-gate))
    activated = gate * sigma
    hidden[...] = (activated * up).astype(BF16)
    grad_hidden = dot(cot[...], down_w(), (1, 1), BF16).astype(F32)
    grad_up[...] = (grad_hidden * activated).astype(BF16)
    grad_gate[...] = (grad_hidden * up * (sigma * (1.0 + gate * (1.0 - sigma)))).astype(BF16)
    total = dot(grad_gate[...], gate_w(), (1, 1)) + dot(grad_up[...], up_w(), (1, 1))
    grad_normed[...] = total.astype(BF16)
    out[...] = dot(hidden[...], down_w(), (1, 0), BF16)


def ffn(normed, cot, gate_w, up_w, down_w):
    count, width = normed.shape
    units = gate_w.shape[1]
    tile = math.gcd(count, 256)
    token = pl.BlockSpec((tile, width), lambda t: (t, 0))
    inner = pl.BlockSpec((tile, units), lambda t: (t, 0))
    fixed = lambda shape: pl.BlockSpec(shape, lambda t: (0, 0), pipeline_mode=pl.Buffered(1))
    return pl.pallas_call(
        ffn_kernel,
        grid=(count // tile,),
        in_specs=[token, token, fixed(gate_w.shape), fixed(up_w.shape), fixed(down_w.shape)],
        out_specs=[inner, inner, inner, token, token],
        out_shape=[jax.ShapeDtypeStruct((count, units), BF16)] * 3
        + [jax.ShapeDtypeStruct((count, width), BF16)] * 2,
        name="ffn",
        **limits(12 * count * width * units, 6 * width * units + 8 * count * width),
    )(normed, cot, gate_w, up_w, down_w)


def dp_swap(value, k):
    size = lax.axis_size("dp")
    return lax.ppermute(value, "dp", [(i, i ^ k) for i in range(size)])


def z_swap(value, k):
    size = lax.axis_size("fsdp")
    return lax.ppermute(value, "fsdp", [(i, i ^ (2 * k)) for i in range(size)])


def core_swap(value):
    size = lax.axis_size("fsdp")
    return lax.ppermute(value, "fsdp", [(i, i ^ 1) for i in range(size)])


def pick(array, index, axis=0):
    return lax.dynamic_index_in_dim(array, index, axis, keepdims=False)


def put(buffer, piece, index, axis=0):
    return lax.dynamic_update_index_in_dim(buffer, piece, index, axis)


def plane_gather(value):
    size = lax.axis_size("dp")
    if size != 4:
        return [value] + [dp_swap(value, k) for k in range(1, size)]
    half = value.shape[0] // 2
    one, two = dp_swap(value, 1), dp_swap(value, 2)
    first = dp_swap(one[:half], 2)
    second = dp_swap(two[half:], 1)
    return [value, one, two, jnp.concatenate([first, second], axis=0)]


def plane_scatter(parts):
    size = len(parts)
    if size != 4:
        total = parts[0].astype(F32)
        for k in range(1, size):
            total = total + dp_swap(parts[k], k).astype(F32)
        return total
    half = parts[0].shape[0] // 2
    far_two = dp_swap(parts[3][:half], 1)
    far_one = dp_swap(parts[3][half:], 2)
    for_two = jnp.concatenate(
        [(parts[2][:half].astype(F32) + far_two.astype(F32)).astype(BF16), parts[2][half:]], axis=0
    )
    for_one = jnp.concatenate(
        [parts[1][:half], (parts[1][half:].astype(F32) + far_one.astype(F32)).astype(BF16)], axis=0
    )
    return (
        parts[0].astype(F32)
        + dp_swap(for_one, 1).astype(F32)
        + dp_swap(for_two, 2).astype(F32)
    )


def line_scatter(terms):
    count = terms.shape[0]
    size = lax.axis_size("fsdp")
    z = lax.axis_index("fsdp") // 2
    right = left = None
    for step in range(count - 1):
        out = pick(terms, jnp.clip(count - 1 - step + z, 0, count - 1))
        if right is not None:
            out = (out.astype(F32) + right.astype(F32)).astype(BF16)
        right = lax.ppermute(
            out, "fsdp", [(i, i + 2) for i in range(size - 2) if i // 2 <= step]
        )
        out = pick(terms, jnp.clip(z - (count - 1 - step), 0, count - 1))
        if left is not None:
            out = (out.astype(F32) + left.astype(F32)).astype(BF16)
        left = lax.ppermute(
            out, "fsdp", [(i, i - 2) for i in range(2, size) if count - 1 - i // 2 <= step]
        )
    return pick(terms, z).astype(F32) + right.astype(F32) + left.astype(F32)


def gather_rows(block):
    t_size, f_size = lax.axis_size("dp"), lax.axis_size("fsdp")
    z_size = f_size // 2
    dp, fs = lax.axis_index("dp"), lax.axis_index("fsdp")
    z, core = fs // 2, fs % 2
    rows, cols = block.shape
    line = jnp.zeros((z_size, rows, cols), block.dtype)
    line = put(line, block, z)
    for k in range(1, z_size):
        line = put(line, z_swap(block, k), z ^ k)
    plane = jnp.zeros((t_size, z_size, rows, cols), block.dtype)
    for k, piece in enumerate(plane_gather(line)):
        plane = put(plane, piece, dp ^ k)
    whole = jnp.zeros((t_size, z_size, 2, rows, cols), block.dtype)
    whole = put(whole, plane, core, 2)
    whole = put(whole, core_swap(plane), 1 - core, 2)
    return whole.reshape(t_size * f_size * rows, cols)


def core_sum(mine, other):
    return (mine.astype(F32) + core_swap(other).astype(F32)).astype(BF16)


def scatter_rows(grads):
    t_size, f_size = lax.axis_size("dp"), lax.axis_size("fsdp")
    z_size = f_size // 2
    dp, fs = lax.axis_index("dp"), lax.axis_index("fsdp")
    core = fs % 2
    rows = grads.shape[0] // (t_size * f_size)
    split = grads.reshape(t_size, z_size, 2, rows, grads.shape[1])
    chip = core_sum(pick(split, core, 2), pick(split, 1 - core, 2))
    line = plane_scatter([pick(chip, dp ^ k) for k in range(t_size)])
    return line_scatter(line.astype(BF16))


def scatter_fsdp(split, axis):
    f_size = lax.axis_size("fsdp")
    core = lax.axis_index("fsdp") % 2
    shape = split.shape
    pairs = split.reshape(shape[:axis] + (f_size // 2, 2) + shape[axis + 1 :])
    chip = core_sum(pick(pairs, core, axis + 1), pick(pairs, 1 - core, axis + 1))
    return line_scatter(jnp.moveaxis(chip, axis, 0))


def norm_back(grad_normed, scaled, inv_rms, gain_full):
    grad_scaled = grad_normed * gain_full
    grad_gain = jnp.sum(grad_normed * scaled, axis=0)
    grad_in = inv_rms * (
        grad_scaled - scaled * jnp.mean(grad_scaled * scaled, axis=-1, keepdims=True)
    )
    return (grad_gain, grad_in)


def update(weight, moment, average, grad, rate):
    moment_new = MOMENTUM * moment + grad
    weight_new = weight - rate * (grad + MOMENTUM * moment_new)
    average_new = AVERAGE * average + (1.0 - AVERAGE) * weight_new
    return (moment_new, weight_new, average_new)


LINE_ORDER = (0, 2, 1, 3)
PIECES = ((0, LINE_ORDER), (1, LINE_ORDER), (2, LINE_ORDER), (3, (0, 2)), (3, (1, 3)))
SMEM = pl.BlockSpec(memory_space=pltpu.SMEM)
VMEM = pl.BlockSpec(memory_space=pltpu.VMEM)
ANY = pl.BlockSpec(memory_space=pl.ANY)


def place():
    fs = lax.axis_index("fsdp")
    return jnp.stack([lax.axis_index("dp"), fs // 2, fs % 2]).astype(jnp.int32)


def after(value, *others):
    leaves, tree = jax.tree.flatten(value)
    kept = lax.optimization_barrier((*leaves, *others))[: len(leaves)]
    return jax.tree.unflatten(tree, kept)


SPLIT = 96


def slices_kernel(spot, gate, up, down, *outs):
    outs, packed = outs[:-1], outs[-1]
    units = packed.shape[1]
    for k, out in enumerate(outs):
        at = pl.ds(pl.multiple_of((spot[0] ^ k) * units, units), units)
        out[0] = gate[:, at].astype(BF16)
        out[1] = up[:, at].astype(BF16)
    rows, width = down.shape
    rest = width - units
    packed[:rows] = down[:, :units].astype(BF16)
    packed[rows:] = jnp.zeros((SPLIT, units), BF16)
    packed[rows : rows + SPLIT, :rest] = down[:SPLIT, units:].astype(BF16)
    packed[rows : 2 * rows - SPLIT, rest : 2 * rest] = down[SPLIT:, units:].astype(BF16)


def slices(spot, gate, up, down, count):
    rows, units = gate.shape[0], gate.shape[1] // count
    return pl.pallas_call(
        slices_kernel,
        in_specs=[SMEM, VMEM, VMEM, VMEM],
        out_specs=[VMEM] * (count + 1),
        out_shape=[jax.ShapeDtypeStruct((2, rows, units), BF16)] * count
        + [jax.ShapeDtypeStruct((down.shape[0] + SPLIT, units), BF16)],
        name="slices",
        **limits(0, 12 * gate.size, 0),
    )(spot, gate, up, down)


def gather_line(block):
    two, one = z_swap(block, 2), z_swap(block, 1)
    return jnp.stack([block, two, one, z_swap(two, 1)])


def plane_near(value):
    return dp_swap(value, 1), dp_swap(value, 2)


def plane_far(one, two):
    first, second = cut(one, 0), cut(two, 1)
    return dp_swap(first, 2), dp_swap(second, 1)


def cut_kernel(whole, out):
    out[...] = whole[...]


def cut(whole, index):
    half = whole.shape[0] // 2
    rest = (0,) * (whole.ndim - 1)
    steps = 2 if whole.ndim > 2 else half // 96
    block = (half // steps,) + whole.shape[1:]
    return pl.pallas_call(
        cut_kernel,
        grid=(steps,),
        in_specs=[pl.BlockSpec(block, lambda g: (index * steps + g,) + rest)],
        out_specs=pl.BlockSpec(block, lambda g: (g,) + rest),
        out_shape=jax.ShapeDtypeStruct((half,) + whole.shape[1:], whole.dtype),
        name="cut",
        **limits(0, 2 * whole.size),
    )(whole)


def fetch_rows(spot, pieces, held, sems):
    z, core = spot[1], spot[2]
    copies = [[] for _ in range(4)]
    for side in range(2):
        for (k, line), piece in zip(PIECES, pieces[side * len(PIECES) :]):
            for at, j in enumerate(line):
                slot = held.at[k, z ^ j, core ^ side]
                sem = sems.at[k, 2 * j + side]
                copies[k].append(pltpu.make_async_copy(piece.at[at], slot, sem))
    for some in copies:
        for copy in some:
            copy.start()
    return copies


def blocks_of(spot, copies, held):
    count, z_size, cores, rows, cols = held.shape
    size = z_size * cores * rows
    for k in range(count):
        for copy in copies[k]:
            copy.wait()
        at = pl.ds(pl.multiple_of((spot[0] ^ k) * size, size), size)
        yield k, at, held[k].reshape(size, cols)


def held_shapes(pieces):
    rows, cols = pieces[0].shape[1:]
    return [pltpu.VMEM((4, 4, 2, rows, cols), BF16), pltpu.SemaphoreType.DMA((4, 8))]


def inverse_rms(values):
    return lax.rsqrt(jnp.mean(values * values, axis=-1, keepdims=True) + EPS)


def enter_kernel(spot, tokens, *refs):
    pieces, (raw, normed, gains, held, sems) = refs[:-5], refs[-5:]
    copies = fetch_rows(spot, pieces, held, sems)
    values = tokens[...].astype(F32)
    inv_rms = inverse_rms(values)
    cols = raw.shape[1]
    for k, at, weight in blocks_of(spot, copies, held):
        turned = weight[:, cols:].astype(F32).T
        gains[:, at] = turned[: gains.shape[0]]
        scaled = tokens[:, at].astype(F32) * inv_rms
        normed[:, at] = (scaled * turned[:1]).astype(BF16)
        found = dot(normed[:, at], weight[:, :cols], (1, 0))
        raw[...] = found if k == 0 else raw[...] + found


def enter(spot, tokens, pieces):
    count, width = tokens.shape
    cols = pieces[0].shape[2] - 128
    return pl.pallas_call(
        enter_kernel,
        in_specs=[SMEM, VMEM] + [ANY] * len(pieces),
        out_specs=[VMEM] * 3,
        out_shape=[
            jax.ShapeDtypeStruct((count, cols), F32),
            jax.ShapeDtypeStruct((count, width), BF16),
            jax.ShapeDtypeStruct((8, width), F32),
        ],
        scratch_shapes=held_shapes(pieces),
        name="enter",
        **limits(2 * count * width * cols, 2 * width * cols, 0),
    )(spot, tokens, *pieces)


def leave_kernel(spot, attended, tokens, gains, *refs):
    pieces, (resid, normed, held, sems) = refs[:-4], refs[-4:]
    copies = fetch_rows(spot, pieces, held, sems)
    resid[...] = tokens[...].astype(F32)
    for _, at, weight in blocks_of(spot, copies, held):
        resid[...] += dot(attended[:, at], weight, (1, 0))
    values = resid[...]
    normed[...] = (values * inverse_rms(values) * gains[1:2]).astype(BF16)


def leave(spot, attended, tokens, gains, pieces):
    count, width = tokens.shape
    return pl.pallas_call(
        leave_kernel,
        in_specs=[SMEM] + [VMEM] * 3 + [ANY] * len(pieces),
        out_specs=[VMEM] * 2,
        out_shape=[
            jax.ShapeDtypeStruct((count, width), F32),
            jax.ShapeDtypeStruct((count, width), BF16),
        ],
        scratch_shapes=held_shapes(pieces),
        name="leave",
        **limits(2 * count * width * width, 2 * width * width, 0),
    )(spot, attended, tokens, gains, *pieces)


def leave_back_kernel(spot, grads, *refs):
    pieces, (out, held, sems) = refs[:-3], refs[-3:]
    copies = fetch_rows(spot, pieces, held, sems)
    for _, at, weight in blocks_of(spot, copies, held):
        out[:, at] = dot(grads[...], weight, (1, 1), BF16)


def leave_back(spot, grads, pieces):
    count, width = grads.shape
    return pl.pallas_call(
        leave_back_kernel,
        in_specs=[SMEM, VMEM] + [ANY] * len(pieces),
        out_specs=VMEM,
        out_shape=jax.ShapeDtypeStruct((count, width), BF16),
        scratch_shapes=held_shapes(pieces),
        name="leave_back",
        **limits(2 * count * width * width, 2 * width * width, 0),
    )(spot, grads, *pieces)


def enter_back_kernel(spot, grads, tokens, gains, grad_resid, *refs):
    pieces, (out, grad_gain, held, sems) = refs[:-4], refs[-4:]
    copies = fetch_rows(spot, pieces, held, sems)
    for _, at, weight in blocks_of(spot, copies, held):
        out[:, at] = dot(grads[...], weight, (1, 1))
    values = tokens[...].astype(F32)
    inv_rms = inverse_rms(values)
    total, through = norm_back(out[...], values * inv_rms, inv_rms, gains[:1])
    grad_gain[...] = jnp.broadcast_to(total[None], grad_gain.shape)
    out[...] = grad_resid[...] + through


def enter_back(spot, grads, tokens, gains, grad_resid, pieces):
    count, width = tokens.shape
    return pl.pallas_call(
        enter_back_kernel,
        in_specs=[SMEM] + [VMEM] * 4 + [ANY] * len(pieces),
        out_specs=[VMEM] * 2,
        out_shape=[
            jax.ShapeDtypeStruct((count, width), F32),
            jax.ShapeDtypeStruct((8, width), F32),
        ],
        scratch_shapes=held_shapes(pieces),
        name="enter_back",
        **limits(2 * count * width * width, 2 * width * width, 0),
    )(spot, grads, tokens, gains, grad_resid, *pieces)


TOKEN_ORDER = (1, 3, 2, 0)


def ffn_all_kernel(spot, *refs):
    ins, held_in = (refs[:5], refs[5:10]), refs[10]
    wholes, (hidden, grad_gate, grad_up, sums, out) = refs[11:13], refs[13:18]
    gate_w, up_w, down_w, tiles, grad_tile, out_tile, sems, in_sems, out_sems = refs[18:]
    count, f_size, rows, units = gate_w.shape
    step = pl.program_id(0)
    first = step == 0
    size = tiles.shape[2]
    half = size // 2
    copies = [
        [
            pltpu.make_async_copy(
                held_in.at[:, pl.ds((2 * k + which) * rows, rows)], buffer.at[spot[0] ^ k],
                sems.at[which, k],
            )
            for k in range(count)
        ]
        for which, buffer in enumerate((gate_w, up_w))
    ]
    above, (low, width) = 2 * count * rows, down_w.shape[1:]
    rest = width - units
    copies.append(
        [
            pltpu.make_async_copy(
                held_in.at[:, pl.ds(above, low)], down_w.at[:, :, pl.ds(0, units)], sems.at[2, 0]
            ),
            pltpu.make_async_copy(
                held_in.at[:, pl.ds(above + low, SPLIT), pl.ds(0, rest)],
                down_w.at[:, pl.ds(0, SPLIT), pl.ds(units, rest)],
                sems.at[2, 1],
            ),
            pltpu.make_async_copy(
                held_in.at[:, pl.ds(above + low, low - SPLIT), pl.ds(rest, rest)],
                down_w.at[:, pl.ds(SPLIT, low - SPLIT), pl.ds(units, rest)],
                sems.at[2, 2],
            ),
        ]
    )

    def brought(at):
        k, some = TOKEN_ORDER[at], []
        for which, pieces in enumerate(ins):
            slot = tiles.at[at % 2, which]
            parts = pieces[k : k + 1] if k < 3 else pieces[3:]
            for i, piece in enumerate(parts):
                target = slot.at[pl.ds(i * half, half)] if k == 3 else slot
                some.append(pltpu.make_async_copy(piece, target, in_sems.at[at % 2, which, i]))
        return some

    def kept(at):
        return [
            pltpu.make_async_copy(
                tiles.at[at % 2, which], whole.at[pl.ds(at * size, size)], out_sems.at[at % 2, which]
            )
            for which, whole in enumerate(wholes)
        ]

    for at in range(4):

        @pl.when(step == at)
        def _():
            if at == 0:
                for copy in brought(0):
                    copy.start()
                for held in copies:
                    for copy in held:
                        copy.start()
            for copy in brought(at):
                copy.wait()
            if at > 0:
                for copy in kept(at - 1):
                    copy.wait()
            for copy in kept(at):
                copy.start()
            if at < 3:
                for copy in brought(at + 1):
                    copy.start()

    normed, cot = tiles.at[step % 2, 0], tiles.at[step % 2, 1]

    def weight(which, buffer):
        waited = []

        def read():
            if not waited:
                waited.append(True)

                @pl.when(first)
                def _():
                    for copy in copies[which]:
                        copy.wait()

            return buffer[...].reshape(-1, buffer.shape[-1])

        return read

    ffn_tile(
        normed, cot, weight(0, gate_w), weight(1, up_w), weight(2, down_w),
        hidden, grad_gate, grad_up, grad_tile, out_tile,
    )
    for i in range(2):
        sums[i, 0] = grad_tile[i * half : (i + 1) * half]
        out[i, 0] = out_tile[i * half : (i + 1) * half]

    @pl.when(step == 3)
    def _():
        for copy in kept(3):
            copy.wait()


def ffn_all(spot, normed, cot, held_in, t_size, low):
    count, width = normed[0].shape
    half = count // 2
    f_size, above, units = held_in.shape
    rows = (above - low - SPLIT) // (2 * t_size)
    inner = pl.BlockSpec((count, units), lambda t: (t, 0))
    sums = pl.BlockSpec((2, 1, half, width), lambda t: (0, t, 0, 0))
    weights = pltpu.VMEM((t_size, f_size, rows, units), BF16)
    total = 4 * count
    return pl.pallas_call(
        ffn_all_kernel,
        grid=(4,),
        in_specs=[SMEM] + [ANY] * 11,
        out_specs=[ANY, ANY, inner, inner, inner, sums, sums],
        scratch_shapes=[
            weights,
            weights,
            pltpu.VMEM((f_size, low, width), BF16),
            pltpu.VMEM((2, 2, count, width), BF16),
            pltpu.VMEM((count, width), BF16),
            pltpu.VMEM((count, width), BF16),
            pltpu.SemaphoreType.DMA((3, t_size)),
            pltpu.SemaphoreType.DMA((2, 2, 2)),
            pltpu.SemaphoreType.DMA((2, 2)),
        ],
        out_shape=[jax.ShapeDtypeStruct((total, width), BF16)] * 2
        + [jax.ShapeDtypeStruct((total, units), BF16)] * 3
        + [jax.ShapeDtypeStruct((2, 4, half, width), BF16)] * 2,
        name="ffn_all",
        **limits(12 * total * width * units, 6 * width * units + 8 * total * width),
    )(spot, *normed, *cot, held_in)


class TokenSum:
    def __init__(self, terms):
        self.own = terms
        self.sent = add([[(terms, 0)], [(terms, 5)]], 2)
        self.a, self.b = dp_swap(self.sent[0], 1), dp_swap(self.sent[1], 2)

    def cross(self):
        self.crossed = add([[(self.own, 2), (self.a, 1)], [(self.own, 4), (self.b, 0)]], 1)
        self.last_a, self.last_b = dp_swap(self.crossed[0], 2), dp_swap(self.crossed[1], 1)

    def parts(self):
        return [
            [(flat(self.own), 3), (self.a, 0), (self.last_a, 0)],
            [(flat(self.own), 7), (self.b, 1), (self.last_b, 0)],
        ]


def add_kernel(counts, *refs):
    outs = refs[len(refs) - len(counts) :]
    at = 0
    for count, out in zip(counts, outs):
        total = refs[at][...].astype(F32)
        for ref in refs[at + 1 : at + count]:
            total = total + ref[...].astype(F32)
        out[...] = total.astype(out.dtype)
        at += count


def flat(array):
    return array.reshape((-1,) + array.shape[-2:])


def add(jobs, count, group=1):
    operands = [flat(array) for job in jobs for array, _ in job]
    starts = [start for job in jobs for _, start in job]
    block = (group,) + operands[0].shape[1:]
    spec = lambda start: pl.BlockSpec(block, lambda g: (g + start // group, 0, 0))
    return pl.pallas_call(
        functools.partial(add_kernel, [len(job) for job in jobs]),
        grid=(count // group,),
        in_specs=[spec(start) for start in starts],
        out_specs=[spec(0)] * len(jobs),
        out_shape=[jax.ShapeDtypeStruct((count,) + block[1:], BF16)] * len(jobs),
        name="add",
        **limits(0, 2 * (len(starts) + len(jobs)) * count * block[1] * block[2]),
    )(*operands)


def turns(step):
    return jnp.minimum(step, 2), jnp.maximum(step - 3, 0)


def half_specs(parts, rows):
    specs = []
    for side, terms in enumerate(parts):
        for array, start in terms:
            shape = (1, rows, array.shape[-1])
            specs.append(
                pl.BlockSpec(shape, lambda t, side=side, start=start: (start, turns(t)[side], 0))
            )
    return specs


def half_total(refs, side):
    some = refs[side * 3 : side * 3 + 3]
    return some[0][0].astype(F32) + some[1][0].astype(F32) + some[2][0].astype(F32)


def branch_kernel(resid, cot, gains, *refs):
    terms, (grad_resid, grad_branch, grad_gain) = refs[:6], refs[6:]
    step = pl.program_id(0)

    def finish(grads):
        inv_rms = inverse_rms(resid[...])
        total, through = norm_back(grads, resid[...] * inv_rms, inv_rms, gains[1:2])
        sums = jnp.broadcast_to(total[None], grad_gain.shape)

        @pl.when(step == 0)
        def _():
            grad_gain[...] = sums

        @pl.when(step > 0)
        def _():
            grad_gain[...] += sums

        grads = cot[...].astype(F32) + through
        grad_resid[...] = grads
        grad_branch[...] = grads.astype(BF16)

    for side in range(2):

        @pl.when(step // 3 == side)
        def _():
            finish(half_total(terms, side))


def branch(resid, cot, gains, parts):
    count, width = resid.shape
    rows = count // 6
    token = pl.BlockSpec((rows, width), lambda t: (t, 0))
    fixed = pl.BlockSpec((8, width), lambda t: (0, 0))
    return pl.pallas_call(
        branch_kernel,
        grid=(6,),
        in_specs=[token, token, fixed] + half_specs(parts, rows),
        out_specs=[token, token, fixed],
        out_shape=[
            jax.ShapeDtypeStruct((count, width), F32),
            jax.ShapeDtypeStruct((count, width), BF16),
            jax.ShapeDtypeStruct((8, width), F32),
        ],
        name="branch",
        **limits(0, 18 * count * width),
    )(resid, cot, gains, *[array for terms in parts for array, _ in terms])


def layer_out_kernel(resid, *refs):
    terms, out = refs[:6], refs[6]
    for side in range(2):

        @pl.when(pl.program_id(0) // 3 == side)
        def _():
            out[...] = resid[...] + half_total(terms, side)


def layer_out_of(resid, parts):
    count, width = resid.shape
    rows = count // 6
    token = pl.BlockSpec((rows, width), lambda t: (t, 0))
    return pl.pallas_call(
        layer_out_kernel,
        grid=(6,),
        in_specs=[token] + half_specs(parts, rows),
        out_specs=token,
        out_shape=jax.ShapeDtypeStruct((count, width), F32),
        name="layer_out",
        **limits(0, 14 * count * width),
    )(resid, *[array for terms in parts for array, _ in terms])


def row_grads_kernel(spot, left, right, *refs):
    gains = refs[:-3]
    mine, other, held = refs[-3:]
    count, _, rows, cols = held.shape
    found = dot(left[...], right[...], (0, 0), BF16)
    if gains:
        shape = (128, left.shape[1])
        which = lax.broadcasted_iota(jnp.int32, shape, 0)
        one, two = gains[0][:1], gains[1][:1]
        extra = jnp.where(which == 0, one, jnp.where(which == 1, two, 0.0)).T.astype(BF16)
    for i in range(count):
        for core in range(2):
            at = (2 * i + core) * rows
            held[i, core, :, : found.shape[1]] = found[at : at + rows]
            if gains:
                held[i, core, :, found.shape[1] :] = extra[at : at + rows]
    z, core = spot[1], spot[2]
    for half in range(2):
        for at in range(2):
            mine[half, 0, at] = held[z ^ (2 * at + half), core]
            other[half, 0, at] = held[z ^ (2 * at + half), 1 - core]


def row_grads(spot, left, right, right_cols, gains=()):
    count, width = left.shape
    rows = width // 32
    cols = right_cols + (128 if gains else 0)
    turn = lambda k, spot: spot[0] ^ k ^ (k >> 1)
    out = pl.BlockSpec((2, 1, 2, rows, cols), lambda k, spot: (0, k, 0, 0, 0))
    gain = pl.BlockSpec((8, width // 4), lambda k, spot: (0, turn(k, spot)))
    return pl.pallas_call(
        row_grads_kernel,
        grid_spec=pltpu.PrefetchScalarGridSpec(
            num_scalar_prefetch=1,
            grid=(4,),
            in_specs=[
                pl.BlockSpec((count, width // 4), lambda k, spot: (0, turn(k, spot))),
                pl.BlockSpec((count, right_cols), lambda k, spot: (0, 0)),
            ]
            + [gain] * len(gains),
            out_specs=[out, out],
            scratch_shapes=[pltpu.VMEM((4, 2, rows, cols), BF16)],
        ),
        out_shape=[jax.ShapeDtypeStruct((2, 4, 2, rows, cols), BF16)] * 2,
        name="row_grads",
        **limits(2 * count * width * cols, 2 * width * cols + 2 * count * (width + cols)),
    )(spot, left, right, *gains)


class RowSum:
    def __init__(self, mine, other):
        self.mine, self.other = mine, core_swap(other)

    def plane(self):
        pair = lambda start: [(self.mine, start), (self.other, start)]
        a, b = self.sent = add([pair(2), pair(12)], 4, 2)
        self.a, self.b = dp_swap(a, 1), dp_swap(b, 2)

    def cross(self):
        a, b = self.crossed = add(
            [
                [(self.mine, 6), (self.other, 6), (self.a, 2)],
                [(self.mine, 10), (self.other, 10), (self.b, 0)],
            ],
            2,
        )
        self.last_a, self.last_b = dp_swap(a, 2), dp_swap(b, 1)

    def near(self):
        terms = [(self.mine, 8), (self.other, 8), (self.b, 2), (self.last_b, 0)]
        self.odd = add([terms], 2)[0]
        self.line = z_swap(self.odd, 1)

    def terms(self, at):
        return [(x, at) for x in (self.mine, self.other, self.a, self.last_a, self.line)]

    def far(self):
        self.rest = add([self.terms(1)], 1)[0]
        self.last = z_swap(self.rest, 2)

    def final(self):
        return self.terms(0) + [(self.last, 0)]


class LineSum:
    def __init__(self, mine, other):
        self.mine, self.other = mine, core_swap(other)

    def line(self):
        blocks = self.mine.shape[0]
        count = flat(self.mine).shape[0]
        self.chip = add([[(self.mine, 0), (self.other, 0)]], count, count // blocks)[0]
        size = lax.axis_size("fsdp")
        groups = [list(range(core, size, 2)) for core in range(2)]
        self.total = lax.psum_scatter(
            self.chip, "fsdp", scatter_dimension=0, axis_index_groups=groups, tiled=True
        )


def chunk_dot(lefts, rights):
    found = dot(lefts[0][...], rights[0][...], (0, 0))
    for left, right in zip(lefts[1:], rights[1:]):
        found = found + dot(left[...], right[...], (0, 0))
    return found.astype(BF16)


def place_line(spot, found, held, mine, other):
    count, _, rows, _ = held.shape
    core = spot[2]
    for i in range(count):
        for side in range(2):
            at = (2 * i + side) * rows
            held[i, side] = found[at : at + rows]
    for at in range(count):
        mine[at] = held[at, core].reshape(mine.shape[1:])
        other[at] = held[at, 1 - core].reshape(other.shape[1:])


def line_grads_kernel(spot, *refs):
    mine, other, held = refs[-3:]
    chunks = (len(refs) - 3) // 2
    found = chunk_dot(refs[:chunks], refs[chunks : 2 * chunks])
    place_line(spot, found, held, mine, other)


def unit_grads(spot, lefts, rights):
    count, width = lefts[0].shape
    units, rows = rights[0].shape[1], width // 32
    out = pl.BlockSpec((4, 1, rows, units), lambda k, spot: (0, k, 0, 0))
    left = pl.BlockSpec((count, width // 4), lambda k, spot: (0, spot[0] ^ k))
    right = pl.BlockSpec((count, units), lambda k, spot: (0, 0), pipeline_mode=pl.Buffered(1))
    total = count * len(lefts)
    return pl.pallas_call(
        line_grads_kernel,
        grid_spec=pltpu.PrefetchScalarGridSpec(
            num_scalar_prefetch=1,
            grid=(4,),
            in_specs=[left] * len(lefts) + [right] * len(rights),
            out_specs=[out, out],
            scratch_shapes=[pltpu.VMEM((4, 2, rows, units), BF16)],
        ),
        out_shape=[jax.ShapeDtypeStruct((4, 4, rows, units), BF16)] * 2,
        name="unit_grads",
        **limits(2 * total * width * units, 2 * width * units + 2 * total * (width + units)),
    )(spot, *lefts, *rights)


def down_grads(spot, lefts, rights):
    count, units = lefts[0].shape
    width = rights[0].shape[1]
    rows, tile = units // 8, width // 4
    out = pl.BlockSpec((4, rows, tile), lambda n, spot: (0, 0, n))
    left = pl.BlockSpec((count, units), lambda n, spot: (0, 0), pipeline_mode=pl.Buffered(1))
    right = pl.BlockSpec((count, tile), lambda n, spot: (0, n))
    total = count * len(lefts)
    return pl.pallas_call(
        line_grads_kernel,
        grid_spec=pltpu.PrefetchScalarGridSpec(
            num_scalar_prefetch=1,
            grid=(4,),
            in_specs=[left] * len(lefts) + [right] * len(rights),
            out_specs=[out, out],
            scratch_shapes=[pltpu.VMEM((4, 2, rows, tile), BF16)],
        ),
        out_shape=[jax.ShapeDtypeStruct((4, rows, width), BF16)] * 2,
        name="down_grads",
        **limits(2 * total * width * units, 2 * width * units + 2 * total * (width + units)),
    )(spot, *lefts, *rights)


def sum_of(refs):
    total = refs[0][0].astype(F32)
    for ref in refs[1:]:
        total = total + ref[0].astype(F32)
    return total


def update_rows_kernel(rates, count, *refs):
    terms, rest = refs[:count], refs[count:]
    held = 3 * len(rates)
    ins, outs = rest[:held], rest[held:]
    grads = sum_of(terms)
    at = 0
    for i, rate in enumerate(rates):
        own = ins[3 * i : 3 * i + 3]
        cols = own[0].shape[1]
        piece = grads[:, at : at + cols]
        at += cols
        results = update(*[ref[...] for ref in own], piece, rate)
        for out, result in zip(outs[3 * i :], results):
            out[...] = result
    if at < grads.shape[1]:
        outs[-1][...] = grads[:, at:]


def update_rows(terms, weights, rates):
    operands = [flat(array) for array, _ in terms]
    block = (1,) + operands[0].shape[1:]
    left = block[2] - sum(w[0].shape[1] for w in weights)
    arrays = [array for some in weights for array in some]
    shapes = [jax.ShapeDtypeStruct(array.shape, F32) for array in arrays]
    if left:
        shapes.append(jax.ShapeDtypeStruct((block[1], left), F32))
    whole = lambda shape: pl.BlockSpec(shape, lambda g: (0, 0))
    return pl.pallas_call(
        functools.partial(update_rows_kernel, rates, len(terms)),
        grid=(1,),
        in_specs=[pl.BlockSpec(block, lambda g, start=start: (start, 0, 0)) for _, start in terms]
        + [whole(array.shape) for array in arrays],
        out_specs=[whole(shape.shape) for shape in shapes],
        out_shape=shapes,
        name="update_rows",
        **limits(0, 32 * arrays[0].size),
    )(*operands, *arrays)


def update_units_kernel(rate, spot, weight, moment, average, *refs):
    pieces, outs = refs[:4], refs[4:]
    units = pieces[0].shape[-1]
    for k in range(4):
        grads = pieces[k][0].astype(F32)
        at = pl.ds(pl.multiple_of((spot[0] ^ k) * units, units), units)
        results = update(weight[:, at], moment[:, at], average[:, at], grads, rate)
        for out, result in zip(outs, results):
            out[:, at] = result


def update_units(spot, weight, moment, average, pieces, rate):
    block = (1,) + pieces[0].shape[1:]
    first = pl.BlockSpec(block, lambda g: (0, 0, 0))
    whole = pl.BlockSpec(weight.shape, lambda g: (0, 0))
    return pl.pallas_call(
        functools.partial(update_units_kernel, rate),
        grid=(1,),
        in_specs=[SMEM] + [whole] * 3 + [first] * 4,
        out_specs=[whole] * 3,
        out_shape=[jax.ShapeDtypeStruct(weight.shape, F32)] * 3,
        name="update_units",
        **limits(0, 32 * weight.size),
    )(spot, weight, moment, average, *pieces)


def shards_any(
    tokens_in,
    out_grad,
    kv_grad_next,
    doc_ids,
    gains,
    gains_mom,
    gains_ema,
    w_query,
    query_mom,
    query_ema,
    w_keyval,
    keyval_mom,
    keyval_ema,
    w_output,
    output_mom,
    output_ema,
    w_gate,
    gate_mom,
    gate_ema,
    w_up,
    up_mom,
    up_ema,
    w_down,
    down_mom,
    down_ema,
):
    t_size, f_size = lax.axis_size("dp"), lax.axis_size("fsdp")
    dp = lax.axis_index("dp")
    seq_count, length = doc_ids.shape
    width = tokens_in.shape[1]
    head_dim = w_keyval.shape[1] // 2
    head_count = w_query.shape[1] // head_dim
    hidden_units = w_gate.shape[1]
    rows = seq_count * length
    heads_width = head_count * head_dim
    tokens_total = rows * t_size * f_size
    own_rows = w_query.shape[0]
    slice_units = hidden_units // t_size

    gain_cols = jnp.zeros((own_rows, 128), BF16).at[:, :2].set(gains.astype(BF16).T)
    qkv_block = jnp.concatenate([w_query.astype(BF16), w_keyval.astype(BF16), gain_cols], axis=1)

    def to_slices(weight):
        split = weight.astype(BF16).reshape(own_rows, t_size, slice_units)
        held = jnp.zeros((t_size, own_rows, slice_units), BF16)
        held = put(held, pick(split, dp, 1), dp)
        for k in range(1, t_size):
            held = put(held, dp_swap(pick(split, dp ^ k, 1), k), dp ^ k)
        whole = lax.all_gather(held, "fsdp", axis=0)
        return jnp.swapaxes(whole, 0, 1).reshape(width, slice_units)

    qkv_full = gather_rows(qkv_block)
    output_full = gather_rows(w_output.astype(BF16))
    gate_slice = to_slices(w_gate)
    up_slice = to_slices(w_up)
    gain_rows = qkv_full[:, -128:]
    down_block = w_down.astype(BF16)
    down_slice = lax.all_gather(down_block, "fsdp", axis=0, tiled=True)
    cot_all = jnp.concatenate(plane_gather(out_grad), axis=0)

    inputs = tokens_in.astype(F32)
    inv_rms = lax.rsqrt(jnp.mean(inputs * inputs, axis=-1, keepdims=True) + EPS)
    scaled = inputs * inv_rms
    gains_full = gain_rows[:, :2].astype(F32).T
    gain_attn, gain_ffn = gains_full[0], gains_full[1]
    normed = (scaled * gain_attn).astype(BF16)
    raw = dot(normed, qkv_full, (1, 0))
    cosine, sine = rotation(positions_of(doc_ids).reshape(rows), head_dim)
    queries, attended, shared = attend(raw, cosine, sine, doc_ids, head_count, head_dim)
    resid = inputs + dot(attended, output_full, (1, 0))

    inv_rms2 = lax.rsqrt(jnp.mean(resid * resid, axis=-1, keepdims=True) + EPS)
    scaled2 = resid * inv_rms2
    normed2 = (scaled2 * gain_ffn).astype(BF16)
    normed2_all = jnp.concatenate(plane_gather(normed2), axis=0)
    results = ffn(normed2_all, cot_all, gate_slice, up_slice, down_slice)
    hidden, grad_gate, grad_up, grad_normed2_part, ffn_part = results
    grad_normed2 = plane_scatter(
        [grad_normed2_part[k * rows : (k + 1) * rows] for k in range(t_size)]
    )
    ffn_out = plane_scatter([ffn_part[k * rows : (k + 1) * rows] for k in range(t_size)])
    layer_out = resid + ffn_out
    def from_slices(grads):
        own = scatter_fsdp(grads.reshape(t_size, f_size, own_rows, slice_units), 1)
        own = own.reshape(t_size, own_rows, slice_units)
        held = jnp.zeros((own_rows, t_size, slice_units), F32)
        held = put(held, pick(own, dp), dp, 1)
        for k in range(1, t_size):
            sent = dp_swap(pick(own, dp ^ k).astype(BF16), k)
            held = put(held, sent.astype(F32), dp ^ k, 1)
        return held.reshape(own_rows, hidden_units)

    grad_down_w = dot(hidden, cot_all, (0, 0), BF16)
    down_sum = scatter_fsdp(grad_down_w.reshape(f_size, -1, width), 0)
    gate_sum = from_slices(dot(normed2_all, grad_gate, (0, 0), BF16))
    up_sum = from_slices(dot(normed2_all, grad_up, (0, 0), BF16))

    grad_gain_ffn, grad_through = norm_back(grad_normed2, scaled2, inv_rms2, gain_ffn)
    grad_resid = out_grad.astype(F32) + grad_through
    grad_branch = grad_resid.astype(BF16)
    grad_attended = dot(grad_branch, output_full, (1, 1), BF16)
    output_sum = scatter_rows(dot(attended, grad_branch, (0, 0), BF16))
    grad_raw = attend_back(
        queries, grad_attended, shared, kv_grad_next, cosine, sine, doc_ids, head_count, head_dim
    )
    grad_normed = dot(grad_raw, qkv_full, (1, 1))
    grad_gain_attn, grad_first = norm_back(grad_normed, scaled, inv_rms, gain_attn)
    input_grad = grad_resid + grad_first
    gain_grads = jnp.zeros((width, 128), BF16)
    gain_grads = gain_grads.at[:, :2].set(
        jnp.stack([grad_gain_attn, grad_gain_ffn], axis=0).astype(BF16).T
    )
    qkv_sum = scatter_rows(dot(normed, grad_raw, (0, 0), BF16).at[:, -128:].set(gain_grads))
    query_sum = qkv_sum[:, :heads_width]
    keyval_sum = qkv_sum[:, heads_width : heads_width + 2 * head_dim]
    gains_sum = qkv_sum[:, -128:-126].T

    def rate(strength, fan):
        return strength / math.sqrt(fan * tokens_total)

    gains_out = update(gains, gains_mom, gains_ema, gains_sum, rate(0.1, 1))
    query_out = update(w_query, query_mom, query_ema, query_sum, rate(0.6, width))
    keyval_out = update(w_keyval, keyval_mom, keyval_ema, keyval_sum, rate(0.15, width))
    output_out = update(w_output, output_mom, output_ema, output_sum, rate(5.0, heads_width))
    gate_out = update(w_gate, gate_mom, gate_ema, gate_sum, rate(0.6, width))
    up_out = update(w_up, up_mom, up_ema, up_sum, rate(0.6, width))
    down_out = update(w_down, down_mom, down_ema, down_sum, rate(1.5, hidden_units))
    return (
        layer_out,
        shared.astype(F32),
        input_grad,
        *gains_out,
        *query_out,
        *keyval_out,
        *output_out,
        *gate_out,
        *up_out,
        *down_out,
    )


def shards_fast(
    tokens_in,
    out_grad,
    kv_grad_next,
    doc_ids,
    gains,
    gains_mom,
    gains_ema,
    w_query,
    query_mom,
    query_ema,
    w_keyval,
    keyval_mom,
    keyval_ema,
    w_output,
    output_mom,
    output_ema,
    w_gate,
    gate_mom,
    gate_ema,
    w_up,
    up_mom,
    up_ema,
    w_down,
    down_mom,
    down_ema,
):
    t_size, f_size = lax.axis_size("dp"), lax.axis_size("fsdp")
    seq_count, length = doc_ids.shape
    width = tokens_in.shape[1]
    head_dim = w_keyval.shape[1] // 2
    head_count = w_query.shape[1] // head_dim
    hidden_units = w_gate.shape[1]
    rows = seq_count * length
    half = rows // 2
    heads_width = head_count * head_dim
    raw_width = heads_width + 2 * head_dim
    tokens_total = rows * t_size * f_size
    own_rows = w_query.shape[0]
    spot = place()

    gain_cols = jnp.zeros((own_rows, 128), BF16).at[:, :2].set(gains.astype(BF16).T)
    qkv_block = jnp.concatenate([w_query.astype(BF16), w_keyval.astype(BF16), gain_cols], axis=1)
    qkv_line = gather_line(qkv_block)

    *sent, packed = slices(spot, w_gate, w_up, w_down, t_size)
    got = [sent[0]] + [dp_swap(sent[k], k) for k in range(1, t_size)]
    packed = jnp.concatenate([flat(piece).reshape(-1, piece.shape[-1]) for piece in got] + [packed])
    output_block = after(w_output.astype(BF16), qkv_line)
    output_two, output_one = z_swap(output_block, 2), z_swap(output_block, 1)
    output_last = z_swap(output_two, 1)
    output_line = [output_block, output_two, output_one, output_last]
    units_all = lax.all_gather(
        after(packed, output_line[1], output_line[3]), "fsdp", axis=0
    )
    output_line = jnp.stack(output_line)

    qkv_near = plane_near(after(qkv_line, packed))
    qkv_far = plane_far(*after(qkv_near, output_last))
    qkv_mine = [qkv_line, *qkv_near, *qkv_far]
    qkv_pieces = qkv_mine + [core_swap(piece) for piece in qkv_mine]
    output_near = plane_near(after(output_line, *qkv_far))
    cot_near = plane_near(after(out_grad, *qkv_pieces[8:]))

    raw, normed, gains_full = enter(spot, after(tokens_in, output_line), qkv_pieces)
    cosine, sine = rotation(positions_of(doc_ids).reshape(rows), head_dim)
    queries, attended, shared = attend(raw, cosine, sine, doc_ids, head_count, head_dim)
    output_mine = [output_line, *output_near, *plane_far(*after(output_near, attended))]
    output_pieces = output_mine + [core_swap(piece) for piece in output_mine]
    cot_first, cot_second = cut(cot_near[0], 0), cut(cot_near[1], 1)
    cot = [out_grad, *cot_near, dp_swap(cot_first, 2), dp_swap(cot_second, 1)]
    resid, normed2 = leave(spot, after(attended, cot_first, cot_second), tokens_in, gains_full, output_pieces)

    normed2_near = plane_near(after(normed2, *cot[3:]))
    normed2_all = [normed2, *normed2_near, *plane_far(*normed2_near)]
    tokens2, cots, hidden, grad_gate, grad_up, grad_terms, out_terms = ffn_all(
        spot, normed2_all, cot, units_all, t_size, w_down.shape[0]
    )
    normed2_sum = TokenSum(grad_terms)
    down = LineSum(*down_grads(spot, [after(hidden, *normed2_sum.sent)], [cots]))
    gate = LineSum(*unit_grads(spot, [after(tokens2, down.mine)], [grad_gate]))
    down.other = after(down.other, gate.mine)
    down.line()
    normed2_sum.a, normed2_sum.b = after((normed2_sum.a, normed2_sum.b), down.chip)
    normed2_sum.cross()
    up = LineSum(*unit_grads(spot, [after(tokens2, *normed2_sum.crossed)], [grad_up]))
    grad_resid, grad_branch, grad_gain_ffn = branch(
        after(resid, up.mine), out_grad, gains_full, normed2_sum.parts()
    )
    out_sum = TokenSum(after(out_terms, grad_branch))

    output = RowSum(*row_grads(spot, attended, after(grad_branch, *out_sum.sent), width))
    grad_attended = leave_back(spot, after(grad_branch, output.mine), output_pieces)
    gate.other, output.other = after((gate.other, output.other), grad_attended)
    output.plane()
    gate.line()
    grad_raw = attend_back(
        queries, after(grad_attended, gate.chip, *output.sent), shared, kv_grad_next, cosine, sine,
        doc_ids, head_count, head_dim,
    )
    input_grad, grad_gain_attn = enter_back(
        spot, grad_raw, tokens_in, gains_full, grad_resid, qkv_pieces
    )
    out_sum.a, out_sum.b, output.a, output.b = after(
        (out_sum.a, out_sum.b, output.a, output.b), input_grad
    )
    output.cross()
    qkv = RowSum(
        *row_grads(
            spot, after(normed, *output.crossed, down.total), grad_raw, raw_width,
            (grad_gain_attn, grad_gain_ffn),
        )
    )
    output.last_a, output.last_b = after((output.last_a, output.last_b), qkv.mine)
    output.near()
    up.other = after(up.other, output.odd)
    up.line()
    gate.total = after(gate.total, up.chip)
    qkv.other = after(qkv.other, gate.total)
    qkv.plane()

    def rate(strength, fan):
        return strength / math.sqrt(fan * tokens_total)

    def exchange(total):
        pieces = [total[k : k + 1] for k in range(t_size)]
        return pieces[:1] + [dp_swap(pieces[k], k) for k in range(1, t_size)]

    down_out = update_rows(
        [(after(down.total, *qkv.sent), 0)], [(w_down, down_mom, down_ema)],
        [rate(1.5, hidden_units)],
    )
    out_sum.a, out_sum.b = after((out_sum.a, out_sum.b), *qkv.sent)
    out_sum.cross()
    qkv.a, qkv.b = after((qkv.a, qkv.b), down_out[0], *out_sum.crossed)
    qkv.cross()
    gate_pieces = exchange(flat(after(gate.total, *qkv.crossed)))
    output.line = after(output.line, *qkv.crossed)
    output.far()
    qkv.last_a, qkv.last_b = after((qkv.last_a, qkv.last_b), output.rest)
    qkv.near()
    out_sum.last_a, out_sum.last_b, gate_pieces = after(
        (out_sum.last_a, out_sum.last_b, gate_pieces), qkv.odd
    )
    layer_out = layer_out_of(resid, out_sum.parts())
    gate_out = update_units(
        spot, w_gate, gate_mom, gate_ema, gate_pieces, rate(0.6, width)
    )
    up_pieces = exchange(flat(after(up.total, qkv.odd)))
    qkv.line = after(qkv.line, layer_out, gate_out[0])
    qkv.far()
    output_out = update_rows(
        [(after(x, qkv.rest), at) for x, at in output.final()],
        [(w_output, output_mom, output_ema)], [rate(5.0, heads_width)],
    )
    up_out = update_units(
        spot, w_up, up_mom, up_ema, after(up_pieces, qkv.rest), rate(0.6, width)
    )
    qkv.last = after(qkv.last, up_out[0], output_out[0])
    *qkv_out, left_over = update_rows(
        qkv.final(),
        [(w_query, query_mom, query_ema), (w_keyval, keyval_mom, keyval_ema)],
        [rate(0.6, width), rate(0.15, width)],
    )
    gains_out = update(gains, gains_mom, gains_ema, left_over[:, :2].T, rate(0.1, 1))
    return (
        layer_out,
        shared.astype(F32),
        input_grad,
        *gains_out,
        *qkv_out,
        *output_out,
        *gate_out,
        *up_out,
        *down_out,
    )


def solution(mesh):
    rows = P(BOTH, None)
    shards = shards_fast if dict(mesh.shape) == {"dp": 4, "fsdp": 8} else shards_any
    cols = P(None, BOTH)
    return jax.shard_map(
        shards,
        mesh=mesh,
        in_specs=(rows,) * 4 + (cols,) * 3 + (rows,) * 18,
        out_specs=(rows,) * 3 + (cols,) * 3 + (rows,) * 18,
        check_vma=False,
    )
```

```python
import functools
import math

import jax
import jax.numpy as jnp
from jax import lax
from jax.experimental import pallas as pl
from jax.experimental.pallas import tpu as pltpu
from jax.sharding import PartitionSpec as P

EPS = 1e-05
THETA = 10000.0
MOMENTUM = 0.9
AVERAGE = 0.75
NEG = -1e30
F32 = jnp.float32
BF16 = jnp.bfloat16
BOTH = ("dp", "fsdp")
COST = 40.0
VMEM_BYTES = 60 * 1024 * 1024


def positions_of(doc_ids):
    length = doc_ids.shape[-1]
    offsets = jnp.arange(length, dtype=jnp.int32)
    same = doc_ids[..., :, None] == doc_ids[..., None, :]
    starts = jnp.min(jnp.where(same, offsets, length), axis=-1)
    return offsets - starts


def rotation(positions, head_dim):
    half_dim = head_dim // 2
    inverse = THETA ** (-(jnp.arange(half_dim, dtype=F32) * 2.0) / head_dim)
    angles = positions.astype(F32)[..., None] * inverse
    cosine, sine = jnp.cos(angles), jnp.sin(angles)
    return (
        jnp.concatenate([cosine, cosine], axis=-1),
        jnp.concatenate([-sine, sine], axis=-1),
    )


def dot(left, right, contract, kind=F32):
    return lax.dot_general(
        left, right, ((contract[:1], contract[1:]), ((), ())), preferred_element_type=F32
    ).astype(kind)


def limits(flops=0, moved=0, steps=1):
    semantics = ("arbitrary",) * steps if steps else None
    return {
        "compiler_params": pltpu.CompilerParams(
            vmem_limit_bytes=VMEM_BYTES, dimension_semantics=semantics
        ),
        "cost_estimate": pl.CostEstimate(
            flops=int(flops * COST), bytes_accessed=int(moved * COST), transcendentals=0
        ),
    }


def swap_halves(values):
    return pltpu.roll(values, values.shape[-1] // 2, values.ndim - 1)


def set_bias(bias, ids_row, ids_col):
    shape = bias.shape
    later = lax.broadcasted_iota(jnp.int32, shape, 1) > lax.broadcasted_iota(jnp.int32, shape, 0)
    apart = (ids_col[0] != ids_row[0]) | later
    bias[...] = jnp.where(apart, NEG, 0.0)


def probabilities(query, keys, bias):
    scores = dot(query, keys, (1, 1)) + bias[...]
    weights = jnp.exp(scores - jnp.max(scores, axis=-1, keepdims=True))
    return weights / jnp.sum(weights, axis=-1, keepdims=True)


def attend_kernel(
    scale, q_raw, k_raw, v_raw, cosine, sine, ids_row, ids_col, queries, attended, shared, bias
):
    head_dim = q_raw.shape[1]

    @pl.when(pl.program_id(1) == 0)
    def _():
        set_bias(bias, ids_row, ids_col)
        key = k_raw[...]
        turned = key * cosine[...] + swap_halves(key) * sine[...]
        shared[:, :head_dim] = turned.astype(BF16)
        shared[:, head_dim:] = v_raw[...].astype(BF16)

    raw = q_raw[...]
    query = ((raw * cosine[...] + swap_halves(raw) * sine[...]) * scale).astype(BF16)
    queries[...] = query
    probs = probabilities(query, shared[:, :head_dim], bias).astype(BF16)
    attended[...] = dot(probs, shared[:, head_dim:], (1, 0), BF16)


def attend(raw, cosine, sine, doc_ids, head_count, head_dim):
    seq_count, length = doc_ids.shape
    rows = seq_count * length
    column = lambda which: pl.BlockSpec((length, head_dim), which)
    whole = pl.BlockSpec((length, head_dim), lambda s, h: (s, 0))
    return pl.pallas_call(
        functools.partial(attend_kernel, head_dim ** (-0.5)),
        grid=(seq_count, head_count),
        in_specs=[
            column(lambda s, h: (s, h)),
            column(lambda s, h: (s, head_count)),
            column(lambda s, h: (s, head_count + 1)),
            whole,
            whole,
            pl.BlockSpec((1, 1, length), lambda s, h: (s, 0, 0)),
            pl.BlockSpec((1, length, 1), lambda s, h: (s, 0, 0)),
        ],
        out_specs=[
            column(lambda s, h: (s, h)),
            column(lambda s, h: (s, h)),
            pl.BlockSpec((length, 2 * head_dim), lambda s, h: (s, 0)),
        ],
        out_shape=[
            jax.ShapeDtypeStruct((rows, head_count * head_dim), BF16),
            jax.ShapeDtypeStruct((rows, head_count * head_dim), BF16),
            jax.ShapeDtypeStruct((rows, 2 * head_dim), BF16),
        ],
        scratch_shapes=[pltpu.VMEM((length, length), F32)],
        name="attend",
        **limits(6 * rows * length * head_dim * head_count, 10 * rows * head_count * head_dim, 2),
    )(raw, raw, raw, cosine, sine, doc_ids[:, None, :], doc_ids[:, :, None])


def attend_back_kernel(
    scale, head_count, query_ref, grad_ref, shared, kv_next, cosine, sine, ids_row, ids_col,
    out, bias, grad_keys, grad_values,
):
    head_dim = query_ref.shape[1]
    head = pl.program_id(1)

    def turn_back(grads):
        return grads * cosine[...] - swap_halves(grads) * sine[...]

    @pl.when(head == 0)
    def _():
        set_bias(bias, ids_row, ids_col)
        grad_keys[...] = jnp.zeros_like(grad_keys)
        grad_values[...] = jnp.zeros_like(grad_values)

    @pl.when(head < head_count)
    def _():
        query, grad = query_ref[...], grad_ref[...]
        keys, values = shared[:, :head_dim], shared[:, head_dim:]
        probs = probabilities(query, keys, bias)
        grad_probs = dot(grad, values, (1, 1))
        inner = jnp.sum(probs * grad_probs, axis=-1, keepdims=True)
        grad_scores = (probs * (grad_probs - inner)).astype(BF16)
        grad_query = dot(grad_scores, keys, (1, 0), BF16).astype(F32) * scale
        out[...] = turn_back(grad_query).astype(BF16)
        grad_keys[...] += dot(grad_scores, query, (0, 0))
        grad_values[...] += dot(probs.astype(BF16), grad, (0, 0))

    @pl.when(head == head_count)
    def _():
        grads = (grad_keys[...] + kv_next[:, :head_dim].astype(F32)).astype(BF16).astype(F32)
        out[...] = turn_back(grads).astype(BF16)

    @pl.when(head == head_count + 1)
    def _():
        out[...] = (grad_values[...] + kv_next[:, head_dim:].astype(F32)).astype(BF16)

    @pl.when(head == head_count + 2)
    def _():
        out[...] = jnp.zeros_like(out)


def attend_back(queries, grads, shared, kv_next, cosine, sine, doc_ids, head_count, head_dim):
    seq_count, length = doc_ids.shape
    rows = seq_count * length
    block = (length, head_dim)
    own = pl.BlockSpec(block, lambda s, h: (s, jnp.minimum(h, head_count - 1)))
    whole = pl.BlockSpec(block, lambda s, h: (s, 0))
    pair = pl.BlockSpec((length, 2 * head_dim), lambda s, h: (s, 0))
    return pl.pallas_call(
        functools.partial(attend_back_kernel, head_dim ** (-0.5), head_count),
        grid=(seq_count, head_count + 3),
        in_specs=[
            own,
            own,
            pair,
            pair,
            whole,
            whole,
            pl.BlockSpec((1, 1, length), lambda s, h: (s, 0, 0)),
            pl.BlockSpec((1, length, 1), lambda s, h: (s, 0, 0)),
        ],
        out_specs=pl.BlockSpec(block, lambda s, h: (s, h)),
        out_shape=jax.ShapeDtypeStruct((rows, (head_count + 3) * head_dim), BF16),
        scratch_shapes=[
            pltpu.VMEM((length, length), F32),
            pltpu.VMEM(block, F32),
            pltpu.VMEM(block, F32),
        ],
        name="attend_back",
        **limits(14 * rows * length * head_dim * head_count, 8 * rows * head_count * head_dim, 2),
    )(queries, grads, shared, kv_next, cosine, sine, doc_ids[:, None, :], doc_ids[:, :, None])


def ffn_kernel(normed, cot, gate_w, up_w, down_w, hidden, grad_gate, grad_up, grad_normed, out):
    whole = lambda ref: lambda: ref[...]
    ffn_tile(
        normed, cot, whole(gate_w), whole(up_w), whole(down_w), hidden, grad_gate, grad_up,
        grad_normed, out,
    )


def ffn_tile(normed, cot, gate_w, up_w, down_w, hidden, grad_gate, grad_up, grad_normed, out):
    gate = dot(normed[...], gate_w(), (1, 0))
    up = dot(normed[...], up_w(), (1, 0))
    sigma = 1.0 / (1.0 + jnp.exp(-gate))
    activated = gate * sigma
    hidden[...] = (activated * up).astype(BF16)
    grad_hidden = dot(cot[...], down_w(), (1, 1), BF16).astype(F32)
    grad_up[...] = (grad_hidden * activated).astype(BF16)
    grad_gate[...] = (grad_hidden * up * (sigma * (1.0 + gate * (1.0 - sigma)))).astype(BF16)
    total = dot(grad_gate[...], gate_w(), (1, 1)) + dot(grad_up[...], up_w(), (1, 1))
    grad_normed[...] = total.astype(BF16)
    out[...] = dot(hidden[...], down_w(), (1, 0), BF16)


def ffn(normed, cot, gate_w, up_w, down_w):
    count, width = normed.shape
    units = gate_w.shape[1]
    tile = math.gcd(count, 256)
    token = pl.BlockSpec((tile, width), lambda t: (t, 0))
    inner = pl.BlockSpec((tile, units), lambda t: (t, 0))
    fixed = lambda shape: pl.BlockSpec(shape, lambda t: (0, 0), pipeline_mode=pl.Buffered(1))
    return pl.pallas_call(
        ffn_kernel,
        grid=(count // tile,),
        in_specs=[token, token, fixed(gate_w.shape), fixed(up_w.shape), fixed(down_w.shape)],
        out_specs=[inner, inner, inner, token, token],
        out_shape=[jax.ShapeDtypeStruct((count, units), BF16)] * 3
        + [jax.ShapeDtypeStruct((count, width), BF16)] * 2,
        name="ffn",
        **limits(12 * count * width * units, 6 * width * units + 8 * count * width),
    )(normed, cot, gate_w, up_w, down_w)


def dp_swap(value, k):
    size = lax.axis_size("dp")
    return lax.ppermute(value, "dp", [(i, i ^ k) for i in range(size)])


def z_swap(value, k):
    size = lax.axis_size("fsdp")
    return lax.ppermute(value, "fsdp", [(i, i ^ (2 * k)) for i in range(size)])


def core_swap(value):
    size = lax.axis_size("fsdp")
    return lax.ppermute(value, "fsdp", [(i, i ^ 1) for i in range(size)])


def pick(array, index, axis=0):
    return lax.dynamic_index_in_dim(array, index, axis, keepdims=False)


def put(buffer, piece, index, axis=0):
    return lax.dynamic_update_index_in_dim(buffer, piece, index, axis)


def plane_gather(value):
    size = lax.axis_size("dp")
    if size != 4:
        return [value] + [dp_swap(value, k) for k in range(1, size)]
    half = value.shape[0] // 2
    one, two = dp_swap(value, 1), dp_swap(value, 2)
    first = dp_swap(one[:half], 2)
    second = dp_swap(two[half:], 1)
    return [value, one, two, jnp.concatenate([first, second], axis=0)]


def plane_scatter(parts):
    size = len(parts)
    if size != 4:
        total = parts[0].astype(F32)
        for k in range(1, size):
            total = total + dp_swap(parts[k], k).astype(F32)
        return total
    half = parts[0].shape[0] // 2
    far_two = dp_swap(parts[3][:half], 1)
    far_one = dp_swap(parts[3][half:], 2)
    for_two = jnp.concatenate(
        [(parts[2][:half].astype(F32) + far_two.astype(F32)).astype(BF16), parts[2][half:]], axis=0
    )
    for_one = jnp.concatenate(
        [parts[1][:half], (parts[1][half:].astype(F32) + far_one.astype(F32)).astype(BF16)], axis=0
    )
    return (
        parts[0].astype(F32)
        + dp_swap(for_one, 1).astype(F32)
        + dp_swap(for_two, 2).astype(F32)
    )


def line_scatter(terms):
    count = terms.shape[0]
    size = lax.axis_size("fsdp")
    z = lax.axis_index("fsdp") // 2
    right = left = None
    for step in range(count - 1):
        out = pick(terms, jnp.clip(count - 1 - step + z, 0, count - 1))
        if right is not None:
            out = (out.astype(F32) + right.astype(F32)).astype(BF16)
        right = lax.ppermute(
            out, "fsdp", [(i, i + 2) for i in range(size - 2) if i // 2 <= step]
        )
        out = pick(terms, jnp.clip(z - (count - 1 - step), 0, count - 1))
        if left is not None:
            out = (out.astype(F32) + left.astype(F32)).astype(BF16)
        left = lax.ppermute(
            out, "fsdp", [(i, i - 2) for i in range(2, size) if count - 1 - i // 2 <= step]
        )
    return pick(terms, z).astype(F32) + right.astype(F32) + left.astype(F32)


def gather_rows(block):
    t_size, f_size = lax.axis_size("dp"), lax.axis_size("fsdp")
    z_size = f_size // 2
    dp, fs = lax.axis_index("dp"), lax.axis_index("fsdp")
    z, core = fs // 2, fs % 2
    rows, cols = block.shape
    line = jnp.zeros((z_size, rows, cols), block.dtype)
    line = put(line, block, z)
    for k in range(1, z_size):
        line = put(line, z_swap(block, k), z ^ k)
    plane = jnp.zeros((t_size, z_size, rows, cols), block.dtype)
    for k, piece in enumerate(plane_gather(line)):
        plane = put(plane, piece, dp ^ k)
    whole = jnp.zeros((t_size, z_size, 2, rows, cols), block.dtype)
    whole = put(whole, plane, core, 2)
    whole = put(whole, core_swap(plane), 1 - core, 2)
    return whole.reshape(t_size * f_size * rows, cols)


def core_sum(mine, other):
    return (mine.astype(F32) + core_swap(other).astype(F32)).astype(BF16)


def scatter_rows(grads):
    t_size, f_size = lax.axis_size("dp"), lax.axis_size("fsdp")
    z_size = f_size // 2
    dp, fs = lax.axis_index("dp"), lax.axis_index("fsdp")
    core = fs % 2
    rows = grads.shape[0] // (t_size * f_size)
    split = grads.reshape(t_size, z_size, 2, rows, grads.shape[1])
    chip = core_sum(pick(split, core, 2), pick(split, 1 - core, 2))
    line = plane_scatter([pick(chip, dp ^ k) for k in range(t_size)])
    return line_scatter(line.astype(BF16))


def scatter_fsdp(split, axis):
    f_size = lax.axis_size("fsdp")
    core = lax.axis_index("fsdp") % 2
    shape = split.shape
    pairs = split.reshape(shape[:axis] + (f_size // 2, 2) + shape[axis + 1 :])
    chip = core_sum(pick(pairs, core, axis + 1), pick(pairs, 1 - core, axis + 1))
    return line_scatter(jnp.moveaxis(chip, axis, 0))


def norm_back(grad_normed, scaled, inv_rms, gain_full):
    grad_scaled = grad_normed * gain_full
    grad_gain = jnp.sum(grad_normed * scaled, axis=0)
    grad_in = inv_rms * (
        grad_scaled - scaled * jnp.mean(grad_scaled * scaled, axis=-1, keepdims=True)
    )
    return (grad_gain, grad_in)


def update(weight, moment, average, grad, rate):
    moment_new = MOMENTUM * moment + grad
    weight_new = weight - rate * (grad + MOMENTUM * moment_new)
    average_new = AVERAGE * average + (1.0 - AVERAGE) * weight_new
    return (moment_new, weight_new, average_new)


LINE_ORDER = (0, 2, 1, 3)
PIECES = ((0, LINE_ORDER), (1, LINE_ORDER), (2, LINE_ORDER), (3, (0, 2)), (3, (1, 3)))
SMEM = pl.BlockSpec(memory_space=pltpu.SMEM)
VMEM = pl.BlockSpec(memory_space=pltpu.VMEM)
ANY = pl.BlockSpec(memory_space=pl.ANY)


def place():
    fs = lax.axis_index("fsdp")
    return jnp.stack([lax.axis_index("dp"), fs // 2, fs % 2]).astype(jnp.int32)


def after(value, *others):
    leaves, tree = jax.tree.flatten(value)
    kept = lax.optimization_barrier((*leaves, *others))[: len(leaves)]
    return jax.tree.unflatten(tree, kept)


SPLIT = 96


def slices_kernel(spot, gate, up, down, *outs):
    outs, packed = outs[:-1], outs[-1]
    units = packed.shape[1]
    for k, out in enumerate(outs):
        at = pl.ds(pl.multiple_of((spot[0] ^ k) * units, units), units)
        out[0] = gate[:, at].astype(BF16)
        out[1] = up[:, at].astype(BF16)
    rows, width = down.shape
    rest = width - units
    packed[:rows] = down[:, :units].astype(BF16)
    packed[rows:] = jnp.zeros((SPLIT, units), BF16)
    packed[rows : rows + SPLIT, :rest] = down[:SPLIT, units:].astype(BF16)
    packed[rows : 2 * rows - SPLIT, rest : 2 * rest] = down[SPLIT:, units:].astype(BF16)


def slices(spot, gate, up, down, count):
    rows, units = gate.shape[0], gate.shape[1] // count
    return pl.pallas_call(
        slices_kernel,
        in_specs=[SMEM, VMEM, VMEM, VMEM],
        out_specs=[VMEM] * (count + 1),
        out_shape=[jax.ShapeDtypeStruct((2, rows, units), BF16)] * count
        + [jax.ShapeDtypeStruct((down.shape[0] + SPLIT, units), BF16)],
        name="slices",
        **limits(0, 12 * gate.size, 0),
    )(spot, gate, up, down)


def gather_line(block):
    two, one = z_swap(block, 2), z_swap(block, 1)
    return jnp.stack([block, two, one, z_swap(two, 1)])


def plane_near(value):
    return dp_swap(value, 1), dp_swap(value, 2)


def plane_far(one, two):
    first, second = cut(one, 0), cut(two, 1)
    return dp_swap(first, 2), dp_swap(second, 1)


def cut_kernel(whole, out):
    out[...] = whole[...]


def cut(whole, index):
    half = whole.shape[0] // 2
    rest = (0,) * (whole.ndim - 1)
    steps = 2 if whole.ndim > 2 else half // 96
    block = (half // steps,) + whole.shape[1:]
    return pl.pallas_call(
        cut_kernel,
        grid=(steps,),
        in_specs=[pl.BlockSpec(block, lambda g: (index * steps + g,) + rest)],
        out_specs=pl.BlockSpec(block, lambda g: (g,) + rest),
        out_shape=jax.ShapeDtypeStruct((half,) + whole.shape[1:], whole.dtype),
        name="cut",
        **limits(0, 2 * whole.size),
    )(whole)


def fetch_rows(spot, pieces, held, sems):
    z, core = spot[1], spot[2]
    copies = [[] for _ in range(4)]
    for side in range(2):
        for (k, line), piece in zip(PIECES, pieces[side * len(PIECES) :]):
            for at, j in enumerate(line):
                slot = held.at[k, z ^ j, core ^ side]
                sem = sems.at[k, 2 * j + side]
                copies[k].append(pltpu.make_async_copy(piece.at[at], slot, sem))
    for some in copies:
        for copy in some:
            copy.start()
    return copies


def blocks_of(spot, copies, held):
    count, z_size, cores, rows, cols = held.shape
    size = z_size * cores * rows
    for k in range(count):
        for copy in copies[k]:
            copy.wait()
        at = pl.ds(pl.multiple_of((spot[0] ^ k) * size, size), size)
        yield k, at, held[k].reshape(size, cols)


def held_shapes(pieces):
    rows, cols = pieces[0].shape[1:]
    return [pltpu.VMEM((4, 4, 2, rows, cols), BF16), pltpu.SemaphoreType.DMA((4, 8))]


def inverse_rms(values):
    return lax.rsqrt(jnp.mean(values * values, axis=-1, keepdims=True) + EPS)


def enter_kernel(spot, tokens, *refs):
    pieces, (raw, normed, gains, held, sems) = refs[:-5], refs[-5:]
    copies = fetch_rows(spot, pieces, held, sems)
    values = tokens[...].astype(F32)
    inv_rms = inverse_rms(values)
    cols = raw.shape[1]
    for k, at, weight in blocks_of(spot, copies, held):
        turned = weight[:, cols:].astype(F32).T
        gains[:, at] = turned[: gains.shape[0]]
        scaled = tokens[:, at].astype(F32) * inv_rms
        normed[:, at] = (scaled * turned[:1]).astype(BF16)
        found = dot(normed[:, at], weight[:, :cols], (1, 0))
        raw[...] = found if k == 0 else raw[...] + found


def enter(spot, tokens, pieces):
    count, width = tokens.shape
    cols = pieces[0].shape[2] - 128
    return pl.pallas_call(
        enter_kernel,
        in_specs=[SMEM, VMEM] + [ANY] * len(pieces),
        out_specs=[VMEM] * 3,
        out_shape=[
            jax.ShapeDtypeStruct((count, cols), F32),
            jax.ShapeDtypeStruct((count, width), BF16),
            jax.ShapeDtypeStruct((8, width), F32),
        ],
        scratch_shapes=held_shapes(pieces),
        name="enter",
        **limits(2 * count * width * cols, 2 * width * cols, 0),
    )(spot, tokens, *pieces)


def leave_kernel(spot, attended, tokens, gains, *refs):
    pieces, (resid, normed, held, sems) = refs[:-4], refs[-4:]
    copies = fetch_rows(spot, pieces, held, sems)
    resid[...] = tokens[...].astype(F32)
    for _, at, weight in blocks_of(spot, copies, held):
        resid[...] += dot(attended[:, at], weight, (1, 0))
    values = resid[...]
    normed[...] = (values * inverse_rms(values) * gains[1:2]).astype(BF16)


def leave(spot, attended, tokens, gains, pieces):
    count, width = tokens.shape
    return pl.pallas_call(
        leave_kernel,
        in_specs=[SMEM] + [VMEM] * 3 + [ANY] * len(pieces),
        out_specs=[VMEM] * 2,
        out_shape=[
            jax.ShapeDtypeStruct((count, width), F32),
            jax.ShapeDtypeStruct((count, width), BF16),
        ],
        scratch_shapes=held_shapes(pieces),
        name="leave",
        **limits(2 * count * width * width, 2 * width * width, 0),
    )(spot, attended, tokens, gains, *pieces)


def leave_back_kernel(spot, grads, *refs):
    pieces, (out, held, sems) = refs[:-3], refs[-3:]
    copies = fetch_rows(spot, pieces, held, sems)
    for _, at, weight in blocks_of(spot, copies, held):
        out[:, at] = dot(grads[...], weight, (1, 1), BF16)


def leave_back(spot, grads, pieces):
    count, width = grads.shape
    return pl.pallas_call(
        leave_back_kernel,
        in_specs=[SMEM, VMEM] + [ANY] * len(pieces),
        out_specs=VMEM,
        out_shape=jax.ShapeDtypeStruct((count, width), BF16),
        scratch_shapes=held_shapes(pieces),
        name="leave_back",
        **limits(2 * count * width * width, 2 * width * width, 0),
    )(spot, grads, *pieces)


def enter_back_kernel(spot, grads, tokens, gains, grad_resid, *refs):
    pieces, (out, grad_gain, held, sems) = refs[:-4], refs[-4:]
    copies = fetch_rows(spot, pieces, held, sems)
    for _, at, weight in blocks_of(spot, copies, held):
        out[:, at] = dot(grads[...], weight, (1, 1))
    values = tokens[...].astype(F32)
    inv_rms = inverse_rms(values)
    total, through = norm_back(out[...], values * inv_rms, inv_rms, gains[:1])
    grad_gain[...] = jnp.broadcast_to(total[None], grad_gain.shape)
    out[...] = grad_resid[...] + through


def enter_back(spot, grads, tokens, gains, grad_resid, pieces):
    count, width = tokens.shape
    return pl.pallas_call(
        enter_back_kernel,
        in_specs=[SMEM] + [VMEM] * 4 + [ANY] * len(pieces),
        out_specs=[VMEM] * 2,
        out_shape=[
            jax.ShapeDtypeStruct((count, width), F32),
            jax.ShapeDtypeStruct((8, width), F32),
        ],
        scratch_shapes=held_shapes(pieces),
        name="enter_back",
        **limits(2 * count * width * width, 2 * width * width, 0),
    )(spot, grads, tokens, gains, grad_resid, *pieces)


TOKEN_ORDER = (1, 3, 2, 0)


def ffn_all_kernel(spot, *refs):
    ins, held_in = (refs[:5], refs[5:10]), refs[10]
    wholes, (hidden, grad_gate, grad_up, sums, out) = refs[11:13], refs[13:18]
    sent_a, sent_b = refs[18:20]
    gate_w, up_w, down_w, tiles, grad_tile, out_tile, sems, in_sems, out_sems = refs[20:]
    count, f_size, rows, units = gate_w.shape
    step = pl.program_id(0)
    first = step == 0
    size = tiles.shape[2]
    half = size // 2
    copies = [
        [
            pltpu.make_async_copy(
                held_in.at[:, pl.ds((2 * k + which) * rows, rows)], buffer.at[spot[0] ^ k],
                sems.at[which, k],
            )
            for k in range(count)
        ]
        for which, buffer in enumerate((gate_w, up_w))
    ]
    above, (low, width) = 2 * count * rows, down_w.shape[1:]
    rest = width - units
    copies.append(
        [
            pltpu.make_async_copy(
                held_in.at[:, pl.ds(above, low)], down_w.at[:, :, pl.ds(0, units)], sems.at[2, 0]
            ),
            pltpu.make_async_copy(
                held_in.at[:, pl.ds(above + low, SPLIT), pl.ds(0, rest)],
                down_w.at[:, pl.ds(0, SPLIT), pl.ds(units, rest)],
                sems.at[2, 1],
            ),
            pltpu.make_async_copy(
                held_in.at[:, pl.ds(above + low, low - SPLIT), pl.ds(rest, rest)],
                down_w.at[:, pl.ds(SPLIT, low - SPLIT), pl.ds(units, rest)],
                sems.at[2, 2],
            ),
        ]
    )

    def brought(at):
        k, some = TOKEN_ORDER[at], []
        for which, pieces in enumerate(ins):
            slot = tiles.at[at % 2, which]
            parts = pieces[k : k + 1] if k < 3 else pieces[3:]
            for i, piece in enumerate(parts):
                target = slot.at[pl.ds(i * half, half)] if k == 3 else slot
                some.append(pltpu.make_async_copy(piece, target, in_sems.at[at % 2, which, i]))
        return some

    def kept(at):
        return [
            pltpu.make_async_copy(
                tiles.at[at % 2, which], whole.at[pl.ds(at * size, size)], out_sems.at[at % 2, which]
            )
            for which, whole in enumerate(wholes)
        ]

    for at in range(4):

        @pl.when(step == at)
        def _():
            if at == 0:
                for copy in brought(0):
                    copy.start()
                for held in copies:
                    for copy in held:
                        copy.start()
            for copy in brought(at):
                copy.wait()
            if at > 0:
                for copy in kept(at - 1):
                    copy.wait()
            for copy in kept(at):
                copy.start()
            if at < 3:
                for copy in brought(at + 1):
                    copy.start()

    normed, cot = tiles.at[step % 2, 0], tiles.at[step % 2, 1]

    def weight(which, buffer):
        waited = []

        def read():
            if not waited:
                waited.append(True)

                @pl.when(first)
                def _():
                    for copy in copies[which]:
                        copy.wait()

            return buffer[...].reshape(-1, buffer.shape[-1])

        return read

    ffn_tile(
        normed, cot, weight(0, gate_w), weight(1, up_w), weight(2, down_w),
        hidden, grad_gate, grad_up, grad_tile, out_tile,
    )
    for i in range(2):
        sums[i, 0] = grad_tile[i * half : (i + 1) * half]
        out[i, 0] = out_tile[i * half : (i + 1) * half]

    @pl.when(step < 2)
    def _():
        sent_a[0] = grad_tile[:half]

    @pl.when((step > 0) & (step < 3))
    def _():
        sent_b[0] = grad_tile[half:]

    @pl.when(step == 3)
    def _():
        for copy in kept(3):
            copy.wait()


def ffn_all(spot, normed, cot, held_in, t_size, low):
    count, width = normed[0].shape
    half = count // 2
    f_size, above, units = held_in.shape
    rows = (above - low - SPLIT) // (2 * t_size)
    inner = pl.BlockSpec((count, units), lambda t: (t, 0))
    sums = pl.BlockSpec((2, 1, half, width), lambda t: (0, t, 0, 0))
    sent = lambda low: pl.BlockSpec(
        (1, half, width), lambda t: (jnp.clip(t - low, 0, 1), 0, 0)
    )
    weights = pltpu.VMEM((t_size, f_size, rows, units), BF16)
    total = 4 * count
    return pl.pallas_call(
        ffn_all_kernel,
        grid=(4,),
        in_specs=[SMEM] + [ANY] * 11,
        out_specs=[ANY, ANY, inner, inner, inner, sums, sums, sent(0), sent(1)],
        scratch_shapes=[
            weights,
            weights,
            pltpu.VMEM((f_size, low, width), BF16),
            pltpu.VMEM((2, 2, count, width), BF16),
            pltpu.VMEM((count, width), BF16),
            pltpu.VMEM((count, width), BF16),
            pltpu.SemaphoreType.DMA((3, t_size)),
            pltpu.SemaphoreType.DMA((2, 2, 2)),
            pltpu.SemaphoreType.DMA((2, 2)),
        ],
        out_shape=[jax.ShapeDtypeStruct((total, width), BF16)] * 2
        + [jax.ShapeDtypeStruct((total, units), BF16)] * 3
        + [jax.ShapeDtypeStruct((2, 4, half, width), BF16)] * 2
        + [jax.ShapeDtypeStruct((2, half, width), BF16)] * 2,
        name="ffn_all",
        **limits(12 * total * width * units, 6 * width * units + 8 * total * width),
    )(spot, *normed, *cot, held_in)


class TokenSum:
    def __init__(self, terms, sent=None):
        self.own = terms
        self.sent = sent or add([[(terms, 0)], [(terms, 5)]], 2)
        self.a, self.b = dp_swap(self.sent[0], 1), dp_swap(self.sent[1], 2)

    def cross(self):
        self.crossed = add([[(self.own, 2), (self.a, 1)], [(self.own, 4), (self.b, 0)]], 1)
        self.last_a, self.last_b = dp_swap(self.crossed[0], 2), dp_swap(self.crossed[1], 1)

    def parts(self):
        return [
            [(flat(self.own), 3), (self.a, 0), (self.last_a, 0)],
            [(flat(self.own), 7), (self.b, 1), (self.last_b, 0)],
        ]


def add_kernel(counts, *refs):
    outs = refs[len(refs) - len(counts) :]
    at = 0
    for count, out in zip(counts, outs):
        total = refs[at][...].astype(F32)
        for ref in refs[at + 1 : at + count]:
            total = total + ref[...].astype(F32)
        out[...] = total.astype(out.dtype)
        at += count


def flat(array):
    return array.reshape((-1,) + array.shape[-2:])


def add(jobs, count, group=1):
    operands = [flat(array) for job in jobs for array, _ in job]
    starts = [start for job in jobs for _, start in job]
    block = (group,) + operands[0].shape[1:]
    spec = lambda start: pl.BlockSpec(block, lambda g: (g + start // group, 0, 0))
    return pl.pallas_call(
        functools.partial(add_kernel, [len(job) for job in jobs]),
        grid=(count // group,),
        in_specs=[spec(start) for start in starts],
        out_specs=[spec(0)] * len(jobs),
        out_shape=[jax.ShapeDtypeStruct((count,) + block[1:], BF16)] * len(jobs),
        name="add",
        **limits(0, 2 * (len(starts) + len(jobs)) * count * block[1] * block[2]),
    )(*operands)


def turns(step):
    return jnp.minimum(step, 2), jnp.maximum(step - 3, 0)


def half_specs(parts, rows):
    specs = []
    for side, terms in enumerate(parts):
        for array, start in terms:
            shape = (1, rows, array.shape[-1])
            specs.append(
                pl.BlockSpec(shape, lambda t, side=side, start=start: (start, turns(t)[side], 0))
            )
    return specs


def half_total(refs, side):
    some = refs[side * 3 : side * 3 + 3]
    return some[0][0].astype(F32) + some[1][0].astype(F32) + some[2][0].astype(F32)


def branch_kernel(resid, cot, gains, *refs):
    terms, (grad_resid, grad_branch, grad_gain) = refs[:6], refs[6:]
    step = pl.program_id(0)

    def finish(grads):
        inv_rms = inverse_rms(resid[...])
        total, through = norm_back(grads, resid[...] * inv_rms, inv_rms, gains[1:2])
        sums = jnp.broadcast_to(total[None], grad_gain.shape)

        @pl.when(step == 0)
        def _():
            grad_gain[...] = sums

        @pl.when(step > 0)
        def _():
            grad_gain[...] += sums

        grads = cot[...].astype(F32) + through
        grad_resid[...] = grads
        grad_branch[...] = grads.astype(BF16)

    for side in range(2):

        @pl.when(step // 3 == side)
        def _():
            finish(half_total(terms, side))


def branch(resid, cot, gains, parts):
    count, width = resid.shape
    rows = count // 6
    token = pl.BlockSpec((rows, width), lambda t: (t, 0))
    fixed = pl.BlockSpec((8, width), lambda t: (0, 0))
    return pl.pallas_call(
        branch_kernel,
        grid=(6,),
        in_specs=[token, token, fixed] + half_specs(parts, rows),
        out_specs=[token, token, fixed],
        out_shape=[
            jax.ShapeDtypeStruct((count, width), F32),
            jax.ShapeDtypeStruct((count, width), BF16),
            jax.ShapeDtypeStruct((8, width), F32),
        ],
        name="branch",
        **limits(0, 18 * count * width),
    )(resid, cot, gains, *[array for terms in parts for array, _ in terms])


def layer_out_kernel(resid, *refs):
    terms, out = refs[:6], refs[6]
    for side in range(2):

        @pl.when(pl.program_id(0) // 3 == side)
        def _():
            out[...] = resid[...] + half_total(terms, side)


def layer_out_of(resid, parts):
    count, width = resid.shape
    rows = count // 6
    token = pl.BlockSpec((rows, width), lambda t: (t, 0))
    return pl.pallas_call(
        layer_out_kernel,
        grid=(6,),
        in_specs=[token] + half_specs(parts, rows),
        out_specs=token,
        out_shape=jax.ShapeDtypeStruct((count, width), F32),
        name="layer_out",
        **limits(0, 14 * count * width),
    )(resid, *[array for terms in parts for array, _ in terms])


def row_grads_kernel(spot, left, right, *refs):
    gains = refs[:-3]
    mine, other, held = refs[-3:]
    count, _, rows, cols = held.shape
    found = dot(left[...], right[...], (0, 0), BF16)
    if gains:
        shape = (128, left.shape[1])
        which = lax.broadcasted_iota(jnp.int32, shape, 0)
        one, two = gains[0][:1], gains[1][:1]
        extra = jnp.where(which == 0, one, jnp.where(which == 1, two, 0.0)).T.astype(BF16)
    for i in range(count):
        for core in range(2):
            at = (2 * i + core) * rows
            held[i, core, :, : found.shape[1]] = found[at : at + rows]
            if gains:
                held[i, core, :, found.shape[1] :] = extra[at : at + rows]
    z, core = spot[1], spot[2]
    for half in range(2):
        for at in range(2):
            mine[half, 0, at] = held[z ^ (2 * at + half), core]
            other[half, 0, at] = held[z ^ (2 * at + half), 1 - core]


def row_grads(spot, left, right, right_cols, gains=()):
    count, width = left.shape
    rows = width // 32
    cols = right_cols + (128 if gains else 0)
    turn = lambda k, spot: spot[0] ^ k ^ (k >> 1)
    out = pl.BlockSpec((2, 1, 2, rows, cols), lambda k, spot: (0, k, 0, 0, 0))
    gain = pl.BlockSpec((8, width // 4), lambda k, spot: (0, turn(k, spot)))
    return pl.pallas_call(
        row_grads_kernel,
        grid_spec=pltpu.PrefetchScalarGridSpec(
            num_scalar_prefetch=1,
            grid=(4,),
            in_specs=[
                pl.BlockSpec((count, width // 4), lambda k, spot: (0, turn(k, spot))),
                pl.BlockSpec((count, right_cols), lambda k, spot: (0, 0)),
            ]
            + [gain] * len(gains),
            out_specs=[out, out],
            scratch_shapes=[pltpu.VMEM((4, 2, rows, cols), BF16)],
        ),
        out_shape=[jax.ShapeDtypeStruct((2, 4, 2, rows, cols), BF16)] * 2,
        name="row_grads",
        **limits(2 * count * width * cols, 2 * width * cols + 2 * count * (width + cols)),
    )(spot, left, right, *gains)


class RowSum:
    def __init__(self, mine, other):
        self.mine, self.other = mine, core_swap(other)

    def plane(self):
        pair = lambda start: [(self.mine, start), (self.other, start)]
        a, b = self.sent = add([pair(2), pair(12)], 4, 2)
        self.a, self.b = dp_swap(a, 1), dp_swap(b, 2)

    def cross(self):
        a, b = self.crossed = add(
            [
                [(self.mine, 6), (self.other, 6), (self.a, 2)],
                [(self.mine, 10), (self.other, 10), (self.b, 0)],
            ],
            2,
        )
        self.last_a, self.last_b = dp_swap(a, 2), dp_swap(b, 1)

    def near(self):
        terms = [(self.mine, 8), (self.other, 8), (self.b, 2), (self.last_b, 0)]
        self.odd = add([terms], 2)[0]
        self.line = z_swap(self.odd, 1)

    def terms(self, at):
        return [(x, at) for x in (self.mine, self.other, self.a, self.last_a, self.line)]

    def far(self):
        self.rest = add([self.terms(1)], 1)[0]
        self.last = z_swap(self.rest, 2)

    def final(self):
        return self.terms(0) + [(self.last, 0)]


class LineSum:
    def __init__(self, mine, other):
        self.mine, self.other = mine, core_swap(other)

    def line(self):
        blocks = self.mine.shape[0]
        count = flat(self.mine).shape[0]
        self.chip = add([[(self.mine, 0), (self.other, 0)]], count, count // blocks)[0]
        size = lax.axis_size("fsdp")
        groups = [list(range(core, size, 2)) for core in range(2)]
        self.total = lax.psum_scatter(
            self.chip, "fsdp", scatter_dimension=0, axis_index_groups=groups, tiled=True
        )


def chunk_dot(lefts, rights):
    found = dot(lefts[0][...], rights[0][...], (0, 0))
    for left, right in zip(lefts[1:], rights[1:]):
        found = found + dot(left[...], right[...], (0, 0))
    return found.astype(BF16)


def place_line(spot, found, held, mine, other):
    count, _, rows, _ = held.shape
    core = spot[2]
    for i in range(count):
        for side in range(2):
            at = (2 * i + side) * rows
            held[i, side] = found[at : at + rows]
    for at in range(count):
        mine[at] = held[at, core].reshape(mine.shape[1:])
        other[at] = held[at, 1 - core].reshape(other.shape[1:])


def line_grads_kernel(spot, *refs):
    mine, other, held = refs[-3:]
    chunks = (len(refs) - 3) // 2
    found = chunk_dot(refs[:chunks], refs[chunks : 2 * chunks])
    place_line(spot, found, held, mine, other)


def unit_grads(spot, lefts, rights):
    count, width = lefts[0].shape
    units, rows = rights[0].shape[1], width // 32
    out = pl.BlockSpec((4, 1, rows, units), lambda k, spot: (0, k, 0, 0))
    left = pl.BlockSpec((count, width // 4), lambda k, spot: (0, spot[0] ^ k))
    right = pl.BlockSpec((count, units), lambda k, spot: (0, 0), pipeline_mode=pl.Buffered(1))
    total = count * len(lefts)
    return pl.pallas_call(
        line_grads_kernel,
        grid_spec=pltpu.PrefetchScalarGridSpec(
            num_scalar_prefetch=1,
            grid=(4,),
            in_specs=[left] * len(lefts) + [right] * len(rights),
            out_specs=[out, out],
            scratch_shapes=[pltpu.VMEM((4, 2, rows, units), BF16)],
        ),
        out_shape=[jax.ShapeDtypeStruct((4, 4, rows, units), BF16)] * 2,
        name="unit_grads",
        **limits(2 * total * width * units, 2 * width * units + 2 * total * (width + units)),
    )(spot, *lefts, *rights)


def down_grads(spot, lefts, rights):
    count, units = lefts[0].shape
    width = rights[0].shape[1]
    rows, tile = units // 8, width // 4
    out = pl.BlockSpec((4, rows, tile), lambda n, spot: (0, 0, n))
    left = pl.BlockSpec((count, units), lambda n, spot: (0, 0), pipeline_mode=pl.Buffered(1))
    right = pl.BlockSpec((count, tile), lambda n, spot: (0, n))
    total = count * len(lefts)
    return pl.pallas_call(
        line_grads_kernel,
        grid_spec=pltpu.PrefetchScalarGridSpec(
            num_scalar_prefetch=1,
            grid=(4,),
            in_specs=[left] * len(lefts) + [right] * len(rights),
            out_specs=[out, out],
            scratch_shapes=[pltpu.VMEM((4, 2, rows, tile), BF16)],
        ),
        out_shape=[jax.ShapeDtypeStruct((4, rows, width), BF16)] * 2,
        name="down_grads",
        **limits(2 * total * width * units, 2 * width * units + 2 * total * (width + units)),
    )(spot, *lefts, *rights)


def sum_of(refs):
    total = refs[0][0].astype(F32)
    for ref in refs[1:]:
        total = total + ref[0].astype(F32)
    return total


def update_rows_kernel(rates, count, *refs):
    terms, rest = refs[:count], refs[count:]
    held = 3 * len(rates)
    ins, outs = rest[:held], rest[held:]
    grads = sum_of(terms)
    at = 0
    for i, rate in enumerate(rates):
        own = ins[3 * i : 3 * i + 3]
        cols = own[0].shape[1]
        piece = grads[:, at : at + cols]
        at += cols
        results = update(*[ref[...] for ref in own], piece, rate)
        for out, result in zip(outs[3 * i :], results):
            out[...] = result
    if at < grads.shape[1]:
        outs[-1][...] = grads[:, at:]


def update_rows(terms, weights, rates):
    operands = [flat(array) for array, _ in terms]
    block = (1,) + operands[0].shape[1:]
    left = block[2] - sum(w[0].shape[1] for w in weights)
    arrays = [array for some in weights for array in some]
    shapes = [jax.ShapeDtypeStruct(array.shape, F32) for array in arrays]
    if left:
        shapes.append(jax.ShapeDtypeStruct((block[1], left), F32))
    whole = lambda shape: pl.BlockSpec(shape, lambda g: (0, 0))
    return pl.pallas_call(
        functools.partial(update_rows_kernel, rates, len(terms)),
        grid=(1,),
        in_specs=[pl.BlockSpec(block, lambda g, start=start: (start, 0, 0)) for _, start in terms]
        + [whole(array.shape) for array in arrays],
        out_specs=[whole(shape.shape) for shape in shapes],
        out_shape=shapes,
        name="update_rows",
        **limits(0, 32 * arrays[0].size),
    )(*operands, *arrays)


def update_units_kernel(rate, spot, weight, moment, average, *refs):
    pieces, outs = refs[:4], refs[4:]
    units = pieces[0].shape[-1]
    for k in range(4):
        grads = pieces[k][0].astype(F32)
        at = pl.ds(pl.multiple_of((spot[0] ^ k) * units, units), units)
        results = update(weight[:, at], moment[:, at], average[:, at], grads, rate)
        for out, result in zip(outs, results):
            out[:, at] = result


def update_units(spot, weight, moment, average, pieces, which, rate):
    block = (1,) + pieces[0].shape[1:]
    first = pl.BlockSpec(block, lambda g: (which, 0, 0))
    whole = pl.BlockSpec(weight.shape, lambda g: (0, 0))
    return pl.pallas_call(
        functools.partial(update_units_kernel, rate),
        grid=(1,),
        in_specs=[SMEM] + [whole] * 3 + [first] * 4,
        out_specs=[whole] * 3,
        out_shape=[jax.ShapeDtypeStruct(weight.shape, F32)] * 3,
        name="update_units",
        **limits(0, 32 * weight.size),
    )(spot, weight, moment, average, *pieces)


def shards_any(
    tokens_in,
    out_grad,
    kv_grad_next,
    doc_ids,
    gains,
    gains_mom,
    gains_ema,
    w_query,
    query_mom,
    query_ema,
    w_keyval,
    keyval_mom,
    keyval_ema,
    w_output,
    output_mom,
    output_ema,
    w_gate,
    gate_mom,
    gate_ema,
    w_up,
    up_mom,
    up_ema,
    w_down,
    down_mom,
    down_ema,
):
    t_size, f_size = lax.axis_size("dp"), lax.axis_size("fsdp")
    dp = lax.axis_index("dp")
    seq_count, length = doc_ids.shape
    width = tokens_in.shape[1]
    head_dim = w_keyval.shape[1] // 2
    head_count = w_query.shape[1] // head_dim
    hidden_units = w_gate.shape[1]
    rows = seq_count * length
    heads_width = head_count * head_dim
    tokens_total = rows * t_size * f_size
    own_rows = w_query.shape[0]
    slice_units = hidden_units // t_size

    gain_cols = jnp.zeros((own_rows, 128), BF16).at[:, :2].set(gains.astype(BF16).T)
    qkv_block = jnp.concatenate([w_query.astype(BF16), w_keyval.astype(BF16), gain_cols], axis=1)

    def to_slices(weight):
        split = weight.astype(BF16).reshape(own_rows, t_size, slice_units)
        held = jnp.zeros((t_size, own_rows, slice_units), BF16)
        held = put(held, pick(split, dp, 1), dp)
        for k in range(1, t_size):
            held = put(held, dp_swap(pick(split, dp ^ k, 1), k), dp ^ k)
        whole = lax.all_gather(held, "fsdp", axis=0)
        return jnp.swapaxes(whole, 0, 1).reshape(width, slice_units)

    qkv_full = gather_rows(qkv_block)
    output_full = gather_rows(w_output.astype(BF16))
    gate_slice = to_slices(w_gate)
    up_slice = to_slices(w_up)
    gain_rows = qkv_full[:, -128:]
    down_block = w_down.astype(BF16)
    down_slice = lax.all_gather(down_block, "fsdp", axis=0, tiled=True)
    cot_all = jnp.concatenate(plane_gather(out_grad), axis=0)

    inputs = tokens_in.astype(F32)
    inv_rms = lax.rsqrt(jnp.mean(inputs * inputs, axis=-1, keepdims=True) + EPS)
    scaled = inputs * inv_rms
    gains_full = gain_rows[:, :2].astype(F32).T
    gain_attn, gain_ffn = gains_full[0], gains_full[1]
    normed = (scaled * gain_attn).astype(BF16)
    raw = dot(normed, qkv_full, (1, 0))
    cosine, sine = rotation(positions_of(doc_ids).reshape(rows), head_dim)
    queries, attended, shared = attend(raw, cosine, sine, doc_ids, head_count, head_dim)
    resid = inputs + dot(attended, output_full, (1, 0))

    inv_rms2 = lax.rsqrt(jnp.mean(resid * resid, axis=-1, keepdims=True) + EPS)
    scaled2 = resid * inv_rms2
    normed2 = (scaled2 * gain_ffn).astype(BF16)
    normed2_all = jnp.concatenate(plane_gather(normed2), axis=0)
    results = ffn(normed2_all, cot_all, gate_slice, up_slice, down_slice)
    hidden, grad_gate, grad_up, grad_normed2_part, ffn_part = results
    grad_normed2 = plane_scatter(
        [grad_normed2_part[k * rows : (k + 1) * rows] for k in range(t_size)]
    )
    ffn_out = plane_scatter([ffn_part[k * rows : (k + 1) * rows] for k in range(t_size)])
    layer_out = resid + ffn_out
    def from_slices(grads):
        own = scatter_fsdp(grads.reshape(t_size, f_size, own_rows, slice_units), 1)
        own = own.reshape(t_size, own_rows, slice_units)
        held = jnp.zeros((own_rows, t_size, slice_units), F32)
        held = put(held, pick(own, dp), dp, 1)
        for k in range(1, t_size):
            sent = dp_swap(pick(own, dp ^ k).astype(BF16), k)
            held = put(held, sent.astype(F32), dp ^ k, 1)
        return held.reshape(own_rows, hidden_units)

    grad_down_w = dot(hidden, cot_all, (0, 0), BF16)
    down_sum = scatter_fsdp(grad_down_w.reshape(f_size, -1, width), 0)
    gate_sum = from_slices(dot(normed2_all, grad_gate, (0, 0), BF16))
    up_sum = from_slices(dot(normed2_all, grad_up, (0, 0), BF16))

    grad_gain_ffn, grad_through = norm_back(grad_normed2, scaled2, inv_rms2, gain_ffn)
    grad_resid = out_grad.astype(F32) + grad_through
    grad_branch = grad_resid.astype(BF16)
    grad_attended = dot(grad_branch, output_full, (1, 1), BF16)
    output_sum = scatter_rows(dot(attended, grad_branch, (0, 0), BF16))
    grad_raw = attend_back(
        queries, grad_attended, shared, kv_grad_next, cosine, sine, doc_ids, head_count, head_dim
    )
    grad_normed = dot(grad_raw, qkv_full, (1, 1))
    grad_gain_attn, grad_first = norm_back(grad_normed, scaled, inv_rms, gain_attn)
    input_grad = grad_resid + grad_first
    gain_grads = jnp.zeros((width, 128), BF16)
    gain_grads = gain_grads.at[:, :2].set(
        jnp.stack([grad_gain_attn, grad_gain_ffn], axis=0).astype(BF16).T
    )
    qkv_sum = scatter_rows(dot(normed, grad_raw, (0, 0), BF16).at[:, -128:].set(gain_grads))
    query_sum = qkv_sum[:, :heads_width]
    keyval_sum = qkv_sum[:, heads_width : heads_width + 2 * head_dim]
    gains_sum = qkv_sum[:, -128:-126].T

    def rate(strength, fan):
        return strength / math.sqrt(fan * tokens_total)

    gains_out = update(gains, gains_mom, gains_ema, gains_sum, rate(0.1, 1))
    query_out = update(w_query, query_mom, query_ema, query_sum, rate(0.6, width))
    keyval_out = update(w_keyval, keyval_mom, keyval_ema, keyval_sum, rate(0.15, width))
    output_out = update(w_output, output_mom, output_ema, output_sum, rate(5.0, heads_width))
    gate_out = update(w_gate, gate_mom, gate_ema, gate_sum, rate(0.6, width))
    up_out = update(w_up, up_mom, up_ema, up_sum, rate(0.6, width))
    down_out = update(w_down, down_mom, down_ema, down_sum, rate(1.5, hidden_units))
    return (
        layer_out,
        shared.astype(F32),
        input_grad,
        *gains_out,
        *query_out,
        *keyval_out,
        *output_out,
        *gate_out,
        *up_out,
        *down_out,
    )


def shards_fast(
    tokens_in,
    out_grad,
    kv_grad_next,
    doc_ids,
    gains,
    gains_mom,
    gains_ema,
    w_query,
    query_mom,
    query_ema,
    w_keyval,
    keyval_mom,
    keyval_ema,
    w_output,
    output_mom,
    output_ema,
    w_gate,
    gate_mom,
    gate_ema,
    w_up,
    up_mom,
    up_ema,
    w_down,
    down_mom,
    down_ema,
):
    t_size, f_size = lax.axis_size("dp"), lax.axis_size("fsdp")
    seq_count, length = doc_ids.shape
    width = tokens_in.shape[1]
    head_dim = w_keyval.shape[1] // 2
    head_count = w_query.shape[1] // head_dim
    hidden_units = w_gate.shape[1]
    rows = seq_count * length
    half = rows // 2
    heads_width = head_count * head_dim
    raw_width = heads_width + 2 * head_dim
    tokens_total = rows * t_size * f_size
    own_rows = w_query.shape[0]
    spot = place()

    gain_cols = jnp.zeros((own_rows, 128), BF16).at[:, :2].set(gains.astype(BF16).T)
    qkv_block = jnp.concatenate([w_query.astype(BF16), w_keyval.astype(BF16), gain_cols], axis=1)
    qkv_line = gather_line(qkv_block)

    *sent, packed = slices(spot, w_gate, w_up, w_down, t_size)
    got = [sent[0]] + [dp_swap(sent[k], k) for k in range(1, t_size)]
    packed = jnp.concatenate([flat(piece).reshape(-1, piece.shape[-1]) for piece in got] + [packed])
    output_block = after(w_output.astype(BF16), qkv_line)
    output_two, output_one = z_swap(output_block, 2), z_swap(output_block, 1)
    output_last = z_swap(output_two, 1)
    output_line = [output_block, output_two, output_one, output_last]
    units_all = lax.all_gather(
        after(packed, output_line[1], output_line[3]), "fsdp", axis=0
    )
    output_line = jnp.stack(output_line)

    qkv_near = plane_near(after(qkv_line, packed))
    qkv_far = plane_far(*after(qkv_near, output_last))
    qkv_mine = [qkv_line, *qkv_near, *qkv_far]
    qkv_pieces = qkv_mine + [core_swap(piece) for piece in qkv_mine]
    output_near = plane_near(after(output_line, *qkv_far))
    cot_near = plane_near(after(out_grad, *qkv_pieces[8:]))

    raw, normed, gains_full = enter(spot, after(tokens_in, output_line), qkv_pieces)
    cosine, sine = rotation(positions_of(doc_ids).reshape(rows), head_dim)
    queries, attended, shared = attend(raw, cosine, sine, doc_ids, head_count, head_dim)
    output_mine = [output_line, *output_near, *plane_far(*after(output_near, attended))]
    output_pieces = output_mine + [core_swap(piece) for piece in output_mine]
    cot_first, cot_second = cut(cot_near[0], 0), cut(cot_near[1], 1)
    cot = [out_grad, *cot_near, dp_swap(cot_first, 2), dp_swap(cot_second, 1)]
    resid, normed2 = leave(spot, after(attended, cot_first, cot_second), tokens_in, gains_full, output_pieces)

    normed2_near = plane_near(after(normed2, *cot[3:]))
    normed2_all = [normed2, *normed2_near, *plane_far(*normed2_near)]
    tokens2, cots, hidden, grad_gate, grad_up, grad_terms, out_terms, *grads_sent = ffn_all(
        spot, normed2_all, cot, units_all, t_size, w_down.shape[0]
    )
    normed2_sum = TokenSum(grad_terms, grads_sent)
    down = LineSum(*down_grads(spot, [hidden], [cots]))
    gate = LineSum(*unit_grads(spot, [after(tokens2, down.mine)], [grad_gate]))
    down.other = after(down.other, gate.mine)
    down.line()
    normed2_sum.a, normed2_sum.b = after((normed2_sum.a, normed2_sum.b), down.chip)
    normed2_sum.cross()
    up = LineSum(*unit_grads(spot, [after(tokens2, *normed2_sum.crossed)], [grad_up]))
    grad_resid, grad_branch, grad_gain_ffn = branch(
        after(resid, up.mine), out_grad, gains_full, normed2_sum.parts()
    )
    out_sum = TokenSum(after(out_terms, grad_branch))

    output = RowSum(*row_grads(spot, attended, after(grad_branch, *out_sum.sent), width))
    grad_attended = leave_back(spot, after(grad_branch, output.mine), output_pieces)
    gate.other, output.other = after((gate.other, output.other), grad_attended)
    output.plane()
    gate.line()
    grad_raw = attend_back(
        queries, after(grad_attended, gate.chip, *output.sent), shared, kv_grad_next, cosine, sine,
        doc_ids, head_count, head_dim,
    )
    input_grad, grad_gain_attn = enter_back(
        spot, grad_raw, tokens_in, gains_full, grad_resid, qkv_pieces
    )
    out_sum.a, out_sum.b, output.a, output.b = after(
        (out_sum.a, out_sum.b, output.a, output.b), input_grad
    )
    output.cross()
    qkv = RowSum(
        *row_grads(
            spot, after(normed, *output.crossed, down.total), grad_raw, raw_width,
            (grad_gain_attn, grad_gain_ffn),
        )
    )
    up.other = after(up.other, qkv.mine)
    up.line()
    output.last_a, output.last_b = after((output.last_a, output.last_b), up.chip)
    output.near()
    gate.total = after(gate.total, output.odd)
    qkv.other = after(qkv.other, gate.total)
    qkv.plane()

    def rate(strength, fan):
        return strength / math.sqrt(fan * tokens_total)

    def exchange(*totals):
        totals = [flat(total) for total in totals]
        pieces = [jnp.stack([total[k] for total in totals]) for k in range(t_size)]
        return pieces[:1] + [dp_swap(pieces[k], k) for k in range(1, t_size)]

    down_out = update_rows(
        [(after(down.total, *qkv.sent), 0)], [(w_down, down_mom, down_ema)],
        [rate(1.5, hidden_units)],
    )
    out_sum.a, out_sum.b = after((out_sum.a, out_sum.b), *qkv.sent)
    out_sum.cross()
    qkv.a, qkv.b = after((qkv.a, qkv.b), down_out[0], *out_sum.crossed)
    qkv.cross()
    qkv.near()
    pieces = exchange(after(gate.total, qkv.odd), after(up.total, qkv.odd))
    output.line = after(output.line, qkv.odd)
    output.far()
    qkv.line = after(qkv.line, output.rest)
    qkv.far()
    out_sum.last_a, out_sum.last_b = after((out_sum.last_a, out_sum.last_b), qkv.rest)
    layer_out = layer_out_of(resid, out_sum.parts())
    pieces = after(pieces, qkv.rest)
    gate_out = update_units(spot, w_gate, gate_mom, gate_ema, pieces, 0, rate(0.6, width))
    up_out = update_units(spot, w_up, up_mom, up_ema, pieces, 1, rate(0.6, width))
    output_out = update_rows(
        [(after(x, qkv.rest), at) for x, at in output.final()],
        [(w_output, output_mom, output_ema)], [rate(5.0, heads_width)],
    )
    qkv.last = after(qkv.last, gate_out[0], layer_out)
    *qkv_out, left_over = update_rows(
        qkv.final(),
        [(w_query, query_mom, query_ema), (w_keyval, keyval_mom, keyval_ema)],
        [rate(0.6, width), rate(0.15, width)],
    )
    gains_out = update(gains, gains_mom, gains_ema, left_over[:, :2].T, rate(0.1, 1))
    return (
        layer_out,
        shared.astype(F32),
        input_grad,
        *gains_out,
        *qkv_out,
        *output_out,
        *gate_out,
        *up_out,
        *down_out,
    )


def solution(mesh):
    rows = P(BOTH, None)
    shards = shards_fast if dict(mesh.shape) == {"dp": 4, "fsdp": 8} else shards_any
    cols = P(None, BOTH)
    return jax.shard_map(
        shards,
        mesh=mesh,
        in_specs=(rows,) * 4 + (cols,) * 3 + (rows,) * 18,
        out_specs=(rows,) * 3 + (cols,) * 3 + (rows,) * 18,
        check_vma=False,
    )
```

```python
import functools
import math

import jax
import jax.numpy as jnp
from jax import lax
from jax.experimental import pallas as pl
from jax.experimental.pallas import tpu as pltpu
from jax.sharding import PartitionSpec as P

EPS = 1e-05
THETA = 10000.0
MOMENTUM = 0.9
AVERAGE = 0.75
NEG = -1e30
F32 = jnp.float32
BF16 = jnp.bfloat16
BOTH = ("dp", "fsdp")
COST = 40.0
VMEM_BYTES = 60 * 1024 * 1024


def positions_of(doc_ids):
    length = doc_ids.shape[-1]
    offsets = jnp.arange(length, dtype=jnp.int32)
    same = doc_ids[..., :, None] == doc_ids[..., None, :]
    starts = jnp.min(jnp.where(same, offsets, length), axis=-1)
    return offsets - starts


def rotation(positions, head_dim):
    half_dim = head_dim // 2
    inverse = THETA ** (-(jnp.arange(half_dim, dtype=F32) * 2.0) / head_dim)
    angles = positions.astype(F32)[..., None] * inverse
    cosine, sine = jnp.cos(angles), jnp.sin(angles)
    return (
        jnp.concatenate([cosine, cosine], axis=-1),
        jnp.concatenate([-sine, sine], axis=-1),
    )


def dot(left, right, contract, kind=F32):
    return lax.dot_general(
        left, right, ((contract[:1], contract[1:]), ((), ())), preferred_element_type=F32
    ).astype(kind)


def limits(flops=0, moved=0, steps=1):
    semantics = ("arbitrary",) * steps if steps else None
    return {
        "compiler_params": pltpu.CompilerParams(
            vmem_limit_bytes=VMEM_BYTES, dimension_semantics=semantics
        ),
        "cost_estimate": pl.CostEstimate(
            flops=int(flops * COST), bytes_accessed=int(moved * COST), transcendentals=0
        ),
    }


def swap_halves(values):
    return pltpu.roll(values, values.shape[-1] // 2, values.ndim - 1)


def set_bias(bias, ids_row, ids_col):
    shape = bias.shape
    later = lax.broadcasted_iota(jnp.int32, shape, 1) > lax.broadcasted_iota(jnp.int32, shape, 0)
    apart = (ids_col[0] != ids_row[0]) | later
    bias[...] = jnp.where(apart, NEG, 0.0)


def probabilities(query, keys, bias):
    scores = dot(query, keys, (1, 1)) + bias[...]
    weights = jnp.exp(scores - jnp.max(scores, axis=-1, keepdims=True))
    return weights / jnp.sum(weights, axis=-1, keepdims=True)


def attend_kernel(
    scale, q_raw, k_raw, v_raw, cosine, sine, ids_row, ids_col, queries, attended, shared, bias
):
    head_dim = q_raw.shape[1]

    @pl.when(pl.program_id(1) == 0)
    def _():
        set_bias(bias, ids_row, ids_col)
        key = k_raw[...]
        turned = key * cosine[...] + swap_halves(key) * sine[...]
        shared[:, :head_dim] = turned.astype(BF16)
        shared[:, head_dim:] = v_raw[...].astype(BF16)

    raw = q_raw[...]
    query = ((raw * cosine[...] + swap_halves(raw) * sine[...]) * scale).astype(BF16)
    queries[...] = query
    probs = probabilities(query, shared[:, :head_dim], bias).astype(BF16)
    attended[...] = dot(probs, shared[:, head_dim:], (1, 0), BF16)


def attend(raw, cosine, sine, doc_ids, head_count, head_dim):
    seq_count, length = doc_ids.shape
    rows = seq_count * length
    column = lambda which: pl.BlockSpec((length, head_dim), which)
    whole = pl.BlockSpec((length, head_dim), lambda s, h: (s, 0))
    return pl.pallas_call(
        functools.partial(attend_kernel, head_dim ** (-0.5)),
        grid=(seq_count, head_count),
        in_specs=[
            column(lambda s, h: (s, h)),
            column(lambda s, h: (s, head_count)),
            column(lambda s, h: (s, head_count + 1)),
            whole,
            whole,
            pl.BlockSpec((1, 1, length), lambda s, h: (s, 0, 0)),
            pl.BlockSpec((1, length, 1), lambda s, h: (s, 0, 0)),
        ],
        out_specs=[
            column(lambda s, h: (s, h)),
            column(lambda s, h: (s, h)),
            pl.BlockSpec((length, 2 * head_dim), lambda s, h: (s, 0)),
        ],
        out_shape=[
            jax.ShapeDtypeStruct((rows, head_count * head_dim), BF16),
            jax.ShapeDtypeStruct((rows, head_count * head_dim), BF16),
            jax.ShapeDtypeStruct((rows, 2 * head_dim), BF16),
        ],
        scratch_shapes=[pltpu.VMEM((length, length), F32)],
        name="attend",
        **limits(6 * rows * length * head_dim * head_count, 10 * rows * head_count * head_dim, 2),
    )(raw, raw, raw, cosine, sine, doc_ids[:, None, :], doc_ids[:, :, None])


def attend_back_kernel(
    scale, head_count, query_ref, grad_ref, shared, kv_next, cosine, sine, ids_row, ids_col,
    out, bias, grad_keys, grad_values,
):
    head_dim = query_ref.shape[1]
    head = pl.program_id(1)

    def turn_back(grads):
        return grads * cosine[...] - swap_halves(grads) * sine[...]

    @pl.when(head == 0)
    def _():
        set_bias(bias, ids_row, ids_col)
        grad_keys[...] = jnp.zeros_like(grad_keys)
        grad_values[...] = jnp.zeros_like(grad_values)

    @pl.when(head < head_count)
    def _():
        query, grad = query_ref[...], grad_ref[...]
        keys, values = shared[:, :head_dim], shared[:, head_dim:]
        probs = probabilities(query, keys, bias)
        grad_probs = dot(grad, values, (1, 1))
        inner = jnp.sum(probs * grad_probs, axis=-1, keepdims=True)
        grad_scores = (probs * (grad_probs - inner)).astype(BF16)
        grad_query = dot(grad_scores, keys, (1, 0), BF16).astype(F32) * scale
        out[...] = turn_back(grad_query).astype(BF16)
        grad_keys[...] += dot(grad_scores, query, (0, 0))
        grad_values[...] += dot(probs.astype(BF16), grad, (0, 0))

    @pl.when(head == head_count)
    def _():
        grads = (grad_keys[...] + kv_next[:, :head_dim].astype(F32)).astype(BF16).astype(F32)
        out[...] = turn_back(grads).astype(BF16)

    @pl.when(head == head_count + 1)
    def _():
        out[...] = (grad_values[...] + kv_next[:, head_dim:].astype(F32)).astype(BF16)

    @pl.when(head == head_count + 2)
    def _():
        out[...] = jnp.zeros_like(out)


def attend_back(queries, grads, shared, kv_next, cosine, sine, doc_ids, head_count, head_dim):
    seq_count, length = doc_ids.shape
    rows = seq_count * length
    block = (length, head_dim)
    own = pl.BlockSpec(block, lambda s, h: (s, jnp.minimum(h, head_count - 1)))
    whole = pl.BlockSpec(block, lambda s, h: (s, 0))
    pair = pl.BlockSpec((length, 2 * head_dim), lambda s, h: (s, 0))
    return pl.pallas_call(
        functools.partial(attend_back_kernel, head_dim ** (-0.5), head_count),
        grid=(seq_count, head_count + 3),
        in_specs=[
            own,
            own,
            pair,
            pair,
            whole,
            whole,
            pl.BlockSpec((1, 1, length), lambda s, h: (s, 0, 0)),
            pl.BlockSpec((1, length, 1), lambda s, h: (s, 0, 0)),
        ],
        out_specs=pl.BlockSpec(block, lambda s, h: (s, h)),
        out_shape=jax.ShapeDtypeStruct((rows, (head_count + 3) * head_dim), BF16),
        scratch_shapes=[
            pltpu.VMEM((length, length), F32),
            pltpu.VMEM(block, F32),
            pltpu.VMEM(block, F32),
        ],
        name="attend_back",
        **limits(14 * rows * length * head_dim * head_count, 8 * rows * head_count * head_dim, 2),
    )(queries, grads, shared, kv_next, cosine, sine, doc_ids[:, None, :], doc_ids[:, :, None])


def ffn_kernel(normed, cot, gate_w, up_w, down_w, hidden, grad_gate, grad_up, grad_normed, out):
    whole = lambda ref: lambda: ref[...]
    ffn_tile(
        normed, cot, whole(gate_w), whole(up_w), whole(down_w), hidden, grad_gate, grad_up,
        grad_normed, out,
    )


def ffn_tile(normed, cot, gate_w, up_w, down_w, hidden, grad_gate, grad_up, grad_normed, out):
    gate = dot(normed[...], gate_w(), (1, 0))
    up = dot(normed[...], up_w(), (1, 0))
    sigma = 1.0 / (1.0 + jnp.exp(-gate))
    activated = gate * sigma
    hidden[...] = (activated * up).astype(BF16)
    grad_hidden = dot(cot[...], down_w(), (1, 1), BF16).astype(F32)
    grad_up[...] = (grad_hidden * activated).astype(BF16)
    grad_gate[...] = (grad_hidden * up * (sigma * (1.0 + gate * (1.0 - sigma)))).astype(BF16)
    total = dot(grad_gate[...], gate_w(), (1, 1)) + dot(grad_up[...], up_w(), (1, 1))
    grad_normed[...] = total.astype(BF16)
    out[...] = dot(hidden[...], down_w(), (1, 0), BF16)


def ffn(normed, cot, gate_w, up_w, down_w):
    count, width = normed.shape
    units = gate_w.shape[1]
    tile = math.gcd(count, 256)
    token = pl.BlockSpec((tile, width), lambda t: (t, 0))
    inner = pl.BlockSpec((tile, units), lambda t: (t, 0))
    fixed = lambda shape: pl.BlockSpec(shape, lambda t: (0, 0), pipeline_mode=pl.Buffered(1))
    return pl.pallas_call(
        ffn_kernel,
        grid=(count // tile,),
        in_specs=[token, token, fixed(gate_w.shape), fixed(up_w.shape), fixed(down_w.shape)],
        out_specs=[inner, inner, inner, token, token],
        out_shape=[jax.ShapeDtypeStruct((count, units), BF16)] * 3
        + [jax.ShapeDtypeStruct((count, width), BF16)] * 2,
        name="ffn",
        **limits(12 * count * width * units, 6 * width * units + 8 * count * width),
    )(normed, cot, gate_w, up_w, down_w)


def dp_swap(value, k):
    size = lax.axis_size("dp")
    return lax.ppermute(value, "dp", [(i, i ^ k) for i in range(size)])


def z_swap(value, k):
    size = lax.axis_size("fsdp")
    return lax.ppermute(value, "fsdp", [(i, i ^ (2 * k)) for i in range(size)])


def core_swap(value):
    size = lax.axis_size("fsdp")
    return lax.ppermute(value, "fsdp", [(i, i ^ 1) for i in range(size)])


def pick(array, index, axis=0):
    return lax.dynamic_index_in_dim(array, index, axis, keepdims=False)


def put(buffer, piece, index, axis=0):
    return lax.dynamic_update_index_in_dim(buffer, piece, index, axis)


def plane_gather(value):
    size = lax.axis_size("dp")
    if size != 4:
        return [value] + [dp_swap(value, k) for k in range(1, size)]
    half = value.shape[0] // 2
    one, two = dp_swap(value, 1), dp_swap(value, 2)
    first = dp_swap(one[:half], 2)
    second = dp_swap(two[half:], 1)
    return [value, one, two, jnp.concatenate([first, second], axis=0)]


def plane_scatter(parts):
    size = len(parts)
    if size != 4:
        total = parts[0].astype(F32)
        for k in range(1, size):
            total = total + dp_swap(parts[k], k).astype(F32)
        return total
    half = parts[0].shape[0] // 2
    far_two = dp_swap(parts[3][:half], 1)
    far_one = dp_swap(parts[3][half:], 2)
    for_two = jnp.concatenate(
        [(parts[2][:half].astype(F32) + far_two.astype(F32)).astype(BF16), parts[2][half:]], axis=0
    )
    for_one = jnp.concatenate(
        [parts[1][:half], (parts[1][half:].astype(F32) + far_one.astype(F32)).astype(BF16)], axis=0
    )
    return (
        parts[0].astype(F32)
        + dp_swap(for_one, 1).astype(F32)
        + dp_swap(for_two, 2).astype(F32)
    )


def line_scatter(terms):
    count = terms.shape[0]
    size = lax.axis_size("fsdp")
    z = lax.axis_index("fsdp") // 2
    right = left = None
    for step in range(count - 1):
        out = pick(terms, jnp.clip(count - 1 - step + z, 0, count - 1))
        if right is not None:
            out = (out.astype(F32) + right.astype(F32)).astype(BF16)
        right = lax.ppermute(
            out, "fsdp", [(i, i + 2) for i in range(size - 2) if i // 2 <= step]
        )
        out = pick(terms, jnp.clip(z - (count - 1 - step), 0, count - 1))
        if left is not None:
            out = (out.astype(F32) + left.astype(F32)).astype(BF16)
        left = lax.ppermute(
            out, "fsdp", [(i, i - 2) for i in range(2, size) if count - 1 - i // 2 <= step]
        )
    return pick(terms, z).astype(F32) + right.astype(F32) + left.astype(F32)


def gather_rows(block):
    t_size, f_size = lax.axis_size("dp"), lax.axis_size("fsdp")
    z_size = f_size // 2
    dp, fs = lax.axis_index("dp"), lax.axis_index("fsdp")
    z, core = fs // 2, fs % 2
    rows, cols = block.shape
    line = jnp.zeros((z_size, rows, cols), block.dtype)
    line = put(line, block, z)
    for k in range(1, z_size):
        line = put(line, z_swap(block, k), z ^ k)
    plane = jnp.zeros((t_size, z_size, rows, cols), block.dtype)
    for k, piece in enumerate(plane_gather(line)):
        plane = put(plane, piece, dp ^ k)
    whole = jnp.zeros((t_size, z_size, 2, rows, cols), block.dtype)
    whole = put(whole, plane, core, 2)
    whole = put(whole, core_swap(plane), 1 - core, 2)
    return whole.reshape(t_size * f_size * rows, cols)


def core_sum(mine, other):
    return (mine.astype(F32) + core_swap(other).astype(F32)).astype(BF16)


def scatter_rows(grads):
    t_size, f_size = lax.axis_size("dp"), lax.axis_size("fsdp")
    z_size = f_size // 2
    dp, fs = lax.axis_index("dp"), lax.axis_index("fsdp")
    core = fs % 2
    rows = grads.shape[0] // (t_size * f_size)
    split = grads.reshape(t_size, z_size, 2, rows, grads.shape[1])
    chip = core_sum(pick(split, core, 2), pick(split, 1 - core, 2))
    line = plane_scatter([pick(chip, dp ^ k) for k in range(t_size)])
    return line_scatter(line.astype(BF16))


def scatter_fsdp(split, axis):
    f_size = lax.axis_size("fsdp")
    core = lax.axis_index("fsdp") % 2
    shape = split.shape
    pairs = split.reshape(shape[:axis] + (f_size // 2, 2) + shape[axis + 1 :])
    chip = core_sum(pick(pairs, core, axis + 1), pick(pairs, 1 - core, axis + 1))
    return line_scatter(jnp.moveaxis(chip, axis, 0))


def norm_back(grad_normed, scaled, inv_rms, gain_full):
    grad_scaled = grad_normed * gain_full
    grad_gain = jnp.sum(grad_normed * scaled, axis=0)
    grad_in = inv_rms * (
        grad_scaled - scaled * jnp.mean(grad_scaled * scaled, axis=-1, keepdims=True)
    )
    return (grad_gain, grad_in)


def update(weight, moment, average, grad, rate):
    moment_new = MOMENTUM * moment + grad
    weight_new = weight - rate * (grad + MOMENTUM * moment_new)
    average_new = AVERAGE * average + (1.0 - AVERAGE) * weight_new
    return (moment_new, weight_new, average_new)


LINE_ORDER = (0, 2, 1, 3)
PIECES = ((0, LINE_ORDER), (1, LINE_ORDER), (2, LINE_ORDER), (3, (0, 2)), (3, (1, 3)))
SMEM = pl.BlockSpec(memory_space=pltpu.SMEM)
VMEM = pl.BlockSpec(memory_space=pltpu.VMEM)
ANY = pl.BlockSpec(memory_space=pl.ANY)


def place():
    fs = lax.axis_index("fsdp")
    return jnp.stack([lax.axis_index("dp"), fs // 2, fs % 2]).astype(jnp.int32)


def after(value, *others):
    leaves, tree = jax.tree.flatten(value)
    kept = lax.optimization_barrier((*leaves, *others))[: len(leaves)]
    return jax.tree.unflatten(tree, kept)


SPLIT = 96


def slices_kernel(spot, gate, up, down, *outs):
    outs, packed = outs[:-1], outs[-1]
    units = packed.shape[1]
    for k, out in enumerate(outs):
        at = pl.ds(pl.multiple_of((spot[0] ^ k) * units, units), units)
        out[0] = gate[:, at].astype(BF16)
        out[1] = up[:, at].astype(BF16)
    rows, width = down.shape
    rest = width - units
    packed[:rows] = down[:, :units].astype(BF16)
    packed[rows:] = jnp.zeros((SPLIT, units), BF16)
    packed[rows : rows + SPLIT, :rest] = down[:SPLIT, units:].astype(BF16)
    packed[rows : 2 * rows - SPLIT, rest : 2 * rest] = down[SPLIT:, units:].astype(BF16)


def slices(spot, gate, up, down, count):
    rows, units = gate.shape[0], gate.shape[1] // count
    return pl.pallas_call(
        slices_kernel,
        in_specs=[SMEM, VMEM, VMEM, VMEM],
        out_specs=[VMEM] * (count + 1),
        out_shape=[jax.ShapeDtypeStruct((2, rows, units), BF16)] * count
        + [jax.ShapeDtypeStruct((down.shape[0] + SPLIT, units), BF16)],
        name="slices",
        **limits(0, 12 * gate.size, 0),
    )(spot, gate, up, down)


def gather_line(block):
    two, one = z_swap(block, 2), z_swap(block, 1)
    return jnp.stack([block, two, one, z_swap(two, 1)])


def plane_near(value):
    return dp_swap(value, 1), dp_swap(value, 2)


def plane_far(one, two):
    first, second = cut(one, 0), cut(two, 1)
    return dp_swap(first, 2), dp_swap(second, 1)


def cut_kernel(whole, out):
    out[...] = whole[...]


def cut(whole, index):
    half = whole.shape[0] // 2
    rest = (0,) * (whole.ndim - 1)
    steps = 2 if whole.ndim > 2 else half // 96
    block = (half // steps,) + whole.shape[1:]
    return pl.pallas_call(
        cut_kernel,
        grid=(steps,),
        in_specs=[pl.BlockSpec(block, lambda g: (index * steps + g,) + rest)],
        out_specs=pl.BlockSpec(block, lambda g: (g,) + rest),
        out_shape=jax.ShapeDtypeStruct((half,) + whole.shape[1:], whole.dtype),
        name="cut",
        **limits(0, 2 * whole.size),
    )(whole)


def fetch_rows(spot, pieces, held, sems):
    z, core = spot[1], spot[2]
    copies = [[] for _ in range(4)]
    for side in range(2):
        for (k, line), piece in zip(PIECES, pieces[side * len(PIECES) :]):
            for at, j in enumerate(line):
                slot = held.at[k, z ^ j, core ^ side]
                sem = sems.at[k, 2 * j + side]
                copies[k].append(pltpu.make_async_copy(piece.at[at], slot, sem))
    for some in copies:
        for copy in some:
            copy.start()
    return copies


def blocks_of(spot, copies, held):
    count, z_size, cores, rows, cols = held.shape
    size = z_size * cores * rows
    for k in range(count):
        for copy in copies[k]:
            copy.wait()
        at = pl.ds(pl.multiple_of((spot[0] ^ k) * size, size), size)
        yield k, at, held[k].reshape(size, cols)


def held_shapes(pieces):
    rows, cols = pieces[0].shape[1:]
    return [pltpu.VMEM((4, 4, 2, rows, cols), BF16), pltpu.SemaphoreType.DMA((4, 8))]


def inverse_rms(values):
    return lax.rsqrt(jnp.mean(values * values, axis=-1, keepdims=True) + EPS)


def enter_kernel(spot, tokens, *refs):
    pieces, (raw, normed, gains, held, sems) = refs[:-5], refs[-5:]
    copies = fetch_rows(spot, pieces, held, sems)
    values = tokens[...].astype(F32)
    inv_rms = inverse_rms(values)
    cols = raw.shape[1]
    for k, at, weight in blocks_of(spot, copies, held):
        turned = weight[:, cols:].astype(F32).T
        gains[:, at] = turned[: gains.shape[0]]
        scaled = tokens[:, at].astype(F32) * inv_rms
        normed[:, at] = (scaled * turned[:1]).astype(BF16)
        found = dot(normed[:, at], weight[:, :cols], (1, 0))
        raw[...] = found if k == 0 else raw[...] + found


def enter(spot, tokens, pieces):
    count, width = tokens.shape
    cols = pieces[0].shape[2] - 128
    return pl.pallas_call(
        enter_kernel,
        in_specs=[SMEM, VMEM] + [ANY] * len(pieces),
        out_specs=[VMEM] * 3,
        out_shape=[
            jax.ShapeDtypeStruct((count, cols), F32),
            jax.ShapeDtypeStruct((count, width), BF16),
            jax.ShapeDtypeStruct((8, width), F32),
        ],
        scratch_shapes=held_shapes(pieces),
        name="enter",
        **limits(2 * count * width * cols, 2 * width * cols, 0),
    )(spot, tokens, *pieces)


def leave_kernel(spot, attended, tokens, gains, *refs):
    pieces, (resid, normed, held, sems) = refs[:-4], refs[-4:]
    copies = fetch_rows(spot, pieces, held, sems)
    resid[...] = tokens[...].astype(F32)
    for _, at, weight in blocks_of(spot, copies, held):
        resid[...] += dot(attended[:, at], weight, (1, 0))
    values = resid[...]
    normed[...] = (values * inverse_rms(values) * gains[1:2]).astype(BF16)


def leave(spot, attended, tokens, gains, pieces):
    count, width = tokens.shape
    return pl.pallas_call(
        leave_kernel,
        in_specs=[SMEM] + [VMEM] * 3 + [ANY] * len(pieces),
        out_specs=[VMEM] * 2,
        out_shape=[
            jax.ShapeDtypeStruct((count, width), F32),
            jax.ShapeDtypeStruct((count, width), BF16),
        ],
        scratch_shapes=held_shapes(pieces),
        name="leave",
        **limits(2 * count * width * width, 2 * width * width, 0),
    )(spot, attended, tokens, gains, *pieces)


def leave_back_kernel(spot, grads, *refs):
    pieces, (out, held, sems) = refs[:-3], refs[-3:]
    copies = fetch_rows(spot, pieces, held, sems)
    for _, at, weight in blocks_of(spot, copies, held):
        out[:, at] = dot(grads[...], weight, (1, 1), BF16)


def leave_back(spot, grads, pieces):
    count, width = grads.shape
    return pl.pallas_call(
        leave_back_kernel,
        in_specs=[SMEM, VMEM] + [ANY] * len(pieces),
        out_specs=VMEM,
        out_shape=jax.ShapeDtypeStruct((count, width), BF16),
        scratch_shapes=held_shapes(pieces),
        name="leave_back",
        **limits(2 * count * width * width, 2 * width * width, 0),
    )(spot, grads, *pieces)


def enter_back_kernel(spot, grads, tokens, gains, grad_resid, *refs):
    pieces, (out, grad_gain, held, sems) = refs[:-4], refs[-4:]
    copies = fetch_rows(spot, pieces, held, sems)
    for _, at, weight in blocks_of(spot, copies, held):
        out[:, at] = dot(grads[...], weight, (1, 1))
    values = tokens[...].astype(F32)
    inv_rms = inverse_rms(values)
    total, through = norm_back(out[...], values * inv_rms, inv_rms, gains[:1])
    grad_gain[...] = jnp.broadcast_to(total[None], grad_gain.shape)
    out[...] = grad_resid[...] + through


def enter_back(spot, grads, tokens, gains, grad_resid, pieces):
    count, width = tokens.shape
    return pl.pallas_call(
        enter_back_kernel,
        in_specs=[SMEM] + [VMEM] * 4 + [ANY] * len(pieces),
        out_specs=[VMEM] * 2,
        out_shape=[
            jax.ShapeDtypeStruct((count, width), F32),
            jax.ShapeDtypeStruct((8, width), F32),
        ],
        scratch_shapes=held_shapes(pieces),
        name="enter_back",
        **limits(2 * count * width * width, 2 * width * width, 0),
    )(spot, grads, tokens, gains, grad_resid, *pieces)


TOKEN_ORDER = (1, 3, 2, 0)


def ffn_all_kernel(spot, *refs):
    ins, held_in = (refs[:5], refs[5:10]), refs[10]
    wholes, (hidden, grad_gate, grad_up, sums, out) = refs[11:13], refs[13:18]
    sent_a, sent_b, out_a, out_b = refs[18:22]
    gate_w, up_w, down_w, tiles, grad_tile, out_tile, sems, in_sems, out_sems = refs[22:]
    count, f_size, rows, units = gate_w.shape
    step = pl.program_id(0)
    first = step == 0
    size = tiles.shape[2]
    half = size // 2
    copies = [
        [
            pltpu.make_async_copy(
                held_in.at[:, pl.ds((2 * k + which) * rows, rows)], buffer.at[spot[0] ^ k],
                sems.at[which, k],
            )
            for k in range(count)
        ]
        for which, buffer in enumerate((gate_w, up_w))
    ]
    above, (low, width) = 2 * count * rows, down_w.shape[1:]
    rest = width - units
    copies.append(
        [
            pltpu.make_async_copy(
                held_in.at[:, pl.ds(above, low)], down_w.at[:, :, pl.ds(0, units)], sems.at[2, 0]
            ),
            pltpu.make_async_copy(
                held_in.at[:, pl.ds(above + low, SPLIT), pl.ds(0, rest)],
                down_w.at[:, pl.ds(0, SPLIT), pl.ds(units, rest)],
                sems.at[2, 1],
            ),
            pltpu.make_async_copy(
                held_in.at[:, pl.ds(above + low, low - SPLIT), pl.ds(rest, rest)],
                down_w.at[:, pl.ds(SPLIT, low - SPLIT), pl.ds(units, rest)],
                sems.at[2, 2],
            ),
        ]
    )

    def brought(at):
        k, some = TOKEN_ORDER[at], []
        for which, pieces in enumerate(ins):
            slot = tiles.at[at % 2, which]
            parts = pieces[k : k + 1] if k < 3 else pieces[3:]
            for i, piece in enumerate(parts):
                target = slot.at[pl.ds(i * half, half)] if k == 3 else slot
                some.append(pltpu.make_async_copy(piece, target, in_sems.at[at % 2, which, i]))
        return some

    def kept(at):
        return [
            pltpu.make_async_copy(
                tiles.at[at % 2, which], whole.at[pl.ds(at * size, size)], out_sems.at[at % 2, which]
            )
            for which, whole in enumerate(wholes)
        ]

    for at in range(4):

        @pl.when(step == at)
        def _():
            if at == 0:
                for copy in brought(0):
                    copy.start()
                for held in copies:
                    for copy in held:
                        copy.start()
            for copy in brought(at):
                copy.wait()
            if at > 0:
                for copy in kept(at - 1):
                    copy.wait()
            for copy in kept(at):
                copy.start()
            if at < 3:
                for copy in brought(at + 1):
                    copy.start()

    normed, cot = tiles.at[step % 2, 0], tiles.at[step % 2, 1]

    def weight(which, buffer):
        waited = []

        def read():
            if not waited:
                waited.append(True)

                @pl.when(first)
                def _():
                    for copy in copies[which]:
                        copy.wait()

            return buffer[...].reshape(-1, buffer.shape[-1])

        return read

    ffn_tile(
        normed, cot, weight(0, gate_w), weight(1, up_w), weight(2, down_w),
        hidden, grad_gate, grad_up, grad_tile, out_tile,
    )
    for i in range(2):
        sums[i, 0] = grad_tile[i * half : (i + 1) * half]
        out[i, 0] = out_tile[i * half : (i + 1) * half]

    @pl.when(step < 2)
    def _():
        sent_a[0] = grad_tile[:half]
        out_a[0] = out_tile[:half]

    @pl.when((step > 0) & (step < 3))
    def _():
        sent_b[0] = grad_tile[half:]
        out_b[0] = out_tile[half:]

    @pl.when(step == 3)
    def _():
        for copy in kept(3):
            copy.wait()


def ffn_all(spot, normed, cot, held_in, t_size, low):
    count, width = normed[0].shape
    half = count // 2
    f_size, above, units = held_in.shape
    rows = (above - low - SPLIT) // (2 * t_size)
    inner = pl.BlockSpec((count, units), lambda t: (t, 0))
    sums = pl.BlockSpec((2, 1, half, width), lambda t: (0, t, 0, 0))
    sent = lambda low: pl.BlockSpec(
        (1, half, width), lambda t: (jnp.clip(t - low, 0, 1), 0, 0)
    )
    weights = pltpu.VMEM((t_size, f_size, rows, units), BF16)
    total = 4 * count
    return pl.pallas_call(
        ffn_all_kernel,
        grid=(4,),
        in_specs=[SMEM] + [ANY] * 11,
        out_specs=[ANY, ANY, inner, inner, inner, sums, sums]
        + [sent(0), sent(1)] * 2,
        scratch_shapes=[
            weights,
            weights,
            pltpu.VMEM((f_size, low, width), BF16),
            pltpu.VMEM((2, 2, count, width), BF16),
            pltpu.VMEM((count, width), BF16),
            pltpu.VMEM((count, width), BF16),
            pltpu.SemaphoreType.DMA((3, t_size)),
            pltpu.SemaphoreType.DMA((2, 2, 2)),
            pltpu.SemaphoreType.DMA((2, 2)),
        ],
        out_shape=[jax.ShapeDtypeStruct((total, width), BF16)] * 2
        + [jax.ShapeDtypeStruct((total, units), BF16)] * 3
        + [jax.ShapeDtypeStruct((2, 4, half, width), BF16)] * 2
        + [jax.ShapeDtypeStruct((2, half, width), BF16)] * 4,
        name="ffn_all",
        **limits(12 * total * width * units, 6 * width * units + 8 * total * width),
    )(spot, *normed, *cot, held_in)


class TokenSum:
    def __init__(self, terms, sent=None):
        self.own = terms
        self.sent = sent or add([[(terms, 0)], [(terms, 5)]], 2)
        self.a, self.b = dp_swap(self.sent[0], 1), dp_swap(self.sent[1], 2)

    def cross(self):
        self.crossed = add([[(self.own, 2), (self.a, 1)], [(self.own, 4), (self.b, 0)]], 1)
        self.last_a, self.last_b = dp_swap(self.crossed[0], 2), dp_swap(self.crossed[1], 1)

    def parts(self):
        return [
            [(flat(self.own), 3), (self.a, 0), (self.last_a, 0)],
            [(flat(self.own), 7), (self.b, 1), (self.last_b, 0)],
        ]


def add_kernel(counts, *refs):
    outs = refs[len(refs) - len(counts) :]
    at = 0
    for count, out in zip(counts, outs):
        total = refs[at][...].astype(F32)
        for ref in refs[at + 1 : at + count]:
            total = total + ref[...].astype(F32)
        out[...] = total.astype(out.dtype)
        at += count


def flat(array):
    return array.reshape((-1,) + array.shape[-2:])


def add(jobs, count, group=1):
    operands = [flat(array) for job in jobs for array, _ in job]
    starts = [start for job in jobs for _, start in job]
    block = (group,) + operands[0].shape[1:]
    spec = lambda start: pl.BlockSpec(block, lambda g: (g + start // group, 0, 0))
    return pl.pallas_call(
        functools.partial(add_kernel, [len(job) for job in jobs]),
        grid=(count // group,),
        in_specs=[spec(start) for start in starts],
        out_specs=[spec(0)] * len(jobs),
        out_shape=[jax.ShapeDtypeStruct((count,) + block[1:], BF16)] * len(jobs),
        name="add",
        **limits(0, 2 * (len(starts) + len(jobs)) * count * block[1] * block[2]),
    )(*operands)


def turns(step):
    return jnp.minimum(step, 2), jnp.maximum(step - 3, 0)


def half_specs(parts, rows):
    specs = []
    for side, terms in enumerate(parts):
        for array, start in terms:
            shape = (1, rows, array.shape[-1])
            specs.append(
                pl.BlockSpec(shape, lambda t, side=side, start=start: (start, turns(t)[side], 0))
            )
    return specs


def half_total(refs, side):
    some = refs[side * 3 : side * 3 + 3]
    return some[0][0].astype(F32) + some[1][0].astype(F32) + some[2][0].astype(F32)


def branch_kernel(resid, cot, gains, *refs):
    terms, (grad_resid, grad_branch, grad_gain) = refs[:6], refs[6:]
    step = pl.program_id(0)

    def finish(grads):
        inv_rms = inverse_rms(resid[...])
        total, through = norm_back(grads, resid[...] * inv_rms, inv_rms, gains[1:2])
        sums = jnp.broadcast_to(total[None], grad_gain.shape)

        @pl.when(step == 0)
        def _():
            grad_gain[...] = sums

        @pl.when(step > 0)
        def _():
            grad_gain[...] += sums

        grads = cot[...].astype(F32) + through
        grad_resid[...] = grads
        grad_branch[...] = grads.astype(BF16)

    for side in range(2):

        @pl.when(step // 3 == side)
        def _():
            finish(half_total(terms, side))


def branch(resid, cot, gains, parts):
    count, width = resid.shape
    rows = count // 6
    token = pl.BlockSpec((rows, width), lambda t: (t, 0))
    fixed = pl.BlockSpec((8, width), lambda t: (0, 0))
    return pl.pallas_call(
        branch_kernel,
        grid=(6,),
        in_specs=[token, token, fixed] + half_specs(parts, rows),
        out_specs=[token, token, fixed],
        out_shape=[
            jax.ShapeDtypeStruct((count, width), F32),
            jax.ShapeDtypeStruct((count, width), BF16),
            jax.ShapeDtypeStruct((8, width), F32),
        ],
        name="branch",
        **limits(0, 18 * count * width),
    )(resid, cot, gains, *[array for terms in parts for array, _ in terms])


def layer_out_kernel(resid, *refs):
    terms, out = refs[:6], refs[6]
    for side in range(2):

        @pl.when(pl.program_id(0) // 3 == side)
        def _():
            out[...] = resid[...] + half_total(terms, side)


def layer_out_of(resid, parts):
    count, width = resid.shape
    rows = count // 6
    token = pl.BlockSpec((rows, width), lambda t: (t, 0))
    return pl.pallas_call(
        layer_out_kernel,
        grid=(6,),
        in_specs=[token] + half_specs(parts, rows),
        out_specs=token,
        out_shape=jax.ShapeDtypeStruct((count, width), F32),
        name="layer_out",
        **limits(0, 14 * count * width),
    )(resid, *[array for terms in parts for array, _ in terms])


def row_grads_kernel(spot, left, right, *refs):
    gains = refs[:-3]
    mine, other, held = refs[-3:]
    count, _, rows, cols = held.shape
    found = dot(left[...], right[...], (0, 0), BF16)
    if gains:
        shape = (128, left.shape[1])
        which = lax.broadcasted_iota(jnp.int32, shape, 0)
        one, two = gains[0][:1], gains[1][:1]
        extra = jnp.where(which == 0, one, jnp.where(which == 1, two, 0.0)).T.astype(BF16)
    for i in range(count):
        for core in range(2):
            at = (2 * i + core) * rows
            held[i, core, :, : found.shape[1]] = found[at : at + rows]
            if gains:
                held[i, core, :, found.shape[1] :] = extra[at : at + rows]
    z, core = spot[1], spot[2]
    for half in range(2):
        for at in range(2):
            mine[half, 0, at] = held[z ^ (2 * at + half), core]
            other[half, 0, at] = held[z ^ (2 * at + half), 1 - core]


def row_grads(spot, left, right, right_cols, gains=()):
    count, width = left.shape
    rows = width // 32
    cols = right_cols + (128 if gains else 0)
    turn = lambda k, spot: spot[0] ^ k ^ (k >> 1)
    out = pl.BlockSpec((2, 1, 2, rows, cols), lambda k, spot: (0, k, 0, 0, 0))
    gain = pl.BlockSpec((8, width // 4), lambda k, spot: (0, turn(k, spot)))
    return pl.pallas_call(
        row_grads_kernel,
        grid_spec=pltpu.PrefetchScalarGridSpec(
            num_scalar_prefetch=1,
            grid=(4,),
            in_specs=[
                pl.BlockSpec((count, width // 4), lambda k, spot: (0, turn(k, spot))),
                pl.BlockSpec((count, right_cols), lambda k, spot: (0, 0)),
            ]
            + [gain] * len(gains),
            out_specs=[out, out],
            scratch_shapes=[pltpu.VMEM((4, 2, rows, cols), BF16)],
        ),
        out_shape=[jax.ShapeDtypeStruct((2, 4, 2, rows, cols), BF16)] * 2,
        name="row_grads",
        **limits(2 * count * width * cols, 2 * width * cols + 2 * count * (width + cols)),
    )(spot, left, right, *gains)


class RowSum:
    def __init__(self, mine, other):
        self.mine, self.other = mine, core_swap(other)

    def plane(self):
        pair = lambda start: [(self.mine, start), (self.other, start)]
        a, b = self.sent = add([pair(2), pair(12)], 4, 2)
        self.a, self.b = dp_swap(a, 1), dp_swap(b, 2)

    def cross(self):
        a, b = self.crossed = add(
            [
                [(self.mine, 6), (self.other, 6), (self.a, 2)],
                [(self.mine, 10), (self.other, 10), (self.b, 0)],
            ],
            2,
        )
        self.last_a, self.last_b = dp_swap(a, 2), dp_swap(b, 1)

    def near(self):
        terms = [(self.mine, 8), (self.other, 8), (self.b, 2), (self.last_b, 0)]
        self.odd = add([terms], 2)[0]
        self.line = z_swap(self.odd, 1)

    def terms(self, at):
        return [(x, at) for x in (self.mine, self.other, self.a, self.last_a, self.line)]

    def far(self):
        self.rest = add([self.terms(1)], 1)[0]
        self.last = z_swap(self.rest, 2)

    def final(self):
        return self.terms(0) + [(self.last, 0)]


class LineSum:
    def __init__(self, mine, other):
        self.mine, self.other = mine, core_swap(other)

    def line(self):
        blocks = self.mine.shape[0]
        count = flat(self.mine).shape[0]
        self.chip = add([[(self.mine, 0), (self.other, 0)]], count, count // blocks)[0]
        size = lax.axis_size("fsdp")
        groups = [list(range(core, size, 2)) for core in range(2)]
        self.total = lax.psum_scatter(
            self.chip, "fsdp", scatter_dimension=0, axis_index_groups=groups, tiled=True
        )


def chunk_dot(lefts, rights):
    found = dot(lefts[0][...], rights[0][...], (0, 0))
    for left, right in zip(lefts[1:], rights[1:]):
        found = found + dot(left[...], right[...], (0, 0))
    return found.astype(BF16)


def place_line(spot, found, held, mine, other):
    count, _, rows, _ = held.shape
    core = spot[2]
    for i in range(count):
        for side in range(2):
            at = (2 * i + side) * rows
            held[i, side] = found[at : at + rows]
    for at in range(count):
        mine[at] = held[at, core].reshape(mine.shape[1:])
        other[at] = held[at, 1 - core].reshape(other.shape[1:])


def line_grads_kernel(spot, *refs):
    mine, other, held = refs[-3:]
    chunks = (len(refs) - 3) // 2
    found = chunk_dot(refs[:chunks], refs[chunks : 2 * chunks])
    place_line(spot, found, held, mine, other)


def unit_grads(spot, lefts, rights):
    count, width = lefts[0].shape
    units, rows = rights[0].shape[1], width // 32
    out = pl.BlockSpec((4, 1, rows, units), lambda k, spot: (0, k, 0, 0))
    left = pl.BlockSpec((count, width // 4), lambda k, spot: (0, spot[0] ^ k))
    right = pl.BlockSpec((count, units), lambda k, spot: (0, 0), pipeline_mode=pl.Buffered(1))
    total = count * len(lefts)
    return pl.pallas_call(
        line_grads_kernel,
        grid_spec=pltpu.PrefetchScalarGridSpec(
            num_scalar_prefetch=1,
            grid=(4,),
            in_specs=[left] * len(lefts) + [right] * len(rights),
            out_specs=[out, out],
            scratch_shapes=[pltpu.VMEM((4, 2, rows, units), BF16)],
        ),
        out_shape=[jax.ShapeDtypeStruct((4, 4, rows, units), BF16)] * 2,
        name="unit_grads",
        **limits(2 * total * width * units, 2 * width * units + 2 * total * (width + units)),
    )(spot, *lefts, *rights)


def down_grads(spot, lefts, rights):
    count, units = lefts[0].shape
    width = rights[0].shape[1]
    rows, tile = units // 8, width // 4
    out = pl.BlockSpec((4, rows, tile), lambda n, spot: (0, 0, n))
    left = pl.BlockSpec((count, units), lambda n, spot: (0, 0), pipeline_mode=pl.Buffered(1))
    right = pl.BlockSpec((count, tile), lambda n, spot: (0, n))
    total = count * len(lefts)
    return pl.pallas_call(
        line_grads_kernel,
        grid_spec=pltpu.PrefetchScalarGridSpec(
            num_scalar_prefetch=1,
            grid=(4,),
            in_specs=[left] * len(lefts) + [right] * len(rights),
            out_specs=[out, out],
            scratch_shapes=[pltpu.VMEM((4, 2, rows, tile), BF16)],
        ),
        out_shape=[jax.ShapeDtypeStruct((4, rows, width), BF16)] * 2,
        name="down_grads",
        **limits(2 * total * width * units, 2 * width * units + 2 * total * (width + units)),
    )(spot, *lefts, *rights)


def sum_of(refs):
    total = refs[0][0].astype(F32)
    for ref in refs[1:]:
        total = total + ref[0].astype(F32)
    return total


def update_rows_kernel(rates, count, *refs):
    terms, rest = refs[:count], refs[count:]
    held = 3 * len(rates)
    ins, outs = rest[:held], rest[held:]
    grads = sum_of(terms)
    at = 0
    for i, rate in enumerate(rates):
        own = ins[3 * i : 3 * i + 3]
        cols = own[0].shape[1]
        piece = grads[:, at : at + cols]
        at += cols
        results = update(*[ref[...] for ref in own], piece, rate)
        for out, result in zip(outs[3 * i :], results):
            out[...] = result
    if at < grads.shape[1]:
        outs[-1][...] = grads[:, at:]


def update_rows(terms, weights, rates):
    operands = [flat(array) for array, _ in terms]
    block = (1,) + operands[0].shape[1:]
    left = block[2] - sum(w[0].shape[1] for w in weights)
    arrays = [array for some in weights for array in some]
    shapes = [jax.ShapeDtypeStruct(array.shape, F32) for array in arrays]
    if left:
        shapes.append(jax.ShapeDtypeStruct((block[1], left), F32))
    whole = lambda shape: pl.BlockSpec(shape, lambda g: (0, 0))
    return pl.pallas_call(
        functools.partial(update_rows_kernel, rates, len(terms)),
        grid=(1,),
        in_specs=[pl.BlockSpec(block, lambda g, start=start: (start, 0, 0)) for _, start in terms]
        + [whole(array.shape) for array in arrays],
        out_specs=[whole(shape.shape) for shape in shapes],
        out_shape=shapes,
        name="update_rows",
        **limits(0, 32 * arrays[0].size),
    )(*operands, *arrays)


def update_units_kernel(rate, spot, weight, moment, average, *refs):
    pieces, outs = refs[:4], refs[4:]
    units = pieces[0].shape[-1]
    for k in range(4):
        grads = pieces[k][0].astype(F32)
        at = pl.ds(pl.multiple_of((spot[0] ^ k) * units, units), units)
        results = update(weight[:, at], moment[:, at], average[:, at], grads, rate)
        for out, result in zip(outs, results):
            out[:, at] = result


def update_units(spot, weight, moment, average, pieces, which, rate):
    block = (1,) + pieces[0].shape[1:]
    first = pl.BlockSpec(block, lambda g: (which, 0, 0))
    whole = pl.BlockSpec(weight.shape, lambda g: (0, 0))
    return pl.pallas_call(
        functools.partial(update_units_kernel, rate),
        grid=(1,),
        in_specs=[SMEM] + [whole] * 3 + [first] * 4,
        out_specs=[whole] * 3,
        out_shape=[jax.ShapeDtypeStruct(weight.shape, F32)] * 3,
        name="update_units",
        **limits(0, 32 * weight.size),
    )(spot, weight, moment, average, *pieces)


def shards_any(
    tokens_in,
    out_grad,
    kv_grad_next,
    doc_ids,
    gains,
    gains_mom,
    gains_ema,
    w_query,
    query_mom,
    query_ema,
    w_keyval,
    keyval_mom,
    keyval_ema,
    w_output,
    output_mom,
    output_ema,
    w_gate,
    gate_mom,
    gate_ema,
    w_up,
    up_mom,
    up_ema,
    w_down,
    down_mom,
    down_ema,
):
    t_size, f_size = lax.axis_size("dp"), lax.axis_size("fsdp")
    dp = lax.axis_index("dp")
    seq_count, length = doc_ids.shape
    width = tokens_in.shape[1]
    head_dim = w_keyval.shape[1] // 2
    head_count = w_query.shape[1] // head_dim
    hidden_units = w_gate.shape[1]
    rows = seq_count * length
    heads_width = head_count * head_dim
    tokens_total = rows * t_size * f_size
    own_rows = w_query.shape[0]
    slice_units = hidden_units // t_size

    gain_cols = jnp.zeros((own_rows, 128), BF16).at[:, :2].set(gains.astype(BF16).T)
    qkv_block = jnp.concatenate([w_query.astype(BF16), w_keyval.astype(BF16), gain_cols], axis=1)

    def to_slices(weight):
        split = weight.astype(BF16).reshape(own_rows, t_size, slice_units)
        held = jnp.zeros((t_size, own_rows, slice_units), BF16)
        held = put(held, pick(split, dp, 1), dp)
        for k in range(1, t_size):
            held = put(held, dp_swap(pick(split, dp ^ k, 1), k), dp ^ k)
        whole = lax.all_gather(held, "fsdp", axis=0)
        return jnp.swapaxes(whole, 0, 1).reshape(width, slice_units)

    qkv_full = gather_rows(qkv_block)
    output_full = gather_rows(w_output.astype(BF16))
    gate_slice = to_slices(w_gate)
    up_slice = to_slices(w_up)
    gain_rows = qkv_full[:, -128:]
    down_block = w_down.astype(BF16)
    down_slice = lax.all_gather(down_block, "fsdp", axis=0, tiled=True)
    cot_all = jnp.concatenate(plane_gather(out_grad), axis=0)

    inputs = tokens_in.astype(F32)
    inv_rms = lax.rsqrt(jnp.mean(inputs * inputs, axis=-1, keepdims=True) + EPS)
    scaled = inputs * inv_rms
    gains_full = gain_rows[:, :2].astype(F32).T
    gain_attn, gain_ffn = gains_full[0], gains_full[1]
    normed = (scaled * gain_attn).astype(BF16)
    raw = dot(normed, qkv_full, (1, 0))
    cosine, sine = rotation(positions_of(doc_ids).reshape(rows), head_dim)
    queries, attended, shared = attend(raw, cosine, sine, doc_ids, head_count, head_dim)
    resid = inputs + dot(attended, output_full, (1, 0))

    inv_rms2 = lax.rsqrt(jnp.mean(resid * resid, axis=-1, keepdims=True) + EPS)
    scaled2 = resid * inv_rms2
    normed2 = (scaled2 * gain_ffn).astype(BF16)
    normed2_all = jnp.concatenate(plane_gather(normed2), axis=0)
    results = ffn(normed2_all, cot_all, gate_slice, up_slice, down_slice)
    hidden, grad_gate, grad_up, grad_normed2_part, ffn_part = results
    grad_normed2 = plane_scatter(
        [grad_normed2_part[k * rows : (k + 1) * rows] for k in range(t_size)]
    )
    ffn_out = plane_scatter([ffn_part[k * rows : (k + 1) * rows] for k in range(t_size)])
    layer_out = resid + ffn_out
    def from_slices(grads):
        own = scatter_fsdp(grads.reshape(t_size, f_size, own_rows, slice_units), 1)
        own = own.reshape(t_size, own_rows, slice_units)
        held = jnp.zeros((own_rows, t_size, slice_units), F32)
        held = put(held, pick(own, dp), dp, 1)
        for k in range(1, t_size):
            sent = dp_swap(pick(own, dp ^ k).astype(BF16), k)
            held = put(held, sent.astype(F32), dp ^ k, 1)
        return held.reshape(own_rows, hidden_units)

    grad_down_w = dot(hidden, cot_all, (0, 0), BF16)
    down_sum = scatter_fsdp(grad_down_w.reshape(f_size, -1, width), 0)
    gate_sum = from_slices(dot(normed2_all, grad_gate, (0, 0), BF16))
    up_sum = from_slices(dot(normed2_all, grad_up, (0, 0), BF16))

    grad_gain_ffn, grad_through = norm_back(grad_normed2, scaled2, inv_rms2, gain_ffn)
    grad_resid = out_grad.astype(F32) + grad_through
    grad_branch = grad_resid.astype(BF16)
    grad_attended = dot(grad_branch, output_full, (1, 1), BF16)
    output_sum = scatter_rows(dot(attended, grad_branch, (0, 0), BF16))
    grad_raw = attend_back(
        queries, grad_attended, shared, kv_grad_next, cosine, sine, doc_ids, head_count, head_dim
    )
    grad_normed = dot(grad_raw, qkv_full, (1, 1))
    grad_gain_attn, grad_first = norm_back(grad_normed, scaled, inv_rms, gain_attn)
    input_grad = grad_resid + grad_first
    gain_grads = jnp.zeros((width, 128), BF16)
    gain_grads = gain_grads.at[:, :2].set(
        jnp.stack([grad_gain_attn, grad_gain_ffn], axis=0).astype(BF16).T
    )
    qkv_sum = scatter_rows(dot(normed, grad_raw, (0, 0), BF16).at[:, -128:].set(gain_grads))
    query_sum = qkv_sum[:, :heads_width]
    keyval_sum = qkv_sum[:, heads_width : heads_width + 2 * head_dim]
    gains_sum = qkv_sum[:, -128:-126].T

    def rate(strength, fan):
        return strength / math.sqrt(fan * tokens_total)

    gains_out = update(gains, gains_mom, gains_ema, gains_sum, rate(0.1, 1))
    query_out = update(w_query, query_mom, query_ema, query_sum, rate(0.6, width))
    keyval_out = update(w_keyval, keyval_mom, keyval_ema, keyval_sum, rate(0.15, width))
    output_out = update(w_output, output_mom, output_ema, output_sum, rate(5.0, heads_width))
    gate_out = update(w_gate, gate_mom, gate_ema, gate_sum, rate(0.6, width))
    up_out = update(w_up, up_mom, up_ema, up_sum, rate(0.6, width))
    down_out = update(w_down, down_mom, down_ema, down_sum, rate(1.5, hidden_units))
    return (
        layer_out,
        shared.astype(F32),
        input_grad,
        *gains_out,
        *query_out,
        *keyval_out,
        *output_out,
        *gate_out,
        *up_out,
        *down_out,
    )


def shards_fast(
    tokens_in,
    out_grad,
    kv_grad_next,
    doc_ids,
    gains,
    gains_mom,
    gains_ema,
    w_query,
    query_mom,
    query_ema,
    w_keyval,
    keyval_mom,
    keyval_ema,
    w_output,
    output_mom,
    output_ema,
    w_gate,
    gate_mom,
    gate_ema,
    w_up,
    up_mom,
    up_ema,
    w_down,
    down_mom,
    down_ema,
):
    t_size, f_size = lax.axis_size("dp"), lax.axis_size("fsdp")
    seq_count, length = doc_ids.shape
    width = tokens_in.shape[1]
    head_dim = w_keyval.shape[1] // 2
    head_count = w_query.shape[1] // head_dim
    hidden_units = w_gate.shape[1]
    rows = seq_count * length
    half = rows // 2
    heads_width = head_count * head_dim
    raw_width = heads_width + 2 * head_dim
    tokens_total = rows * t_size * f_size
    own_rows = w_query.shape[0]
    spot = place()

    gain_cols = jnp.zeros((own_rows, 128), BF16).at[:, :2].set(gains.astype(BF16).T)
    qkv_block = jnp.concatenate([w_query.astype(BF16), w_keyval.astype(BF16), gain_cols], axis=1)
    qkv_line = gather_line(qkv_block)

    *sent, packed = slices(spot, w_gate, w_up, w_down, t_size)
    got = [sent[0]] + [dp_swap(sent[k], k) for k in range(1, t_size)]
    packed = jnp.concatenate([flat(piece).reshape(-1, piece.shape[-1]) for piece in got] + [packed])
    output_block = after(w_output.astype(BF16), qkv_line)
    output_two, output_one = z_swap(output_block, 2), z_swap(output_block, 1)
    output_last = z_swap(output_two, 1)
    output_line = [output_block, output_two, output_one, output_last]
    units_all = lax.all_gather(
        after(packed, output_line[1], output_line[3]), "fsdp", axis=0
    )
    output_line = jnp.stack(output_line)

    qkv_near = plane_near(after(qkv_line, packed))
    qkv_far = plane_far(*after(qkv_near, output_last))
    qkv_mine = [qkv_line, *qkv_near, *qkv_far]
    qkv_pieces = qkv_mine + [core_swap(piece) for piece in qkv_mine]
    output_near = plane_near(after(output_line, *qkv_far))
    cot_near = plane_near(after(out_grad, *qkv_pieces[8:]))

    raw, normed, gains_full = enter(spot, after(tokens_in, output_line), qkv_pieces)
    cosine, sine = rotation(positions_of(doc_ids).reshape(rows), head_dim)
    queries, attended, shared = attend(raw, cosine, sine, doc_ids, head_count, head_dim)
    output_mine = [output_line, *output_near, *plane_far(*after(output_near, attended))]
    output_pieces = output_mine + [core_swap(piece) for piece in output_mine]
    cot_first, cot_second = cut(cot_near[0], 0), cut(cot_near[1], 1)
    cot = [out_grad, *cot_near, dp_swap(cot_first, 2), dp_swap(cot_second, 1)]
    resid, normed2 = leave(spot, after(attended, cot_first, cot_second), tokens_in, gains_full, output_pieces)

    normed2_near = plane_near(after(normed2, *cot[3:]))
    normed2_all = [normed2, *normed2_near, *plane_far(*normed2_near)]
    tokens2, cots, hidden, grad_gate, grad_up, grad_terms, out_terms, *grads_sent = ffn_all(
        spot, normed2_all, cot, units_all, t_size, w_down.shape[0]
    )
    normed2_sum = TokenSum(grad_terms, grads_sent[:2])
    down = LineSum(*down_grads(spot, [hidden], [cots]))
    gate = LineSum(*unit_grads(spot, [after(tokens2, down.mine)], [grad_gate]))
    down.other = after(down.other, gate.mine)
    down.line()
    normed2_sum.a, normed2_sum.b = after((normed2_sum.a, normed2_sum.b), down.chip)
    normed2_sum.cross()
    up = LineSum(*unit_grads(spot, [after(tokens2, *normed2_sum.crossed)], [grad_up]))
    grad_resid, grad_branch, grad_gain_ffn = branch(
        after(resid, up.mine), out_grad, gains_full, normed2_sum.parts()
    )
    out_sum = TokenSum(out_terms, after(grads_sent[2:], grad_branch))

    output = RowSum(*row_grads(spot, attended, after(grad_branch, *out_sum.sent), width))
    grad_attended = leave_back(spot, after(grad_branch, output.mine), output_pieces)
    gate.other, output.other = after((gate.other, output.other), grad_attended)
    output.plane()
    gate.line()
    grad_raw = attend_back(
        queries, after(grad_attended, gate.chip, *output.sent), shared, kv_grad_next, cosine, sine,
        doc_ids, head_count, head_dim,
    )
    input_grad, grad_gain_attn = enter_back(
        spot, grad_raw, tokens_in, gains_full, grad_resid, qkv_pieces
    )
    out_sum.a, out_sum.b, output.a, output.b = after(
        (out_sum.a, out_sum.b, output.a, output.b), input_grad
    )
    output.cross()
    qkv = RowSum(
        *row_grads(
            spot, after(normed, *output.crossed, down.total), grad_raw, raw_width,
            (grad_gain_attn, grad_gain_ffn),
        )
    )
    up.other = after(up.other, qkv.mine)
    up.line()
    output.last_a, output.last_b = after((output.last_a, output.last_b), up.chip)
    output.near()
    gate.total = after(gate.total, output.odd)
    qkv.other = after(qkv.other, gate.total)
    qkv.plane()

    def rate(strength, fan):
        return strength / math.sqrt(fan * tokens_total)

    def exchange(*totals):
        totals = [flat(total) for total in totals]
        pieces = [jnp.stack([total[k] for total in totals]) for k in range(t_size)]
        return pieces[:1] + [dp_swap(pieces[k], k) for k in range(1, t_size)]

    down_out = update_rows(
        [(after(down.total, *qkv.sent), 0)], [(w_down, down_mom, down_ema)],
        [rate(1.5, hidden_units)],
    )
    out_sum.a, out_sum.b = after((out_sum.a, out_sum.b), *qkv.sent)
    out_sum.cross()
    qkv.a, qkv.b = after((qkv.a, qkv.b), down_out[0], *out_sum.crossed)
    qkv.cross()
    qkv.near()
    pieces = exchange(after(gate.total, qkv.odd), after(up.total, qkv.odd))
    output.line = after(output.line, qkv.odd)
    output.far()
    qkv.line = after(qkv.line, output.rest)
    qkv.far()
    out_sum.last_a, out_sum.last_b = after((out_sum.last_a, out_sum.last_b), qkv.rest)
    layer_out = layer_out_of(resid, out_sum.parts())
    pieces = after(pieces, qkv.rest)
    gate_out = update_units(spot, w_gate, gate_mom, gate_ema, pieces, 0, rate(0.6, width))
    up_out = update_units(spot, w_up, up_mom, up_ema, pieces, 1, rate(0.6, width))
    output_out = update_rows(
        [(after(x, qkv.rest), at) for x, at in output.final()],
        [(w_output, output_mom, output_ema)], [rate(5.0, heads_width)],
    )
    qkv.last = after(qkv.last, gate_out[0], layer_out)
    *qkv_out, left_over = update_rows(
        qkv.final(),
        [(w_query, query_mom, query_ema), (w_keyval, keyval_mom, keyval_ema)],
        [rate(0.6, width), rate(0.15, width)],
    )
    gains_out = update(gains, gains_mom, gains_ema, left_over[:, :2].T, rate(0.1, 1))
    return (
        layer_out,
        shared.astype(F32),
        input_grad,
        *gains_out,
        *qkv_out,
        *output_out,
        *gate_out,
        *up_out,
        *down_out,
    )


def solution(mesh):
    rows = P(BOTH, None)
    shards = shards_fast if dict(mesh.shape) == {"dp": 4, "fsdp": 8} else shards_any
    cols = P(None, BOTH)
    return jax.shard_map(
        shards,
        mesh=mesh,
        in_specs=(rows,) * 4 + (cols,) * 3 + (rows,) * 18,
        out_specs=(rows,) * 3 + (cols,) * 3 + (rows,) * 18,
        check_vma=False,
    )
```
